128 devices in a mesh: table: 32 (over z, y, core), rep: 4 (over x).
Axes of the slice: x: 4, y: 4, z: 4, core: 2. Of those that a mesh axis runs over, the one named last changes fastest.
Arguments:
- titles: bfloat16 [3072, 64, 768], P(('table', 'rep')), may hold values from -6 to 6
- ln_gain: float32 [768], replicated, may hold values from 0.25 to 1.75
- w_up: bfloat16 [768, 3072], replicated, may hold values from -0.21875 to 0.21875
- w_down: bfloat16 [3072, 768], replicated, may hold values from -0.109375 to 0.109375
- w_proj: bfloat16 [768, 256], replicated, may hold values from -0.21875 to 0.21875
- sample_grad: bfloat16 [131072, 256], P(('table', 'rep')), may hold values from -6 to 6
- sample_item: int32 [131072], P(('table', 'rep')), may hold values from 0 to 3071
- sample_row: int32 [131072], P(('table', 'rep')), may hold values from 0 to 511
- row_ids: int32 [128, 512], P(('table', 'rep')), may hold values from 0 to 262143, as said below
- table: float32 [262144, 256], P(('table', 'rep')), may hold values from -6 to 6
- accum: float32 [262144, 256], P(('table', 'rep')), may hold values from 0.05 to 1
Outputs:
- d_titles: bfloat16 [3072, 64, 768], P(('table', 'rep'))
- grad_up: float32 [768, 3072], P(None, 'table')
- grad_down: float32 [3072, 768], P('table')
- grad_proj: float32 [768, 256], P('table')
- grad_gain: float32 [768], P('table')
- new_table: float32 [262144, 256], P(('table', 'rep'))
- new_accum: float32 [262144, 256], P(('table', 'rep'))
The draws below stay inside these ranges and needn't reach their ends.
Inputs may be any that keep to these rules, and one draw needn't show every extreme that they name: `row_ids`: in each device's row list, entries k * 4 to (k + 1) * 4 - 1 are distinct rows of the block of 2048 rows held by device k, for every k.
All inputs are finite; a program needn't handle non-finite values.
Results may differ from the reference program's by a relative error of at most 0.0067.
Values sent between devices are 32-bit elements; how exact they have to be, the bound alone decides.
No kernel may reach another device: no remote copies, remote signals or barrier semaphores. Data moves between devices by JAX's collectives and lax.ppermute only.
A program may use at most 192 MiB of HBM per device.

```python
import math
import jax
import jax.numpy as jnp
import numpy as np
from jax import lax

D = 768
FF = 3072
E = 256
L = 64
U_DEV = 24
S_DEV = 1024
RCAP = 4
ROWS_DEV = 2048
ITEMS = 3072
SAMPLES = 131072
UROW = 512
ROWS = 262144
N_TABLE = 32
N_REP = 4


def draw_row_ids(key, part):
    key = jax.random.fold_in(key, 11)
    devices = N_TABLE * N_REP
    stride = ROWS_DEV // RCAP
    slots = jnp.arange(UROW, dtype=jnp.int32)
    owner = slots // RCAP
    within = slots % RCAP
    jitter = jax.random.randint(key, (devices, UROW), 0, stride, dtype=jnp.int32)
    return (owner * ROWS_DEV + within * stride)[None, :] + jitter


def place_ends(entries, key, smallest, top_value):
    extent = entries.shape
    index_at = [jax.random.randint(jax.random.fold_in(key, axis), (), 0, extent[axis]) for axis in range(len(extent))]
    entries = entries.at[tuple(index_at)].set(smallest)
    longest = extent.index(max(extent))
    index_at[longest] = (index_at[longest] + 1) % extent[longest]
    return entries.at[tuple(index_at)].set(top_value)


def steps_of(own_key, extent, cuts, smallest, high):
    def one(position, blocks):
        steps = jax.random.uniform(jax.random.fold_in(jax.random.fold_in(own_key, 6), position), (blocks,), jnp.float32, smallest / len(cuts), high / len(cuts))
        return jnp.repeat(jnp.exp(steps), extent[position] // blocks).reshape((-1,) + (1,) * (len(extent) - position - 1))

    loudness = one(*cuts[0])
    for cut in cuts[1:]:
        loudness = loudness * one(*cut)
    return loudness


def cumulative_ranks(number_of, lean):
    weights = [(1 << 20) // math.isqrt(grade ** lean) + 1 for grade in range(1, number_of + 1)]
    scale = 1 + sum(weights) // (1 << 30)
    return np.cumsum(np.array([max(1, weight // scale) for weight in weights]))


def ranked(rng, shape, count, skew):
    table = cumulative_ranks(count, skew)
    pick = jax.random.randint(jax.random.fold_in(rng, 1), shape, 0, int(table[count - 1]))
    rank = jnp.searchsorted(jnp.asarray(table, jnp.int32), pick, side="right")
    return jax.random.permutation(jax.random.fold_in(rng, 2), count)[rank].astype(jnp.int32)


def bell_draw(key, extent, spread, most, pieces=(), kind=jnp.bfloat16):
    gain = steps_of(key, extent, pieces, -0.22, 0.18) if pieces else 1.0
    entries = jax.random.normal(key, extent, jnp.float32) * spread * gain
    return jnp.minimum(jnp.maximum(entries, -most), most).astype(kind)


def setup_inputs(seed: int = 0) -> dict:
    streams_of = jax.random.split(jax.random.key(seed), 12)
    return {
        "titles": bell_draw(streams_of[0], (ITEMS, L, D), 1.0, 6.0, ((0, 128),)),
        "ln_gain": jnp.clip(1.0 + 0.15 * jax.random.normal(streams_of[1], (D,), jnp.float32), 0.25, 1.75),
        "w_up": bell_draw(streams_of[2], (D, FF), D ** -0.5, 0.21875),
        "w_down": bell_draw(streams_of[3], (FF, D), FF ** -0.5, 0.109375),
        "w_proj": bell_draw(streams_of[4], (D, E), D ** -0.5, 0.21875),
        "sample_grad": bell_draw(streams_of[5], (SAMPLES, E), 1.0, 6.0, ((0, 128),)),
        "sample_item": place_ends(ranked(streams_of[6], (SAMPLES,), ITEMS, 2), jax.random.fold_in(streams_of[6], 3), 0, ITEMS - 1).astype(jnp.int32),
        "sample_row": place_ends(jax.random.randint(streams_of[7], (SAMPLES,), 0, UROW), jax.random.fold_in(streams_of[7], 1), 0, UROW - 1).astype(jnp.int32),
        "row_ids": draw_row_ids(jax.random.fold_in(streams_of[11], 71), 0),
        "table": bell_draw(streams_of[9], (ROWS, E), 1.0, 6.0, ((0, 128),), jnp.float32),
        "accum": jnp.clip(jnp.exp(math.log(1.0) - 2.9957323 * jax.random.uniform(streams_of[10], (ROWS, E), jnp.float32) ** steps_of(streams_of[10], (ROWS, E), ((0, 128),), -0.2, 0.2)), 0.05, 1.0),
    }


GELU_C = 0.7978845608028654
NORM_EPS = 1e-05
LEARN_RATE = 0.1

def gelu_parts(pre):
    inner = GELU_C * (pre + 0.044715 * pre * pre * pre)
    tangent = jnp.tanh(inner)
    value = 0.5 * pre * (1.0 + tangent)
    slope = 0.5 * (1.0 + tangent) + 0.5 * pre * (1.0 - tangent * tangent) * GELU_C * (1.0 + 3.0 * 0.044715 * pre * pre)
    return (value, slope)

def encode_block(block, item_grad, ln_gain, w_up, w_down, w_proj):
    units, length, width = block.shape
    flat = block.reshape(units * length, width).astype(jnp.float32)
    center = lax.optimization_barrier(jnp.mean(flat, axis=1, keepdims=True))
    offset = flat - center
    inv_scale = lax.rsqrt(lax.optimization_barrier(jnp.mean(offset * offset, axis=1, keepdims=True)) + NORM_EPS)
    normed = offset * inv_scale
    normed_b = (normed * ln_gain.astype(jnp.float32)).astype(jnp.bfloat16)
    pre = jnp.dot(normed_b, w_up, preferred_element_type=jnp.float32)
    value, slope = gelu_parts(pre)
    mean_act = lax.optimization_barrier(jnp.mean(value.reshape(units, length, -1), axis=1)).astype(jnp.bfloat16)
    pooled = lax.optimization_barrier(jnp.mean(flat.reshape(units, length, width), axis=1)) + jnp.dot(mean_act, w_down, preferred_element_type=jnp.float32)
    pooled_b = pooled.astype(jnp.bfloat16)
    grad_b = item_grad.astype(jnp.bfloat16)
    proj_term = jnp.dot(pooled_b.T, grad_b, preferred_element_type=jnp.float32)
    d_pooled = jnp.dot(grad_b, w_proj.T, preferred_element_type=jnp.float32)
    d_pooled_b = d_pooled.astype(jnp.bfloat16)
    down_term = jnp.dot(mean_act.T, d_pooled_b, preferred_element_type=jnp.float32)
    d_act = jnp.dot(d_pooled_b, w_down.T, preferred_element_type=jnp.float32) / length
    d_pre = (d_act[:, None, :] * slope.reshape(units, length, -1)).reshape(units * length, -1).astype(jnp.bfloat16)
    up_term = jnp.dot(normed_b.T, d_pre, preferred_element_type=jnp.float32)
    d_normed = jnp.dot(d_pre, w_up.T, preferred_element_type=jnp.float32)
    gain_term = lax.optimization_barrier(jnp.sum(d_normed * normed, axis=0))
    d_hat = d_normed * ln_gain.astype(jnp.float32)
    d_flat = inv_scale * (d_hat - lax.optimization_barrier(jnp.mean(d_hat, axis=1, keepdims=True)) - normed * lax.optimization_barrier(jnp.mean(d_hat * normed, axis=1, keepdims=True)))
    d_block = d_flat.reshape(units, length, width) + (d_pooled / length)[:, None, :]
    return (d_block.astype(jnp.bfloat16), up_term, down_term, proj_term, gain_term)

def reference(titles, ln_gain, w_up, w_down, w_proj, sample_grad, sample_item, sample_row, row_ids, table, accum):
    grads_f = sample_grad.astype(jnp.float32)
    item_grad = jax.ops.segment_sum(grads_f, sample_item, num_segments=ITEMS)
    blocks = ITEMS // U_DEV

    def step(carry, inputs):
        block, block_grad = inputs
        d_block, up_term, down_term, proj_term, gain_term = encode_block(block, block_grad, ln_gain, w_up, w_down, w_proj)
        return ((carry[0] + up_term, carry[1] + down_term, carry[2] + proj_term, carry[3] + gain_term), d_block)
    start = (jnp.zeros((D, FF), jnp.float32), jnp.zeros((FF, D), jnp.float32), jnp.zeros((D, E), jnp.float32), jnp.zeros((D,), jnp.float32))
    sums, d_blocks = lax.scan(step, start, (titles.reshape(blocks, U_DEV, L, D), item_grad.reshape(blocks, U_DEV, E)))
    d_titles = d_blocks.reshape(ITEMS, L, D)
    owner_dev = (jnp.arange(SAMPLES) // S_DEV).astype(jnp.int32)
    global_rows = row_ids[owner_dev, sample_row].astype(jnp.int32)
    row_grad = jax.ops.segment_sum(grads_f, global_rows, num_segments=ROWS)
    new_accum = accum + row_grad * row_grad
    new_table = table - LEARN_RATE * row_grad * lax.rsqrt(new_accum)
    return (d_titles, sums[0], sums[1], sums[2], sums[3], new_table, new_accum)
```

```python
import functools

import jax
import jax.numpy as jnp
from jax import lax
from jax.experimental import pallas as pl
from jax.experimental.pallas import tpu as pltpu
from jax.sharding import Mesh
from jax.sharding import PartitionSpec as P

GELU_C = 0.7978845608028654
NORM_EPS = 1e-05
LEARN_RATE = 0.1
CHIPS = ("z", "y", "x")
DEVICES = ("z", "y", "c", "x")


def contract_first(left, right):
    return lax.dot_general(
        left, right, (((0,), (0,)), ((), ())), preferred_element_type=jnp.float32
    )


def contract_last(left, right):
    return lax.dot_general(
        left, right, (((1,), (1,)), ((), ())), preferred_element_type=jnp.float32
    )


def gelu_parts(pre):
    inner = GELU_C * (pre + 0.044715 * pre * pre * pre)
    tangent = jnp.tanh(inner)
    value = 0.5 * pre * (1.0 + tangent)
    slope = 0.5 * (1.0 + tangent) + 0.5 * pre * (1.0 - tangent * tangent) * GELU_C * (
        1.0 + 3.0 * 0.044715 * pre * pre
    )
    return (value, slope)


def swap_cores(block):
    return lax.ppermute(block, "c", [(0, 1), (1, 0)])


def factor_kernel(part_f, part_d, items_ref, columns_ref, proj_ref, down_out, proj_out):
    @pl.when(pl.program_id(0) == 0)
    def _():
        down_out[...] = jnp.zeros_like(down_out)
        proj_out[...] = jnp.zeros_like(proj_out)

    grad_b = items_ref[...].astype(jnp.bfloat16)
    d_pooled_b = contract_last(grad_b, proj_ref[...]).astype(jnp.bfloat16)
    columns = columns_ref[...].astype(jnp.bfloat16)
    down_out[...] += contract_first(columns, d_pooled_b)[:part_f]
    proj_out[...] += contract_first(columns, grad_b)[part_f : part_f + part_d]


def factor_products(all_items, columns, w_proj, part_f, part_d):
    items, width_e = all_items.shape
    width = w_proj.shape[0]
    step = items // 4
    return pl.pallas_call(
        functools.partial(factor_kernel, part_f, part_d),
        grid=(items // step,),
        in_specs=[
            pl.BlockSpec((step, width_e), lambda i: (i, 0)),
            pl.BlockSpec((step, columns.shape[1]), lambda i: (i, 0)),
            pl.BlockSpec((width, width_e), lambda i: (0, 0)),
        ],
        out_specs=[
            pl.BlockSpec((part_f, width), lambda i: (0, 0)),
            pl.BlockSpec((part_d, width_e), lambda i: (0, 0)),
        ],
        out_shape=[
            jax.ShapeDtypeStruct((part_f, width), jnp.float32),
            jax.ShapeDtypeStruct((part_d, width_e), jnp.float32),
        ],
        compiler_params=pltpu.CompilerParams(vmem_limit_bytes=32 << 20),
        cost_estimate=pl.CostEstimate(
            flops=2 * items * width_e * width, bytes_accessed=items * 2048, transcendentals=0
        ),
    )(all_items, columns, w_proj)


def per_device(
    titles,
    ln_gain,
    w_up,
    w_down,
    w_proj,
    sample_grad,
    sample_item,
    sample_row,
    row_ids,
    table,
    accum,
):
    n_z, n_y, n_c, n_x = (lax.axis_size(name) for name in DEVICES)
    chips = n_z * n_y * n_x
    devices = chips * n_c
    core = lax.axis_index("c")
    units, length, width = titles.shape
    hidden = w_up.shape[1]
    width_e = sample_grad.shape[1]
    part_f = hidden // devices
    part_d = width // devices

    place = lax.iota(jnp.int32, chips * units)
    chip, unit = place // units, place % units

    def item_part(of_core):
        wanted = (((chip // n_x) * n_c + of_core) * n_x + chip % n_x) * units + unit
        onehot = (sample_item[:, None] == wanted[None, :]).astype(jnp.bfloat16)
        return contract_first(onehot, sample_grad)

    got = swap_cores(item_part(1 - core))
    mine = (item_part(core) + got).reshape(chips, units, width_e)
    item_grad = jnp.sum(lax.all_to_all(mine, CHIPS, 0, 0, tiled=True), axis=0)

    flat = titles.reshape(units * length, width).astype(jnp.float32)
    center = jnp.mean(flat, axis=1, keepdims=True)
    offset = flat - center
    inv_scale = lax.rsqrt(jnp.mean(offset * offset, axis=1, keepdims=True) + NORM_EPS)
    normed = offset * inv_scale
    normed_b = (normed * ln_gain).astype(jnp.bfloat16)
    pre = jnp.dot(normed_b, w_up, preferred_element_type=jnp.float32)
    value, slope = gelu_parts(pre)
    mean_act = jnp.mean(value.reshape(units, length, -1), axis=1).astype(jnp.bfloat16)
    pooled = jnp.mean(flat.reshape(units, length, width), axis=1) + jnp.dot(
        mean_act, w_down, preferred_element_type=jnp.float32
    )
    pooled_b = pooled.astype(jnp.bfloat16)

    slot_count = row_ids.shape[1]
    capacity = slot_count // devices
    rows_here = table.shape[0]
    slot_hot = (sample_row[:, None] == lax.iota(jnp.int32, slot_count)[None, :]).astype(
        jnp.bfloat16
    )
    row_part = contract_first(slot_hot, sample_grad).reshape(devices, capacity * width_e)
    local_rows = (row_ids[0] % rows_here).reshape(devices, capacity).astype(jnp.float32)
    spare = -(part_f + part_d) % 32
    columns = jnp.concatenate(
        [
            mean_act.astype(jnp.float32).reshape(units, devices, part_f),
            pooled_b.astype(jnp.float32).reshape(units, devices, part_d),
            jnp.pad(local_rows.T[:, :, None], ((0, units - capacity), (0, 0), (0, spare - 1))),
        ],
        axis=2,
    )
    n_col = columns.shape[2]
    packed = jnp.concatenate(
        [row_part, jnp.swapaxes(columns, 0, 1).reshape(devices, units * n_col)], axis=1
    )
    arrived = lax.all_to_all(packed, DEVICES, 0, 0, tiled=True)
    got_grads = arrived[:, : capacity * width_e].reshape(slot_count, width_e)
    got_columns = arrived[:, capacity * width_e :].reshape(devices, units, n_col)
    got_rows = got_columns[:, :capacity, part_f + part_d].reshape(slot_count).astype(jnp.int32)
    row_grad = jax.ops.segment_sum(got_grads, got_rows, num_segments=rows_here)
    new_accum = accum + row_grad * row_grad
    new_table = table - LEARN_RATE * row_grad * lax.rsqrt(new_accum)

    grad_b = item_grad.astype(jnp.bfloat16)
    d_pooled = contract_last(grad_b, w_proj)
    d_pooled_b = d_pooled.astype(jnp.bfloat16)
    d_act = contract_last(d_pooled_b, w_down) / length
    d_pre = (
        (d_act[:, None, :] * slope.reshape(units, length, -1))
        .reshape(units * length, -1)
        .astype(jnp.bfloat16)
    )
    up_term = contract_first(d_pre, normed_b).reshape(n_z * n_y, n_c, n_x * part_f, width)
    first = core == 0
    got = swap_cores(jnp.where(first, up_term[:, 1], up_term[:, 0]))
    up_mine = (jnp.where(first, up_term[:, 0], up_term[:, 1]) + got).reshape(chips, part_f, width)
    up_share = jnp.sum(lax.all_to_all(up_mine, CHIPS, 0, 0, tiled=True), axis=0)
    grad_up = lax.all_gather(up_share, "x", axis=0, tiled=True).T

    all_items = lax.all_gather(item_grad, DEVICES, axis=0, tiled=True)
    down_share, proj_share = factor_products(
        all_items, got_columns.reshape(devices * units, n_col), w_proj, part_f, part_d
    )
    grad_down = lax.all_gather(down_share, "x", axis=0, tiled=True)
    grad_proj = lax.all_gather(proj_share, "x", axis=0, tiled=True)

    d_normed = contract_last(d_pre, w_up)
    gain_term = jnp.sum(d_normed * normed, axis=0)
    gains = lax.all_gather(gain_term, DEVICES, axis=0)
    t_index = (lax.axis_index("z") * n_y + lax.axis_index("y")) * n_c + core
    cut = width // (n_z * n_y * n_c)
    grad_gain = lax.dynamic_slice_in_dim(jnp.sum(gains, axis=0), t_index * cut, cut, 0)
    d_hat = d_normed * ln_gain
    d_flat = inv_scale * (
        d_hat
        - jnp.mean(d_hat, axis=1, keepdims=True)
        - normed * jnp.mean(d_hat * normed, axis=1, keepdims=True)
    )
    d_block = d_flat.reshape(units, length, width) + (d_pooled / length)[:, None, :]
    return (
        d_block.astype(jnp.bfloat16),
        grad_up,
        grad_down,
        grad_proj,
        grad_gain,
        new_table,
        new_accum,
    )


def solution(mesh):
    n_table, n_rep = mesh.devices.shape
    side = n_rep
    fine = Mesh(mesh.devices.reshape(n_table // (2 * side), side, 2, n_rep), DEVICES)
    split, tab = P(DEVICES), ("z", "y", "c")
    return jax.shard_map(
        per_device,
        mesh=fine,
        in_specs=(split, P(), P(), P(), P(), split, split, split, split, split, split),
        out_specs=(split, P(None, tab), P(tab), P(tab), P(tab), split, split),
        check_vma=False,
    )
```

```python
import functools
import math

import jax
import jax.numpy as jnp
from jax import lax
from jax.experimental import pallas as pl
from jax.experimental.pallas import tpu as pltpu
from jax.sharding import Mesh
from jax.sharding import PartitionSpec as P

GELU_C = 0.7978845608028654
GELU_K = 0.044715
NORM_EPS = 1e-05
LEARN_RATE = 0.1
CHIPS = ("z", "y", "x")
GROUP = ("z", "y", "c")
DEVICES = ("z", "y", "c", "x")
VMEM = 48 << 20


def contract_first(left, right):
    return lax.dot_general(
        left, right, (((0,), (0,)), ((), ())), preferred_element_type=jnp.float32
    )


def contract_last(left, right):
    return lax.dot_general(
        left, right, (((1,), (1,)), ((), ())), preferred_element_type=jnp.float32
    )


def cost(flops, moved, transcendentals=0):
    return pl.CostEstimate(flops=flops, bytes_accessed=moved, transcendentals=transcendentals)


def swap_cores(block):
    return lax.ppermute(block, "c", [(0, 1), (1, 0)])


def along(block, name, step):
    size = lax.axis_size(name)
    return lax.ppermute(block, name, [(i, i ^ step) for i in range(size)])


def partners(name, second):
    sizes = [lax.axis_size(n) for n in DEVICES]
    at = DEVICES.index(name)
    pairs = []
    for index in range(math.prod(sizes)):
        place, rest = [], index
        for size in reversed(sizes):
            place.insert(0, rest % size)
            rest //= size
        place[at] ^= 1 if (place[DEVICES.index("c")] == 1) == second else 3
        to = 0
        for size, p in zip(sizes, place):
            to = to * size + p
        pairs.append((index, to))
    return pairs


def slot_of(core, here, size):
    block = lax.iota(jnp.int32, size) ^ here
    one = jnp.where(block == 0, 0, jnp.where(block == 1, 2, jnp.where(block == 2, 3, 1)))
    two = jnp.where(block < 2, block, 5 - block)
    return jnp.where(core == 0, one, two)


def halve(parts, names, second, also=()):
    kept, sent = [], []
    for part, name in zip(parts, names):
        dim = ("z", "y", "x").index(name)
        middle = part.shape[dim] // 2
        kept.append(lax.slice_in_dim(part, 0, middle, axis=dim))
        sent.append(
            lax.ppermute(
                lax.slice_in_dim(part, middle, None, axis=dim), DEVICES, partners(name, second)
            )
        )
    if also:
        sent, also = lax.optimization_barrier((sent, also))
    return [k + s for k, s in zip(kept, sent)], also


def layer_norm(rows):
    center = jnp.mean(rows, axis=1, keepdims=True)
    offset = rows - center
    inv_scale = lax.rsqrt(jnp.mean(offset * offset, axis=1, keepdims=True) + NORM_EPS)
    return offset * inv_scale, inv_scale


def forward_kernel(units, titles_ref, gain_ref, w_ref, normed_ref, slope_ref, act_ref, mean_ref):
    rows, width = titles_ref.shape
    length = rows // units
    step = 8 * length

    @pl.when(pl.program_id(0) == 0)
    def _():
        for r in range(units // 8):
            block = titles_ref[r * step : (r + 1) * step, :].astype(jnp.float32)
            normed, _ = layer_norm(block)
            normed_ref[r * step : (r + 1) * step, :] = (normed * gain_ref[...]).astype(jnp.bfloat16)
            mean_ref[r * 8 : (r + 1) * 8, :] = jnp.mean(block.reshape(8, length, width), axis=1)

    for r in range(units // 8):
        pre = jnp.dot(
            normed_ref[r * step : (r + 1) * step, :],
            w_ref[...],
            preferred_element_type=jnp.float32,
        )
        square = pre * pre
        tangent = jnp.tanh(pre * (GELU_C + (GELU_C * GELU_K) * square))
        half = 0.5 + 0.5 * tangent
        value = pre * half
        slope = half + value * (1.0 - tangent) * (GELU_C + (3.0 * GELU_C * GELU_K) * square)
        slope_ref[r * step : (r + 1) * step, :] = slope.astype(jnp.bfloat16)
        act_ref[r * 8 : (r + 1) * 8, :] = jnp.mean(value.reshape(8, length, -1), axis=1)


def forward(titles, ln_gain, w_up):
    units, length, width = titles.shape
    rows, hidden = units * length, w_up.shape[1]
    block = 512
    return pl.pallas_call(
        functools.partial(forward_kernel, units),
        grid=(hidden // block,),
        in_specs=[
            pl.BlockSpec((rows, width), lambda i: (0, 0)),
            pl.BlockSpec((1, width), lambda i: (0, 0)),
            pl.BlockSpec((width, block), lambda i: (0, i)),
        ],
        out_specs=[
            pl.BlockSpec((rows, width), lambda i: (0, 0)),
            pl.BlockSpec((rows, block), lambda i: (0, i)),
            pl.BlockSpec((units, block), lambda i: (0, i)),
            pl.BlockSpec((units, width), lambda i: (0, 0)),
        ],
        out_shape=[
            jax.ShapeDtypeStruct((rows, width), jnp.bfloat16),
            jax.ShapeDtypeStruct((rows, hidden), jnp.bfloat16),
            jax.ShapeDtypeStruct((units, hidden), jnp.float32),
            jax.ShapeDtypeStruct((units, width), jnp.float32),
        ],
        compiler_params=pltpu.CompilerParams(vmem_limit_bytes=VMEM),
        cost_estimate=cost(8 * rows * width * hidden, 4 * rows * hidden, rows * hidden),
        name="forward",
    )(titles.reshape(rows, width), ln_gain.reshape(1, width), w_up)


def up_kernel(
    units, slots, core_ref, keep_at, send_at, slope_ref, act_ref, normed_ref, mean_ref, pool_ref,
    grad_ref, pre_ref, *out_refs
):
    rows, block = slope_ref.shape
    length, step = rows // units, rows // units * 8
    part = block // slots
    for r in range(units // 8):
        slope = slope_ref[r * step : (r + 1) * step, :].astype(jnp.float32)
        d_pre = slope.reshape(8, length, block) * act_ref[r * 8 : (r + 1) * 8, :][:, None, :]
        pre_ref[r * step : (r + 1) * step, :] = d_pre.reshape(step, block).astype(jnp.bfloat16)
    up = contract_first(pre_ref[...], normed_ref[...])
    down = contract_first(mean_ref[...], grad_ref[...])
    proj = contract_first(pool_ref[...], grad_ref[...])
    first = core_ref[0] == 0
    half = slots // 2
    n_x = half // 4
    for q in range(half):
        y, x = q // n_x, q % n_x
        even, odd = (y * 2 * n_x + x, (y * 2 + 1) * n_x + x)

        def pieces(k):
            rows_f = up[k * part : (k + 1) * part]
            rows_d = down[k * part : (k + 1) * part]
            out = []
            for p in range(3):
                out.append(rows_f[:, p * 256 : (p + 1) * 256])
                out.append(rows_d[p * 8 : (p + 1) * 8])
            return out + [proj[k * 8 : (k + 1) * 8]]

        a, b = pieces(even), pieces(odd)
        keep = [jnp.where(first, u, v) for u, v in zip(a, b)]
        send = [jnp.where(first, v, u) for u, v in zip(a, b)]
        for values, at, refs in ((keep, keep_at, out_refs[:3]), (send, send_at, out_refs[3:])):
            place = at[1, y] * n_x + at[2, x]
            for p in range(3):
                refs[p][place, :part, :] = values[2 * p]
                refs[p][place, part : part + 8, :] = values[2 * p + 1]
            refs[0][place, part + 8 :, :] = values[6]


def up_products(core, keep_at, send_at, slope, d_act, normed_b, mean_act_b, pooled_b, grad_b):
    rows, hidden = slope.shape
    units, width = d_act.shape[0], normed_b.shape[1]
    width_e = grad_b.shape[1]
    sides = keep_at.shape[1]
    block = hidden // sides
    slots = 2 * sides * sides
    part = block // slots
    tall = (part + 16, part + 8, part + 8)

    def whole(array):
        return pl.BlockSpec(array.shape, lambda i, c, k, s: (0, 0))

    def columns(array):
        return pl.BlockSpec((array.shape[0], array.shape[1] // sides), lambda i, c, k, s: (0, i))

    return pl.pallas_call(
        functools.partial(up_kernel, units, slots),
        grid_spec=pltpu.PrefetchScalarGridSpec(
            num_scalar_prefetch=3,
            grid=(sides,),
            in_specs=[
                columns(slope),
                columns(d_act),
                whole(normed_b),
                columns(mean_act_b),
                columns(pooled_b),
                whole(grad_b),
            ],
            out_specs=[columns(slope)]
            + [
                pl.BlockSpec((slots // 2, h, width_e), lambda i, c, k, s: (k[0, i], 0, 0))
                for h in tall
            ]
            + [
                pl.BlockSpec((slots // 2, h, width_e), lambda i, c, k, s: (s[0, i], 0, 0))
                for h in tall
            ],
        ),
        out_shape=[jax.ShapeDtypeStruct((rows, hidden), jnp.bfloat16)]
        + [jax.ShapeDtypeStruct((sides * slots // 2, h, width_e), jnp.float32) for h in tall * 2],
        compiler_params=pltpu.CompilerParams(vmem_limit_bytes=VMEM),
        cost_estimate=cost(2 * rows * width * hidden, 4 * rows * hidden),
        name="up_products",
    )(core, keep_at, send_at, slope, d_act, normed_b, mean_act_b, pooled_b, grad_b)


def titles_kernel(pre_ref, w_ref, titles_ref, gain_ref, pool_ref, out_ref, gain_out):
    rows, width = titles_ref.shape
    units = pool_ref.shape[0]
    length = rows // units
    d_normed = contract_last(pre_ref[...], w_ref[...])
    normed, inv_scale = layer_norm(titles_ref[...].astype(jnp.float32))
    product = d_normed * normed

    @pl.when(pl.program_id(0) == 0)
    def _():
        gain_out[...] = jnp.zeros_like(gain_out)

    gain_out[...] += jnp.sum(product.reshape(rows // 8, 8, width), axis=0)
    d_hat = d_normed * gain_ref[...]
    d_flat = inv_scale * (
        d_hat
        - jnp.mean(d_hat, axis=1, keepdims=True)
        - normed * jnp.mean(d_hat * normed, axis=1, keepdims=True)
    )
    d_block = d_flat.reshape(units, length, width) + (pool_ref[...] * (1.0 / length))[:, None, :]
    out_ref[...] = d_block.reshape(rows, width).astype(jnp.bfloat16)


def title_grads(d_pre, w_up, titles, ln_gain, d_pooled):
    units, length, width = titles.shape
    rows, hidden = d_pre.shape
    step = 8 * length
    return pl.pallas_call(
        titles_kernel,
        grid=(rows // step,),
        in_specs=[
            pl.BlockSpec((step, hidden), lambda i: (i, 0)),
            pl.BlockSpec((width, hidden), lambda i: (0, 0)),
            pl.BlockSpec((step, width), lambda i: (i, 0)),
            pl.BlockSpec((1, width), lambda i: (0, 0)),
            pl.BlockSpec((8, width), lambda i: (i, 0)),
        ],
        out_specs=[
            pl.BlockSpec((step, width), lambda i: (i, 0)),
            pl.BlockSpec((8, width), lambda i: (0, 0)),
        ],
        out_shape=[
            jax.ShapeDtypeStruct((rows, width), jnp.bfloat16),
            jax.ShapeDtypeStruct((8, width), jnp.float32),
        ],
        compiler_params=pltpu.CompilerParams(vmem_limit_bytes=VMEM),
        cost_estimate=cost(2 * rows * width * hidden, 2 * rows * hidden),
        name="title_grads",
    )(d_pre, w_up, titles.reshape(rows, width), ln_gain.reshape(1, width), d_pooled)


def rows_kernel(arrived_ref, table_ref, accum_ref, table_out, accum_out):
    step, width_e = table_ref.shape
    slots = arrived_ref.shape[0]
    grads = arrived_ref[:, :width_e]
    ids = arrived_ref[:, width_e : width_e + 1].astype(jnp.int32)
    here = lax.broadcasted_iota(jnp.int32, (slots, step), 1) + pl.program_id(0) * step
    onehot = jnp.where(here == ids, 1.0, 0.0).astype(jnp.bfloat16)
    high = grads.astype(jnp.bfloat16)
    low = (grads - high.astype(jnp.float32)).astype(jnp.bfloat16)
    row_grad = contract_first(onehot, high) + contract_first(onehot, low)
    new_accum = accum_ref[...] + row_grad * row_grad
    accum_out[...] = new_accum
    table_out[...] = table_ref[...] - LEARN_RATE * row_grad * lax.rsqrt(new_accum)


def row_update(arrived, table, accum):
    rows, width_e = table.shape
    step = 512
    tile = pl.BlockSpec((step, width_e), lambda i: (i, 0))
    return pl.pallas_call(
        rows_kernel,
        grid=(rows // step,),
        in_specs=[pl.BlockSpec(arrived.shape, lambda i: (0, 0)), tile, tile],
        out_specs=[tile, tile],
        out_shape=[jax.ShapeDtypeStruct((rows, width_e), jnp.float32)] * 2,
        compiler_params=pltpu.CompilerParams(vmem_limit_bytes=VMEM),
        cost_estimate=cost(4 * rows * width_e * arrived.shape[0], 16 * rows * width_e),
        name="row_update",
    )(arrived, table, accum)


def per_device(
    titles,
    ln_gain,
    w_up,
    w_down,
    w_proj,
    sample_grad,
    sample_item,
    sample_row,
    row_ids,
    table,
    accum,
):
    n_z, n_y, n_c, n_x = (lax.axis_size(name) for name in DEVICES)
    chips, groups = n_z * n_y * n_x, n_z * n_y * n_c
    devices = chips * n_c
    core, my_x = lax.axis_index("c"), lax.axis_index("x")
    units, length, width = titles.shape
    hidden = w_up.shape[1]
    width_e = sample_grad.shape[1]
    share_f, share_d = hidden // devices, width // devices

    place = lax.iota(jnp.int32, chips * units)
    chip, unit = place // units, place % units

    def item_part(of_core):
        wanted = (((chip // n_x) * n_c + of_core) * n_x + chip % n_x) * units + unit
        onehot = (sample_item[:, None] == wanted[None, :]).astype(jnp.bfloat16)
        return contract_first(onehot, sample_grad)

    got = swap_cores(item_part(1 - core))
    mine = (item_part(core) + got).reshape(chips, units, width_e)
    item_all = lax.all_to_all(mine, CHIPS, 0, 0, tiled=True)

    slot_count = row_ids.shape[1]
    rows_here = table.shape[0]
    slot_hot = (sample_row[:, None] == lax.iota(jnp.int32, slot_count)[None, :]).astype(
        jnp.bfloat16
    )
    local_rows = (row_ids[0] % rows_here).astype(jnp.float32)
    row_part = jnp.concatenate(
        [
            contract_first(slot_hot, sample_grad),
            jnp.broadcast_to(local_rows[:, None], (slot_count, 128)),
        ],
        axis=1,
    )
    row_all = lax.all_to_all(
        row_part.reshape(devices, slot_count // devices, width_e + 128), DEVICES, 0, 0, tiled=True
    )

    normed_b, slope, mean_act, mean_title = forward(titles, ln_gain, w_up)
    mean_act_b = mean_act.astype(jnp.bfloat16)
    pooled = mean_title + jnp.dot(mean_act_b, w_down, preferred_element_type=jnp.float32)
    lane = lax.iota(jnp.int32, devices * 8)
    source = jnp.where(lane % 8 < share_d, lane // 8 * share_d + lane % 8, -1)
    spread = (lax.iota(jnp.int32, width)[:, None] == source[None, :]).astype(jnp.bfloat16)
    pooled_b = jnp.dot(
        pooled.astype(jnp.bfloat16), spread, preferred_element_type=jnp.float32
    ).astype(jnp.bfloat16)
    item_all, pooled_b = lax.optimization_barrier((item_all, pooled_b))

    item_grad = jnp.sum(item_all, axis=0)
    grad_b = item_grad.astype(jnp.bfloat16)
    d_pooled = contract_last(grad_b, w_proj)
    d_act = contract_last(d_pooled.astype(jnp.bfloat16), w_down) / length

    here = [(lax.axis_index(name), lax.axis_size(name)) for name in CHIPS]
    keep_at = jnp.stack([slot_of(core, at, size) for at, size in here])
    send_at = jnp.stack([slot_of(1 - core, at, size) for at, size in here])
    d_pre, *sums = up_products(
        core.reshape(1), keep_at, send_at, slope, d_act, normed_b, mean_act_b, pooled_b, grad_b
    )
    parts = [
        (keep + swap_cores(send)).reshape(n_z, n_y, n_x, -1, width_e)
        for keep, send in zip(sums[:3], sums[3:])
    ]

    beside = title_grads(d_pre, w_up, titles, ln_gain, d_pooled)
    parts, (d_titles, gain_term) = halve(parts, "xyz", False, tuple(beside))
    beside = row_update(row_all.reshape(slot_count, width_e + 128), table, accum)
    parts, (new_table, new_accum) = halve(parts, "xyz", True, tuple(beside))
    gain_term = gain_term + swap_cores(gain_term)
    for name in ("y", "z"):
        gain_term = gain_term + along(gain_term, name, 1)
        gain_term = gain_term + along(gain_term, name, 2)
    for names in ("yzx", "zxy"):
        parts, _ = halve(parts, names, False)
        parts, _ = halve(parts, names, True)

    flat = [part.reshape(-1, width_e) for part in parts]
    last = jnp.concatenate(
        flat + [gain_term[:, p * width_e : (p + 1) * width_e] for p in range(3)], axis=0
    )
    blocks = jnp.stack([last, along(last, "x", 1), along(last, "x", 2), along(last, "x", 3)])
    ordered = jnp.stack(
        [lax.dynamic_index_in_dim(blocks, my_x ^ j, 0, keepdims=False) for j in range(n_x)]
    )
    starts = [0, share_f + 16, 2 * share_f + 24]
    end = 3 * share_f + 32
    grad_up = jnp.concatenate([ordered[:, at : at + share_f] for at in starts], axis=2)
    grad_up = grad_up.reshape(-1, width).T
    outer = jnp.concatenate(
        [ordered[:, at + share_f : at + share_f + 8] for at in starts], axis=1
    ).reshape(-1, width_e)
    high = outer.astype(jnp.bfloat16)
    low = (outer - high.astype(jnp.float32)).astype(jnp.bfloat16)
    grad_down = contract_last(high, w_proj) + contract_last(low, w_proj)
    grad_proj = ordered[:, share_f + 8 : share_f + 8 + share_d].reshape(-1, width_e)
    gains = jnp.sum(ordered[:, end:].reshape(n_x, 3, 8, width_e), axis=(0, 2)).reshape(width)
    mine_at = (lax.axis_index("z") * n_y + lax.axis_index("y")) * n_c + core
    grad_gain = lax.dynamic_slice_in_dim(gains, mine_at * (width // groups), width // groups, 0)
    return (
        d_titles.reshape(units, length, width),
        grad_up,
        grad_down,
        grad_proj,
        grad_gain,
        new_table,
        new_accum,
    )


def solution(mesh):
    n_table, n_rep = mesh.devices.shape
    side = n_rep
    fine = Mesh(mesh.devices.reshape(n_table // (2 * side), side, 2, n_rep), DEVICES)
    split, tab = P(DEVICES), P(GROUP)
    return jax.shard_map(
        per_device,
        mesh=fine,
        in_specs=(split, P(), P(), P(), P(), split, split, split, split, split, split),
        out_specs=(split, P(None, GROUP), tab, tab, tab, split, split),
        check_vma=False,
    )
```

```python
import functools
import math

import jax
import jax.numpy as jnp
from jax import lax
from jax.experimental import pallas as pl
from jax.experimental.pallas import tpu as pltpu
from jax.sharding import Mesh
from jax.sharding import PartitionSpec as P

GELU_C = 0.7978845608028654
GELU_K = 0.044715
NORM_EPS = 1e-05
LEARN_RATE = 0.1
CHIPS = ("z", "y", "x")
GROUP = ("z", "y", "c")
DEVICES = ("z", "y", "c", "x")
VMEM = 48 << 20


def contract_first(left, right):
    return lax.dot_general(
        left, right, (((0,), (0,)), ((), ())), preferred_element_type=jnp.float32
    )


def contract_last(left, right):
    return lax.dot_general(
        left, right, (((1,), (1,)), ((), ())), preferred_element_type=jnp.float32
    )


def cost(flops, moved, transcendentals=0):
    return pl.CostEstimate(flops=flops, bytes_accessed=moved, transcendentals=transcendentals)


def swap_cores(block):
    return lax.ppermute(block, "c", [(0, 1), (1, 0)])


def along(block, name, step):
    size = lax.axis_size(name)
    return lax.ppermute(block, name, [(i, i ^ step) for i in range(size)])


def partners(name, second):
    sizes = [lax.axis_size(n) for n in DEVICES]
    at = DEVICES.index(name)
    pairs = []
    for index in range(math.prod(sizes)):
        place, rest = [], index
        for size in reversed(sizes):
            place.insert(0, rest % size)
            rest //= size
        place[at] ^= 1 if (place[DEVICES.index("c")] == 1) == second else 3
        to = 0
        for size, p in zip(sizes, place):
            to = to * size + p
        pairs.append((index, to))
    return pairs


def slot_of(core, here, size):
    block = lax.iota(jnp.int32, size) ^ here
    one = jnp.where(block == 0, 0, jnp.where(block == 1, 2, jnp.where(block == 2, 3, 1)))
    two = jnp.where(block < 2, block, 5 - block)
    return jnp.where(core == 0, one, two)


def halve(parts, names, second, also=()):
    kept, sent = [], []
    for part, name in zip(parts, names):
        dim = ("z", "y", "x").index(name)
        middle = part.shape[dim] // 2
        kept.append(lax.slice_in_dim(part, 0, middle, axis=dim))
        sent.append(
            lax.ppermute(
                lax.slice_in_dim(part, middle, None, axis=dim), DEVICES, partners(name, second)
            )
        )
    if also:
        sent, also = lax.optimization_barrier((sent, also))
    return [k + s for k, s in zip(kept, sent)], also


def layer_norm(rows):
    center = jnp.mean(rows, axis=1, keepdims=True)
    offset = rows - center
    inv_scale = lax.rsqrt(jnp.mean(offset * offset, axis=1, keepdims=True) + NORM_EPS)
    return offset * inv_scale, inv_scale


def forward_kernel(units, titles_ref, gain_ref, w_ref, normed_ref, slope_ref, act_ref, mean_ref):
    rows, width = titles_ref.shape
    length = rows // units
    step = 8 * length

    @pl.when(pl.program_id(0) == 0)
    def _():
        for r in range(units // 8):
            block = titles_ref[r * step : (r + 1) * step, :].astype(jnp.float32)
            normed, _ = layer_norm(block)
            normed_ref[r * step : (r + 1) * step, :] = (normed * gain_ref[...]).astype(jnp.bfloat16)
            mean_ref[r * 8 : (r + 1) * 8, :] = jnp.mean(block.reshape(8, length, width), axis=1)

    for r in range(units // 8):
        pre = jnp.dot(
            normed_ref[r * step : (r + 1) * step, :],
            w_ref[...],
            preferred_element_type=jnp.float32,
        )
        square = pre * pre
        tangent = jnp.tanh(pre * (GELU_C + (GELU_C * GELU_K) * square))
        half = 0.5 + 0.5 * tangent
        value = pre * half
        slope = half + value * (1.0 - tangent) * (GELU_C + (3.0 * GELU_C * GELU_K) * square)
        slope_ref[r * step : (r + 1) * step, :] = slope.astype(jnp.bfloat16)
        act_ref[r * 8 : (r + 1) * 8, :] = jnp.mean(value.reshape(8, length, -1), axis=1)


def forward(titles, ln_gain, w_up):
    units, length, width = titles.shape
    rows, hidden = units * length, w_up.shape[1]
    block = 512
    return pl.pallas_call(
        functools.partial(forward_kernel, units),
        grid=(hidden // block,),
        in_specs=[
            pl.BlockSpec((rows, width), lambda i: (0, 0)),
            pl.BlockSpec((1, width), lambda i: (0, 0)),
            pl.BlockSpec((width, block), lambda i: (0, i)),
        ],
        out_specs=[
            pl.BlockSpec((rows, width), lambda i: (0, 0)),
            pl.BlockSpec((rows, block), lambda i: (0, i)),
            pl.BlockSpec((units, block), lambda i: (0, i)),
            pl.BlockSpec((units, width), lambda i: (0, 0)),
        ],
        out_shape=[
            jax.ShapeDtypeStruct((rows, width), jnp.bfloat16),
            jax.ShapeDtypeStruct((rows, hidden), jnp.bfloat16),
            jax.ShapeDtypeStruct((units, hidden), jnp.float32),
            jax.ShapeDtypeStruct((units, width), jnp.float32),
        ],
        compiler_params=pltpu.CompilerParams(vmem_limit_bytes=VMEM),
        cost_estimate=cost(8 * rows * width * hidden, 4 * rows * hidden, rows * hidden),
        name="forward",
    )(titles.reshape(rows, width), ln_gain.reshape(1, width), w_up)


def place_sums(core_ref, keep_at, send_at, ups, down, proj, out_refs):
    slots = proj.shape[0] // 8
    part = down.shape[0] // slots
    n_x = slots // 8
    first = core_ref[0] == 0
    for q in range(slots // 2):
        y, x = q // n_x, q % n_x
        spots = [at[1, y] * n_x + at[2, x] for at in (keep_at, send_at)]
        pair = (y * 2 * n_x + x, (y * 2 + 1) * n_x + x)

        def store(refs, top, rows):
            even, odd = (rows(k) for k in pair)
            end = top + even.shape[0]
            refs[0][spots[0], top:end, :] = jnp.where(first, even, odd)
            refs[1][spots[1], top:end, :] = jnp.where(first, odd, even)

        for index, up, refs in zip(*ups, zip(out_refs[::2], out_refs[1::2])):
            store(refs, 0, lambda k: up[k * part : (k + 1) * part])
            low = index * 8
            store(refs, part, lambda k: down[k * part + low : k * part + low + 8])
            if index == 0:
                store(refs, part + 8, lambda k: proj[k * 8 : (k + 1) * 8])


def first_kernel(
    units, core_ref, keep_at, send_at, slope_ref, act_ref, mean_ref, pool_ref, grad_ref,
    normed_ref, pre_ref, *out_refs
):
    rows, block = slope_ref.shape
    length, step = rows // units, rows // units * 8
    for r in range(units // 8):
        slope = slope_ref[r * step : (r + 1) * step, :].astype(jnp.float32)
        d_pre = slope.reshape(8, length, block) * act_ref[r * 8 : (r + 1) * 8, :][:, None, :]
        pre_ref[r * step : (r + 1) * step, :] = d_pre.reshape(step, block).astype(jnp.bfloat16)
    up = contract_first(pre_ref[...], normed_ref[...])
    down = contract_first(mean_ref[...], grad_ref[...])
    proj = contract_first(pool_ref[...], grad_ref[...])
    place_sums(core_ref, keep_at, send_at, ((0,), (up,)), down, proj, out_refs)


def other_kernel(
    indices, core_ref, keep_at, send_at, pre_ref, mean_ref, pool_ref, grad_ref, *refs
):
    count = len(indices)
    normed = jnp.concatenate([ref[...] for ref in refs[:count]], axis=1)
    up = contract_first(pre_ref[...], normed)
    down = contract_first(mean_ref[...], grad_ref[...])
    wide = grad_ref.shape[1]
    ups = [up[:, p * wide : (p + 1) * wide] for p in range(count)]
    empty = jnp.zeros((pool_ref.shape[1], 1), jnp.float32)
    place_sums(core_ref, keep_at, send_at, (indices, ups), down, empty, refs[count:])


def up_products(tables, indices, left, normed_b, mean_act_b, pooled_b, grad_b):
    rows, hidden = left[0].shape
    units, width_e = grad_b.shape
    sides = tables[1].shape[1]
    slots = 2 * sides * sides
    part = hidden // sides // slots
    tall = [part + 8 + 8 * (index == 0) for index in indices for _ in range(2)]
    first = len(left) == 2

    def columns(array):
        return pl.BlockSpec((array.shape[0], array.shape[1] // sides), lambda i, c, k, s: (0, i))

    def lanes(index):
        return pl.BlockSpec((rows, width_e), lambda i, c, k, s: (0, index))

    def sums(height, table):
        return pl.BlockSpec(
            (slots // 2, height, width_e), lambda i, *tables: (tables[table][0, i], 0, 0)
        )

    out_specs = [sums(h, 1 + n % 2) for n, h in enumerate(tall)]
    out_shape = [jax.ShapeDtypeStruct((sides * slots // 2, h, width_e), jnp.float32) for h in tall]
    if first:
        kernel = functools.partial(first_kernel, units)
        out_specs.insert(0, columns(left[0]))
        out_shape.insert(0, jax.ShapeDtypeStruct((rows, hidden), jnp.bfloat16))
    else:
        kernel = functools.partial(other_kernel, indices)
    return pl.pallas_call(
        kernel,
        grid_spec=pltpu.PrefetchScalarGridSpec(
            num_scalar_prefetch=3,
            grid=(sides,),
            in_specs=[columns(array) for array in left]
            + [columns(mean_act_b), columns(pooled_b)]
            + [pl.BlockSpec(grad_b.shape, lambda i, c, k, s: (0, 0))]
            + [lanes(index) for index in indices],
            out_specs=out_specs,
        ),
        out_shape=out_shape,
        compiler_params=pltpu.CompilerParams(vmem_limit_bytes=VMEM),
        cost_estimate=cost(2 * rows * width_e * len(indices) * hidden, 4 * rows * hidden),
        name="first_products" if first else "other_products",
    )(*tables, *left, mean_act_b, pooled_b, grad_b, *[normed_b] * len(indices))


def titles_kernel(pre_ref, w_ref, titles_ref, gain_ref, pool_ref, out_ref, gain_out):
    rows, width = titles_ref.shape
    units = pool_ref.shape[0]
    length = rows // units
    d_normed = contract_last(pre_ref[...], w_ref[...])
    normed, inv_scale = layer_norm(titles_ref[...].astype(jnp.float32))
    product = d_normed * normed

    @pl.when(pl.program_id(0) == 0)
    def _():
        gain_out[...] = jnp.zeros_like(gain_out)

    gain_out[...] += jnp.sum(product.reshape(rows // 8, 8, width), axis=0)
    d_hat = d_normed * gain_ref[...]
    d_flat = inv_scale * (
        d_hat
        - jnp.mean(d_hat, axis=1, keepdims=True)
        - normed * jnp.mean(d_hat * normed, axis=1, keepdims=True)
    )
    d_block = d_flat.reshape(units, length, width) + (pool_ref[...] * (1.0 / length))[:, None, :]
    out_ref[...] = d_block.reshape(rows, width).astype(jnp.bfloat16)


def title_grads(d_pre, w_up, titles, ln_gain, d_pooled):
    units, length, width = titles.shape
    rows, hidden = d_pre.shape
    step = 8 * length
    return pl.pallas_call(
        titles_kernel,
        grid=(rows // step,),
        in_specs=[
            pl.BlockSpec((step, hidden), lambda i: (i, 0)),
            pl.BlockSpec((width, hidden), lambda i: (0, 0)),
            pl.BlockSpec((step, width), lambda i: (i, 0)),
            pl.BlockSpec((1, width), lambda i: (0, 0)),
            pl.BlockSpec((8, width), lambda i: (i, 0)),
        ],
        out_specs=[
            pl.BlockSpec((step, width), lambda i: (i, 0)),
            pl.BlockSpec((8, width), lambda i: (0, 0)),
        ],
        out_shape=[
            jax.ShapeDtypeStruct((rows, width), jnp.bfloat16),
            jax.ShapeDtypeStruct((8, width), jnp.float32),
        ],
        compiler_params=pltpu.CompilerParams(vmem_limit_bytes=VMEM),
        cost_estimate=cost(2 * rows * width * hidden, 2 * rows * hidden),
        name="title_grads",
    )(d_pre, w_up, titles.reshape(rows, width), ln_gain.reshape(1, width), d_pooled)


def rows_kernel(arrived_ref, table_ref, accum_ref, table_out, accum_out):
    step, width_e = table_ref.shape
    slots = arrived_ref.shape[0]
    grads = arrived_ref[:, :width_e]
    ids = arrived_ref[:, width_e : width_e + 1].astype(jnp.int32)
    here = lax.broadcasted_iota(jnp.int32, (slots, step), 1) + pl.program_id(0) * step
    onehot = jnp.where(here == ids, 1.0, 0.0).astype(jnp.bfloat16)
    high = grads.astype(jnp.bfloat16)
    low = (grads - high.astype(jnp.float32)).astype(jnp.bfloat16)
    row_grad = contract_first(onehot, high) + contract_first(onehot, low)
    new_accum = accum_ref[...] + row_grad * row_grad
    accum_out[...] = new_accum
    table_out[...] = table_ref[...] - LEARN_RATE * row_grad * lax.rsqrt(new_accum)


def row_update(arrived, table, accum):
    rows, width_e = table.shape
    step = 512
    tile = pl.BlockSpec((step, width_e), lambda i: (i, 0))
    return pl.pallas_call(
        rows_kernel,
        grid=(rows // step,),
        in_specs=[pl.BlockSpec(arrived.shape, lambda i: (0, 0)), tile, tile],
        out_specs=[tile, tile],
        out_shape=[jax.ShapeDtypeStruct((rows, width_e), jnp.float32)] * 2,
        compiler_params=pltpu.CompilerParams(vmem_limit_bytes=VMEM),
        cost_estimate=cost(4 * rows * width_e * arrived.shape[0], 16 * rows * width_e),
        name="row_update",
    )(arrived, table, accum)


def per_device(
    titles,
    ln_gain,
    w_up,
    w_down,
    w_proj,
    sample_grad,
    sample_item,
    sample_row,
    row_ids,
    table,
    accum,
):
    n_z, n_y, n_c, n_x = (lax.axis_size(name) for name in DEVICES)
    chips, groups = n_z * n_y * n_x, n_z * n_y * n_c
    devices = chips * n_c
    core, my_x = lax.axis_index("c"), lax.axis_index("x")
    units, length, width = titles.shape
    hidden = w_up.shape[1]
    width_e = sample_grad.shape[1]
    share_f, share_d = hidden // devices, width // devices

    place = lax.iota(jnp.int32, chips * units)
    chip, unit = place // units, place % units

    def item_part(of_core):
        wanted = (((chip // n_x) * n_c + of_core) * n_x + chip % n_x) * units + unit
        onehot = (sample_item[:, None] == wanted[None, :]).astype(jnp.bfloat16)
        return contract_first(onehot, sample_grad)

    got = swap_cores(item_part(1 - core))
    mine = (item_part(core) + got).reshape(chips, units, width_e)
    mine, ln_gain = lax.optimization_barrier((mine, ln_gain))
    item_all = lax.all_to_all(mine, CHIPS, 0, 0, tiled=True)

    slot_count = row_ids.shape[1]
    rows_here = table.shape[0]
    slot_hot = (sample_row[:, None] == lax.iota(jnp.int32, slot_count)[None, :]).astype(
        jnp.bfloat16
    )
    local_rows = (row_ids[0] % rows_here).astype(jnp.float32)
    row_part = jnp.concatenate(
        [
            contract_first(slot_hot, sample_grad),
            jnp.broadcast_to(local_rows[:, None], (slot_count, 128)),
        ],
        axis=1,
    )
    row_part = row_part.reshape(devices, slot_count // devices, width_e + 128)

    normed_b, slope, mean_act, mean_title = forward(titles, ln_gain, w_up)
    mean_act_b = mean_act.astype(jnp.bfloat16)
    pooled = mean_title + jnp.dot(mean_act_b, w_down, preferred_element_type=jnp.float32)
    lane = lax.iota(jnp.int32, devices * 8)
    source = jnp.where(lane % 8 < share_d, lane // 8 * share_d + lane % 8, -1)
    spread = (lax.iota(jnp.int32, width)[:, None] == source[None, :]).astype(jnp.bfloat16)
    pooled_b = jnp.dot(
        pooled.astype(jnp.bfloat16), spread, preferred_element_type=jnp.float32
    ).astype(jnp.bfloat16)
    item_all, pooled_b, row_part = lax.optimization_barrier((item_all, pooled_b, row_part))

    item_grad = jnp.sum(item_all, axis=0)
    grad_b = item_grad.astype(jnp.bfloat16)
    d_pooled = contract_last(grad_b, w_proj)
    d_act = contract_last(d_pooled.astype(jnp.bfloat16), w_down) / length

    here = [(lax.axis_index(name), lax.axis_size(name)) for name in CHIPS]
    keep_at = jnp.stack([slot_of(core, at, size) for at, size in here])
    send_at = jnp.stack([slot_of(1 - core, at, size) for at, size in here])
    tables = (core.reshape(1), keep_at, send_at)
    items = (normed_b, mean_act_b, pooled_b, grad_b)
    d_pre, *sums = up_products(tables, (0,), (slope, d_act), *items)
    sums += up_products(tables, (1, 2), (d_pre,), *items)
    parts = [
        (keep + swap_cores(send)).reshape(n_z, n_y, n_x, -1, width_e)
        for keep, send in zip(sums[::2], sums[1::2])
    ]

    beside = title_grads(d_pre, w_up, titles, ln_gain, d_pooled)
    parts, (d_titles, gain_term) = halve(parts, "xyz", False, tuple(beside))
    parts, row_part = lax.optimization_barrier((parts, row_part))
    row_all = lax.all_to_all(row_part, DEVICES, 0, 0, tiled=True)
    gain_term = (gain_term + swap_cores(gain_term)).reshape(8, 3, width_e)
    gain_term = jnp.pad(jnp.sum(gain_term, axis=0), ((0, 5), (0, 0)))
    parts, (gain_term,) = halve(parts, "xyz", True, (gain_term,))
    gain_term = jnp.broadcast_to(gain_term, parts[0].shape[:3] + gain_term.shape)
    parts[0] = jnp.concatenate([parts[0], gain_term], axis=3)
    parts, _ = halve(parts, "yzx", False)
    parts, (row_all,) = halve(parts, "yzx", True, (row_all,))
    beside = row_update(row_all.reshape(slot_count, width_e + 128), table, accum)
    parts, (new_table, new_accum) = halve(parts, "zxy", False, tuple(beside))
    parts, _ = halve(parts, "zxy", True)

    flat = [part.reshape(-1, width_e) for part in parts]
    last = jnp.concatenate(flat, axis=0)
    blocks = jnp.stack([last, along(last, "x", 1), along(last, "x", 2), along(last, "x", 3)])
    ordered = jnp.stack(
        [lax.dynamic_index_in_dim(blocks, my_x ^ j, 0, keepdims=False) for j in range(n_x)]
    )
    starts = [0, share_f + 24, 2 * share_f + 32]
    grad_up = jnp.concatenate([ordered[:, at : at + share_f] for at in starts], axis=2)
    grad_up = grad_up.reshape(-1, width).T
    outer = jnp.concatenate(
        [ordered[:, at + share_f : at + share_f + 8] for at in starts], axis=1
    ).reshape(-1, width_e)
    high = outer.astype(jnp.bfloat16)
    low = (outer - high.astype(jnp.float32)).astype(jnp.bfloat16)
    grad_down = contract_last(high, w_proj) + contract_last(low, w_proj)
    grad_proj = ordered[:, share_f + 8 : share_f + 8 + share_d].reshape(-1, width_e)
    gains = jnp.sum(ordered[:, share_f + 16 : share_f + 19], axis=0).reshape(width)
    mine_at = (lax.axis_index("z") * n_y + lax.axis_index("y")) * n_c + core
    grad_gain = lax.dynamic_slice_in_dim(gains, mine_at * (width // groups), width // groups, 0)
    return (
        d_titles.reshape(units, length, width),
        grad_up,
        grad_down,
        grad_proj,
        grad_gain,
        new_table,
        new_accum,
    )


def solution(mesh):
    n_table, n_rep = mesh.devices.shape
    side = n_rep
    fine = Mesh(mesh.devices.reshape(n_table // (2 * side), side, 2, n_rep), DEVICES)
    split, tab = P(DEVICES), P(GROUP)
    return jax.shard_map(
        per_device,
        mesh=fine,
        in_specs=(split, P(), P(), P(), P(), split, split, split, split, split, split),
        out_specs=(split, P(None, GROUP), tab, tab, tab, split, split),
        check_vma=False,
    )
```

```python
import functools
import math

import jax
import jax.numpy as jnp
from jax import lax
from jax.experimental import pallas as pl
from jax.experimental.pallas import tpu as pltpu
from jax.sharding import Mesh
from jax.sharding import PartitionSpec as P

GELU_C = 0.7978845608028654
GELU_K = 0.044715
NORM_EPS = 1e-05
LEARN_RATE = 0.1
CHIPS = ("z", "y", "x")
GROUP = ("z", "y", "c")
DEVICES = ("z", "y", "c", "x")
VMEM = 30 << 20


def contract_first(left, right):
    return lax.dot_general(
        left, right, (((0,), (0,)), ((), ())), preferred_element_type=jnp.float32
    )


def contract_last(left, right):
    return lax.dot_general(
        left, right, (((1,), (1,)), ((), ())), preferred_element_type=jnp.float32
    )


def cost(flops, moved, transcendentals=0):
    return pl.CostEstimate(flops=flops, bytes_accessed=moved, transcendentals=transcendentals)


def swap_cores(block):
    return lax.ppermute(block, "c", [(0, 1), (1, 0)])


def along(block, name, step):
    size = lax.axis_size(name)
    return lax.ppermute(block, name, [(i, i ^ step) for i in range(size)])


def partners(name, second):
    sizes = [lax.axis_size(n) for n in DEVICES]
    at = DEVICES.index(name)
    pairs = []
    for index in range(math.prod(sizes)):
        place, rest = [], index
        for size in reversed(sizes):
            place.insert(0, rest % size)
            rest //= size
        place[at] ^= 1 if (place[DEVICES.index("c")] == 1) == second else 3
        to = 0
        for size, p in zip(sizes, place):
            to = to * size + p
        pairs.append((index, to))
    return pairs


def slot_of(core, here, size):
    block = lax.iota(jnp.int32, size) ^ here
    one = jnp.where(block == 0, 0, jnp.where(block == 1, 2, jnp.where(block == 2, 3, 1)))
    two = jnp.where(block < 2, block, 5 - block)
    return jnp.where(core == 0, one, two)


def halve(parts, names, second, also=()):
    kept, sent = [], []
    for part, name in zip(parts, names):
        dim = ("z", "y", "x").index(name)
        middle = part.shape[dim] // 2
        kept.append(lax.slice_in_dim(part, 0, middle, axis=dim))
        sent.append(
            lax.ppermute(
                lax.slice_in_dim(part, middle, None, axis=dim), DEVICES, partners(name, second)
            )
        )
    if also:
        sent, also = lax.optimization_barrier((sent, also))
    return [k + s for k, s in zip(kept, sent)], also


def layer_norm(rows):
    center = jnp.mean(rows, axis=1, keepdims=True)
    offset = rows - center
    inv_scale = lax.rsqrt(jnp.mean(offset * offset, axis=1, keepdims=True) + NORM_EPS)
    return offset * inv_scale, inv_scale


def item_kernel(key_ref, grad_ref, *refs):
    out_ref = refs[-1]
    rows = out_ref.shape[0]
    place = lax.broadcasted_iota(jnp.int32, (rows, key_ref.shape[1]), 0) + pl.program_id(0) * rows
    onehot = jnp.where(place == key_ref[...], 1.0, 0.0).astype(jnp.bfloat16)
    total = jnp.dot(onehot, grad_ref[...], preferred_element_type=jnp.float32)
    for ref in refs[:-1]:
        total = total + ref[...]
    out_ref[...] = total


def segment_sums(key, sample_grad, count, *more):
    samples, width_e = sample_grad.shape
    step = 512
    return pl.pallas_call(
        item_kernel,
        grid=(count // step,),
        in_specs=[
            pl.BlockSpec((1, samples), lambda i: (0, 0)),
            pl.BlockSpec((samples, width_e), lambda i: (0, 0)),
        ]
        + [pl.BlockSpec((step, width_e), lambda i: (i, 0))] * len(more),
        out_specs=pl.BlockSpec((step, width_e), lambda i: (i, 0)),
        out_shape=jax.ShapeDtypeStruct((count, width_e), jnp.float32),
        compiler_params=pltpu.CompilerParams(vmem_limit_bytes=24 << 20),
        cost_estimate=cost(2 * samples * width_e * count, 4 * width_e * count),
        name="segment_sums",
    )(key.reshape(1, samples), sample_grad, *more)


def forward_kernel(units, titles_ref, gain_ref, w_ref, normed_ref, slope_ref, act_ref, mean_ref):
    rows, width = titles_ref.shape
    length = rows // units
    step = 8 * length

    @pl.when(pl.program_id(0) == 0)
    def _():
        for r in range(units // 8):
            block = titles_ref[r * step : (r + 1) * step, :].astype(jnp.float32)
            normed, _ = layer_norm(block)
            normed_ref[r * step : (r + 1) * step, :] = (normed * gain_ref[...]).astype(jnp.bfloat16)
            mean_ref[r * 8 : (r + 1) * 8, :] = jnp.mean(block.reshape(8, length, width), axis=1)

    for r in range(units // 8):
        pre = jnp.dot(
            normed_ref[r * step : (r + 1) * step, :],
            w_ref[...],
            preferred_element_type=jnp.float32,
        )
        square = pre * pre
        tangent = jnp.tanh(pre * (GELU_C + (GELU_C * GELU_K) * square))
        half = 0.5 + 0.5 * tangent
        value = pre * half
        slope = half + value * (1.0 - tangent) * (GELU_C + (3.0 * GELU_C * GELU_K) * square)
        slope_ref[r * step : (r + 1) * step, :] = slope.astype(jnp.bfloat16)
        act_ref[r * 8 : (r + 1) * 8, :] = jnp.mean(value.reshape(8, length, -1), axis=1)


def forward(titles, ln_gain, w_up):
    units, length, width = titles.shape
    rows, hidden = units * length, w_up.shape[1]
    block = 512
    return pl.pallas_call(
        functools.partial(forward_kernel, units),
        grid=(hidden // block,),
        in_specs=[
            pl.BlockSpec((rows, width), lambda i: (0, 0)),
            pl.BlockSpec((1, width), lambda i: (0, 0)),
            pl.BlockSpec((width, block), lambda i: (0, i)),
        ],
        out_specs=[
            pl.BlockSpec((rows, width), lambda i: (0, 0)),
            pl.BlockSpec((rows, block), lambda i: (0, i)),
            pl.BlockSpec((units, block), lambda i: (0, i)),
            pl.BlockSpec((units, width), lambda i: (0, 0)),
        ],
        out_shape=[
            jax.ShapeDtypeStruct((rows, width), jnp.bfloat16),
            pltpu.HBM((rows, hidden), jnp.bfloat16),
            jax.ShapeDtypeStruct((units, hidden), jnp.float32),
            jax.ShapeDtypeStruct((units, width), jnp.float32),
        ],
        compiler_params=pltpu.CompilerParams(vmem_limit_bytes=VMEM),
        cost_estimate=cost(8 * rows * width * hidden, 4 * rows * hidden, rows * hidden),
        name="forward",
    )(titles.reshape(rows, width), ln_gain.reshape(1, width), w_up)


def place_sums(core_ref, keep_at, send_at, ups, down, proj, out_refs):
    slots = proj.shape[0] // 8
    part = down.shape[0] // slots
    n_x = slots // 8
    first = core_ref[0] == 0
    for q in range(slots // 2):
        y, x = q // n_x, q % n_x
        spots = [at[1, y] * n_x + at[2, x] for at in (keep_at, send_at)]
        pair = (y * 2 * n_x + x, (y * 2 + 1) * n_x + x)

        def store(refs, top, rows):
            even, odd = (rows(k) for k in pair)
            end = top + even.shape[0]
            refs[0][spots[0], top:end, :] = jnp.where(first, even, odd)
            refs[1][spots[1], top:end, :] = jnp.where(first, odd, even)

        for index, up, refs in zip(*ups, zip(out_refs[::2], out_refs[1::2])):
            store(refs, 0, lambda k: up[k * part : (k + 1) * part])
            low = index * 8
            store(refs, part, lambda k: down[k * part + low : k * part + low + 8])
            if index == 0:
                store(refs, part + 8, lambda k: proj[k * 8 : (k + 1) * 8])


def first_kernel(
    units, core_ref, keep_at, send_at, slope_ref, act_ref, mean_ref, pool_ref, grad_ref,
    normed_ref, pre_ref, *out_refs
):
    rows, block = slope_ref.shape
    length, step = rows // units, rows // units * 8
    for r in range(units // 8):
        slope = slope_ref[r * step : (r + 1) * step, :].astype(jnp.float32)
        d_pre = slope.reshape(8, length, block) * act_ref[r * 8 : (r + 1) * 8, :][:, None, :]
        pre_ref[r * step : (r + 1) * step, :] = d_pre.reshape(step, block).astype(jnp.bfloat16)
    up = contract_first(pre_ref[...], normed_ref[...])
    down = contract_first(mean_ref[...], grad_ref[...])
    proj = contract_first(pool_ref[...], grad_ref[...])
    place_sums(core_ref, keep_at, send_at, ((0,), (up,)), down, proj, out_refs)


def other_kernel(
    indices, core_ref, keep_at, send_at, pre_ref, mean_ref, pool_ref, grad_ref, *refs
):
    count = len(indices)
    normed = jnp.concatenate([ref[...] for ref in refs[:count]], axis=1)
    up = contract_first(pre_ref[...], normed)
    down = contract_first(mean_ref[...], grad_ref[...])
    wide = grad_ref.shape[1]
    ups = [up[:, p * wide : (p + 1) * wide] for p in range(count)]
    empty = jnp.zeros((pool_ref.shape[1], 1), jnp.float32)
    place_sums(core_ref, keep_at, send_at, (indices, ups), down, empty, refs[count:])


def up_products(tables, indices, left, normed_b, mean_act_b, pooled_b, grad_b):
    rows, hidden = left[0].shape
    units, width_e = grad_b.shape
    sides = tables[1].shape[1]
    slots = 2 * sides * sides
    part = hidden // sides // slots
    tall = [part + 8 + 8 * (index == 0) for index in indices for _ in range(2)]
    first = len(left) == 2

    def columns(array):
        return pl.BlockSpec((array.shape[0], array.shape[1] // sides), lambda i, c, k, s: (0, i))

    def lanes(index):
        return pl.BlockSpec((rows, width_e), lambda i, c, k, s: (0, index))

    def sums(height, table):
        return pl.BlockSpec(
            (slots // 2, height, width_e), lambda i, *tables: (tables[table][0, i], 0, 0)
        )

    out_specs = [sums(h, 1 + n % 2) for n, h in enumerate(tall)]
    out_shape = [jax.ShapeDtypeStruct((sides * slots // 2, h, width_e), jnp.float32) for h in tall]
    if first:
        kernel = functools.partial(first_kernel, units)
        out_specs.insert(0, columns(left[0]))
        out_shape.insert(0, pltpu.VMEM((rows, hidden), jnp.bfloat16))
    else:
        kernel = functools.partial(other_kernel, indices)
    return pl.pallas_call(
        kernel,
        grid_spec=pltpu.PrefetchScalarGridSpec(
            num_scalar_prefetch=3,
            grid=(sides,),
            in_specs=[columns(array) for array in left]
            + [columns(mean_act_b), columns(pooled_b)]
            + [pl.BlockSpec(grad_b.shape, lambda i, c, k, s: (0, 0))]
            + [lanes(index) for index in indices],
            out_specs=out_specs,
        ),
        out_shape=out_shape,
        compiler_params=pltpu.CompilerParams(vmem_limit_bytes=VMEM),
        cost_estimate=cost(2 * rows * width_e * len(indices) * hidden, 4 * rows * hidden),
        name="first_products" if first else "other_products",
    )(*tables, *left, mean_act_b, pooled_b, grad_b, *[normed_b] * len(indices))


def titles_kernel(pre_ref, w_ref, titles_ref, gain_ref, pool_ref, out_ref, gain_out):
    rows, width = titles_ref.shape
    units = pool_ref.shape[0]
    length = rows // units
    d_normed = contract_last(pre_ref[...], w_ref[...])
    normed, inv_scale = layer_norm(titles_ref[...].astype(jnp.float32))
    product = d_normed * normed

    @pl.when(pl.program_id(0) == 0)
    def _():
        gain_out[...] = jnp.zeros_like(gain_out)

    gain_out[...] += jnp.sum(product.reshape(rows // 8, 8, width), axis=0)
    d_hat = d_normed * gain_ref[...]
    d_flat = inv_scale * (
        d_hat
        - jnp.mean(d_hat, axis=1, keepdims=True)
        - normed * jnp.mean(d_hat * normed, axis=1, keepdims=True)
    )
    d_block = d_flat.reshape(units, length, width) + (pool_ref[...] * (1.0 / length))[:, None, :]
    out_ref[...] = d_block.reshape(rows, width).astype(jnp.bfloat16)


def title_grads(d_pre, w_up, titles, ln_gain, d_pooled):
    units, length, width = titles.shape
    rows, hidden = d_pre.shape
    step = 8 * length
    return pl.pallas_call(
        titles_kernel,
        grid=(rows // step,),
        in_specs=[
            pl.BlockSpec((step, hidden), lambda i: (i, 0)),
            pl.BlockSpec((width, hidden), lambda i: (0, 0)),
            pl.BlockSpec((step, width), lambda i: (i, 0)),
            pl.BlockSpec((1, width), lambda i: (0, 0)),
            pl.BlockSpec((8, width), lambda i: (i, 0)),
        ],
        out_specs=[
            pl.BlockSpec((step, width), lambda i: (i, 0)),
            pl.BlockSpec((8, width), lambda i: (0, 0)),
        ],
        out_shape=[
            jax.ShapeDtypeStruct((rows, width), jnp.bfloat16),
            jax.ShapeDtypeStruct((8, width), jnp.float32),
        ],
        compiler_params=pltpu.CompilerParams(vmem_limit_bytes=VMEM),
        cost_estimate=cost(2 * rows * width * hidden, 2 * rows * hidden),
        name="title_grads",
    )(d_pre, w_up, titles.reshape(rows, width), ln_gain.reshape(1, width), d_pooled)


def rows_kernel(arrived_ref, table_ref, accum_ref, table_out, accum_out):
    step, width_e = table_ref.shape
    slots = arrived_ref.shape[0]
    grads = arrived_ref[:, :width_e]
    ids = arrived_ref[:, width_e : width_e + 1].astype(jnp.int32)
    here = lax.broadcasted_iota(jnp.int32, (slots, step), 1) + pl.program_id(0) * step
    onehot = jnp.where(here == ids, 1.0, 0.0).astype(jnp.bfloat16)
    high = grads.astype(jnp.bfloat16)
    low = (grads - high.astype(jnp.float32)).astype(jnp.bfloat16)
    row_grad = contract_first(onehot, high) + contract_first(onehot, low)
    new_accum = accum_ref[...] + row_grad * row_grad
    accum_out[...] = new_accum
    table_out[...] = table_ref[...] - LEARN_RATE * row_grad * lax.rsqrt(new_accum)


def row_update(arrived, table, accum):
    rows, width_e = table.shape
    step = 512
    tile = pl.BlockSpec((step, width_e), lambda i: (i, 0))
    return pl.pallas_call(
        rows_kernel,
        grid=(rows // step,),
        in_specs=[pl.BlockSpec(arrived.shape, lambda i: (0, 0)), tile, tile],
        out_specs=[tile, tile],
        out_shape=[jax.ShapeDtypeStruct((rows, width_e), jnp.float32)] * 2,
        compiler_params=pltpu.CompilerParams(vmem_limit_bytes=16 << 20),
        cost_estimate=cost(4 * rows * width_e * arrived.shape[0], 16 * rows * width_e),
        name="row_update",
    )(arrived, table, accum)


def per_device(
    titles,
    ln_gain,
    w_up,
    w_down,
    w_proj,
    sample_grad,
    sample_item,
    sample_row,
    row_ids,
    table,
    accum,
):
    n_z, n_y, n_c, n_x = (lax.axis_size(name) for name in DEVICES)
    chips, groups = n_z * n_y * n_x, n_z * n_y * n_c
    devices = chips * n_c
    core, my_x = lax.axis_index("c"), lax.axis_index("x")
    units, length, width = titles.shape
    hidden = w_up.shape[1]
    width_e = sample_grad.shape[1]
    share_f, share_d = hidden // devices, width // devices

    owner = sample_item // units
    spot = (owner // (n_c * n_x) * n_x + owner % n_x) * units + sample_item % units
    of_core = owner // n_x % n_c
    sent = segment_sums(jnp.where(of_core == core, -1, spot), sample_grad, chips * units)
    got = swap_cores(sent)
    mine = segment_sums(jnp.where(of_core == core, spot, -1), sample_grad, chips * units, got)
    mine = mine.reshape(chips, units, width_e)
    mine, ln_gain = lax.optimization_barrier((mine, ln_gain))
    item_all = lax.all_to_all(mine, CHIPS, 0, 0, tiled=True)

    slot_count = row_ids.shape[1]
    rows_here = table.shape[0]
    slot_hot = (sample_row[:, None] == lax.iota(jnp.int32, slot_count)[None, :]).astype(
        jnp.bfloat16
    )
    local_rows = (row_ids[0] % rows_here).astype(jnp.float32)
    row_part = jnp.concatenate(
        [
            contract_first(slot_hot, sample_grad),
            jnp.broadcast_to(local_rows[:, None], (slot_count, 128)),
        ],
        axis=1,
    )
    row_part = row_part.reshape(devices, slot_count // devices, width_e + 128)

    normed_b, slope, mean_act, mean_title = forward(titles, ln_gain, w_up)
    mean_act_b = mean_act.astype(jnp.bfloat16)
    pooled = mean_title + jnp.dot(mean_act_b, w_down, preferred_element_type=jnp.float32)
    lane = lax.iota(jnp.int32, devices * 8)
    source = jnp.where(lane % 8 < share_d, lane // 8 * share_d + lane % 8, -1)
    spread = (lax.iota(jnp.int32, width)[:, None] == source[None, :]).astype(jnp.bfloat16)
    pooled_b = jnp.dot(
        pooled.astype(jnp.bfloat16), spread, preferred_element_type=jnp.float32
    ).astype(jnp.bfloat16)
    item_all, pooled_b, row_part = lax.optimization_barrier((item_all, pooled_b, row_part))

    item_grad = jnp.sum(item_all, axis=0)
    grad_b = item_grad.astype(jnp.bfloat16)
    d_pooled = contract_last(grad_b, w_proj)
    d_act = contract_last(d_pooled.astype(jnp.bfloat16), w_down) / length

    here = [(lax.axis_index(name), lax.axis_size(name)) for name in CHIPS]
    keep_at = jnp.stack([slot_of(core, at, size) for at, size in here])
    send_at = jnp.stack([slot_of(1 - core, at, size) for at, size in here])
    tables = (core.reshape(1), keep_at, send_at)
    items = (normed_b, mean_act_b, pooled_b, grad_b)
    slope = pltpu.with_memory_space_constraint(slope, pltpu.HBM)
    d_pre, *sums = up_products(tables, (0,), (slope, d_act), *items)
    d_pre = pltpu.with_memory_space_constraint(d_pre, pltpu.VMEM)
    for index in (1, 2):
        sums += up_products(tables, (index,), (d_pre,), *items)
    parts = [
        (keep + swap_cores(send)).reshape(n_z, n_y, n_x, -1, width_e)
        for keep, send in zip(sums[::2], sums[1::2])
    ]

    beside = title_grads(d_pre, w_up, titles, ln_gain, d_pooled)
    parts, (d_titles, gain_term) = halve(parts, "xyz", False, tuple(beside))
    parts, row_part = lax.optimization_barrier((parts, row_part))
    row_all = lax.all_to_all(row_part, DEVICES, 0, 0, tiled=True)
    gain_term = (gain_term + swap_cores(gain_term)).reshape(8, 3, width_e)
    gain_term = jnp.pad(jnp.sum(gain_term, axis=0), ((0, 5), (0, 0)))
    parts, (gain_term,) = halve(parts, "xyz", True, (gain_term,))
    gain_term = jnp.broadcast_to(gain_term, parts[0].shape[:3] + gain_term.shape)
    parts[0] = jnp.concatenate([parts[0], gain_term], axis=3)
    parts, _ = halve(parts, "yzx", False)
    parts, (row_all,) = halve(parts, "yzx", True, (row_all,))
    beside = row_update(row_all.reshape(slot_count, width_e + 128), table, accum)
    parts, (new_table, new_accum) = halve(parts, "zxy", False, tuple(beside))
    parts, _ = halve(parts, "zxy", True)

    flat = [part.reshape(-1, width_e) for part in parts]
    last = jnp.concatenate(flat, axis=0)
    blocks = jnp.stack([last, along(last, "x", 1), along(last, "x", 2), along(last, "x", 3)])
    ordered = jnp.stack(
        [lax.dynamic_index_in_dim(blocks, my_x ^ j, 0, keepdims=False) for j in range(n_x)]
    )
    starts = [0, share_f + 24, 2 * share_f + 32]
    grad_up = jnp.concatenate([ordered[:, at : at + share_f] for at in starts], axis=2)
    grad_up = grad_up.reshape(-1, width).T
    outer = jnp.concatenate(
        [ordered[:, at + share_f : at + share_f + 8] for at in starts], axis=1
    ).reshape(-1, width_e)
    high = outer.astype(jnp.bfloat16)
    low = (outer - high.astype(jnp.float32)).astype(jnp.bfloat16)
    grad_down = contract_last(high, w_proj) + contract_last(low, w_proj)
    grad_proj = ordered[:, share_f + 8 : share_f + 8 + share_d].reshape(-1, width_e)
    gains = jnp.sum(ordered[:, share_f + 16 : share_f + 19], axis=0).reshape(width)
    mine_at = (lax.axis_index("z") * n_y + lax.axis_index("y")) * n_c + core
    grad_gain = lax.dynamic_slice_in_dim(gains, mine_at * (width // groups), width // groups, 0)
    return (
        d_titles.reshape(units, length, width),
        grad_up,
        grad_down,
        grad_proj,
        grad_gain,
        new_table,
        new_accum,
    )


def solution(mesh):
    n_table, n_rep = mesh.devices.shape
    side = n_rep
    fine = Mesh(mesh.devices.reshape(n_table // (2 * side), side, 2, n_rep), DEVICES)
    split, tab = P(DEVICES), P(GROUP)
    return jax.shard_map(
        per_device,
        mesh=fine,
        in_specs=(split, P(), P(), P(), P(), split, split, split, split, split, split),
        out_specs=(split, P(None, GROUP), tab, tab, tab, split, split),
        check_vma=False,
    )
```

```python
import functools
import math

import jax
import jax.numpy as jnp
from jax import lax
from jax.experimental import pallas as pl
from jax.experimental.pallas import tpu as pltpu
from jax.sharding import Mesh
from jax.sharding import PartitionSpec as P

GELU_C = 0.7978845608028654
GELU_K = 0.044715
NORM_EPS = 1e-05
LEARN_RATE = 0.1
CHIPS = ("z", "y", "x")
GROUP = ("z", "y", "c")
DEVICES = ("z", "y", "c", "x")
VMEM = 30 << 20


def contract_first(left, right):
    return lax.dot_general(
        left, right, (((0,), (0,)), ((), ())), preferred_element_type=jnp.float32
    )


def contract_last(left, right):
    return lax.dot_general(
        left, right, (((1,), (1,)), ((), ())), preferred_element_type=jnp.float32
    )


def cost(flops, moved, transcendentals=0):
    return pl.CostEstimate(flops=flops, bytes_accessed=moved, transcendentals=transcendentals)


def swap_cores(block):
    return lax.ppermute(block, "c", [(0, 1), (1, 0)])


def along(block, name, step):
    size = lax.axis_size(name)
    return lax.ppermute(block, name, [(i, i ^ step) for i in range(size)])


def partners(name, second):
    sizes = [lax.axis_size(n) for n in DEVICES]
    at = DEVICES.index(name)
    pairs = []
    for index in range(math.prod(sizes)):
        place, rest = [], index
        for size in reversed(sizes):
            place.insert(0, rest % size)
            rest //= size
        place[at] ^= 1 if (place[DEVICES.index("c")] == 1) == second else 3
        to = 0
        for size, p in zip(sizes, place):
            to = to * size + p
        pairs.append((index, to))
    return pairs


def slot_of(core, here, size):
    block = lax.iota(jnp.int32, size) ^ here
    one = jnp.where(block == 0, 0, jnp.where(block == 1, 2, jnp.where(block == 2, 3, 1)))
    two = jnp.where(block < 2, block, 5 - block)
    return jnp.where(core == 0, one, two)


def halve(parts, names, second, also=()):
    kept, sent = [], []
    for part, name in zip(parts, names):
        dim = ("z", "y", "x").index(name)
        middle = part.shape[dim] // 2
        kept.append(lax.slice_in_dim(part, 0, middle, axis=dim))
        sent.append(
            lax.ppermute(
                lax.slice_in_dim(part, middle, None, axis=dim), DEVICES, partners(name, second)
            )
        )
    if also:
        sent, also = lax.optimization_barrier((sent, also))
    return [k + s for k, s in zip(kept, sent)], also


def layer_norm(rows):
    center = jnp.mean(rows, axis=1, keepdims=True)
    offset = rows - center
    inv_scale = lax.rsqrt(jnp.mean(offset * offset, axis=1, keepdims=True) + NORM_EPS)
    return offset * inv_scale, inv_scale


def item_kernel(key_ref, grad_ref, *refs):
    out_ref = refs[-1]
    rows = out_ref.shape[0]
    place = lax.broadcasted_iota(jnp.int32, (rows, key_ref.shape[1]), 0) + pl.program_id(0) * rows
    onehot = jnp.where(place == key_ref[...], 1.0, 0.0).astype(jnp.bfloat16)
    total = jnp.dot(onehot, grad_ref[...], preferred_element_type=jnp.float32)
    for ref in refs[:-1]:
        total = total + ref[...]
    out_ref[...] = total


def segment_sums(key, sample_grad, count, *more):
    samples, width_e = sample_grad.shape
    step = 512
    return pl.pallas_call(
        item_kernel,
        grid=(count // step,),
        in_specs=[
            pl.BlockSpec((1, samples), lambda i: (0, 0)),
            pl.BlockSpec((samples, width_e), lambda i: (0, 0)),
        ]
        + [pl.BlockSpec((step, width_e), lambda i: (i, 0))] * len(more),
        out_specs=pl.BlockSpec((step, width_e), lambda i: (i, 0)),
        out_shape=jax.ShapeDtypeStruct((count, width_e), jnp.float32),
        compiler_params=pltpu.CompilerParams(vmem_limit_bytes=24 << 20),
        cost_estimate=cost(2 * samples * width_e * count, 4 * width_e * count),
        name="segment_sums",
    )(key.reshape(1, samples), sample_grad, *more)


def forward_kernel(units, titles_ref, gain_ref, w_ref, normed_ref, slope_ref, act_ref, mean_ref):
    rows, width = titles_ref.shape
    length = rows // units
    step = 8 * length

    @pl.when(pl.program_id(0) == 0)
    def _():
        for r in range(units // 8):
            block = titles_ref[r * step : (r + 1) * step, :].astype(jnp.float32)
            normed, _ = layer_norm(block)
            normed_ref[r * step : (r + 1) * step, :] = (normed * gain_ref[...]).astype(jnp.bfloat16)
            mean_ref[r * 8 : (r + 1) * 8, :] = jnp.mean(block.reshape(8, length, width), axis=1)

    for r in range(units // 8):
        pre = jnp.dot(
            normed_ref[r * step : (r + 1) * step, :],
            w_ref[...],
            preferred_element_type=jnp.float32,
        )
        square = pre * pre
        tangent = jnp.tanh(pre * (GELU_C + (GELU_C * GELU_K) * square))
        half = 0.5 + 0.5 * tangent
        value = pre * half
        slope = half + value * (1.0 - tangent) * (GELU_C + (3.0 * GELU_C * GELU_K) * square)
        slope_ref[r * step : (r + 1) * step, :] = slope.astype(jnp.bfloat16)
        act_ref[r * 8 : (r + 1) * 8, :] = jnp.mean(value.reshape(8, length, -1), axis=1)


def forward(titles, ln_gain, w_up):
    units, length, width = titles.shape
    rows, hidden = units * length, w_up.shape[1]
    block = 512
    return pl.pallas_call(
        functools.partial(forward_kernel, units),
        grid=(hidden // block,),
        in_specs=[
            pl.BlockSpec((rows, width), lambda i: (0, 0)),
            pl.BlockSpec((1, width), lambda i: (0, 0)),
            pl.BlockSpec((width, block), lambda i: (0, i)),
        ],
        out_specs=[
            pl.BlockSpec((rows, width), lambda i: (0, 0)),
            pl.BlockSpec((rows, block), lambda i: (0, i)),
            pl.BlockSpec((units, block), lambda i: (0, i)),
            pl.BlockSpec((units, width), lambda i: (0, 0)),
        ],
        out_shape=[
            jax.ShapeDtypeStruct((rows, width), jnp.bfloat16),
            pltpu.HBM((rows, hidden), jnp.bfloat16),
            jax.ShapeDtypeStruct((units, hidden), jnp.float32),
            jax.ShapeDtypeStruct((units, width), jnp.float32),
        ],
        compiler_params=pltpu.CompilerParams(vmem_limit_bytes=VMEM),
        cost_estimate=cost(8 * rows * width * hidden, 4 * rows * hidden, rows * hidden),
        name="forward",
    )(titles.reshape(rows, width), ln_gain.reshape(1, width), w_up)


def place_sums(core_ref, keep_at, send_at, index, up, down, proj, out_refs):
    slots = 2 * keep_at.shape[1] * keep_at.shape[1]
    part = up.shape[0] // slots
    width_e, width = down.shape[1], up.shape[1]
    half = width_e // 2
    n_x = slots // 8
    first = core_ref[0] == 0
    for q in range(slots // 2):
        y, x = q // n_x, q % n_x
        spots = [at[1, y] * n_x + at[2, x] for at in (keep_at, send_at)]
        pair = (y * 2 * n_x + x, (y * 2 + 1) * n_x + x)

        def store(top, left, rows):
            even, odd = (rows(k) for k in pair)
            end, right = top + even.shape[0], left + even.shape[1]
            out_refs[0][spots[0], top:end, left:right] = jnp.where(first, even, odd)
            out_refs[1][spots[1], top:end, left:right] = jnp.where(first, odd, even)

        store(0, 0, lambda k: up[k * part : (k + 1) * part])
        store(part, 0, lambda k: down[k * part + index * 8 : k * part + index * 8 + 8])
        store(
            part,
            width_e,
            lambda k: down[k * part + 16 : k * part + 24, index * half : (index + 1) * half],
        )
        if index == 0:
            store(part + 8, 0, lambda k: proj[k * 8 : (k + 1) * 8])
            store(part + 8, width_e, lambda k: jnp.zeros((8, width - width_e), jnp.float32))


def first_kernel(
    units, core_ref, keep_at, send_at, slope_ref, act_ref, mean_ref, pool_ref, grad_ref,
    normed_ref, pre_ref, *out_refs
):
    rows, block = slope_ref.shape
    length, step = rows // units, rows // units * 8
    for r in range(units // 8):
        slope = slope_ref[r * step : (r + 1) * step, :].astype(jnp.float32)
        d_pre = slope.reshape(8, length, block) * act_ref[r * 8 : (r + 1) * 8, :][:, None, :]
        pre_ref[r * step : (r + 1) * step, :] = d_pre.reshape(step, block).astype(jnp.bfloat16)
    up = contract_first(pre_ref[...], normed_ref[...])
    down = contract_first(mean_ref[...], grad_ref[...])
    proj = contract_first(pool_ref[...], grad_ref[...])
    place_sums(core_ref, keep_at, send_at, 0, up, down, proj, out_refs)


def other_kernel(
    core_ref, keep_at, send_at, pre_ref, mean_ref, grad_ref, normed_ref, *out_refs
):
    up = contract_first(pre_ref[...], normed_ref[...])
    down = contract_first(mean_ref[...], grad_ref[...])
    place_sums(core_ref, keep_at, send_at, 1, up, down, None, out_refs)


def up_products(tables, index, left, by_column, grad_b, normed_b):
    rows, hidden = left[0].shape
    wide = normed_b.shape[1] // 2
    sides = tables[1].shape[1]
    slots = 2 * sides * sides
    height = hidden // sides // slots + (16, 8)[index]

    def columns(array):
        return pl.BlockSpec((array.shape[0], array.shape[1] // sides), lambda i, c, k, s: (0, i))

    def sums(table):
        return pl.BlockSpec(
            (slots // 2, height, wide), lambda i, *tables: (tables[table][0, i], 0, 0)
        )

    out_specs = [sums(1), sums(2)]
    out_shape = [jax.ShapeDtypeStruct((sides * slots // 2, height, wide), jnp.float32)] * 2
    kernel, name = other_kernel, "other_products"
    if index == 0:
        kernel, name = functools.partial(first_kernel, left[1].shape[0]), "first_products"
        out_specs.insert(0, columns(left[0]))
        out_shape.insert(0, pltpu.VMEM((rows, hidden), jnp.bfloat16))
    return pl.pallas_call(
        kernel,
        grid_spec=pltpu.PrefetchScalarGridSpec(
            num_scalar_prefetch=3,
            grid=(sides,),
            in_specs=[columns(array) for array in left + by_column]
            + [
                pl.BlockSpec(grad_b.shape, lambda i, c, k, s: (0, 0)),
                pl.BlockSpec((rows, wide), lambda i, c, k, s: (0, index)),
            ],
            out_specs=out_specs,
        ),
        out_shape=out_shape,
        compiler_params=pltpu.CompilerParams(vmem_limit_bytes=VMEM),
        cost_estimate=cost(2 * rows * wide * hidden, 4 * rows * hidden),
        name=name,
    )(*tables, *left, *by_column, grad_b, normed_b)


def titles_kernel(pre_ref, w_ref, titles_ref, gain_ref, pool_ref, out_ref, gain_out):
    rows, width = titles_ref.shape
    units = pool_ref.shape[0]
    length = rows // units
    d_normed = contract_last(pre_ref[...], w_ref[...])
    normed, inv_scale = layer_norm(titles_ref[...].astype(jnp.float32))
    product = d_normed * normed

    @pl.when(pl.program_id(0) == 0)
    def _():
        gain_out[...] = jnp.zeros_like(gain_out)

    gain_out[...] += jnp.sum(product.reshape(rows // 8, 8, width), axis=0)
    d_hat = d_normed * gain_ref[...]
    d_flat = inv_scale * (
        d_hat
        - jnp.mean(d_hat, axis=1, keepdims=True)
        - normed * jnp.mean(d_hat * normed, axis=1, keepdims=True)
    )
    d_block = d_flat.reshape(units, length, width) + (pool_ref[...] * (1.0 / length))[:, None, :]
    out_ref[...] = d_block.reshape(rows, width).astype(jnp.bfloat16)


def title_grads(d_pre, w_up, titles, ln_gain, d_pooled):
    units, length, width = titles.shape
    rows, hidden = d_pre.shape
    step = 8 * length
    return pl.pallas_call(
        titles_kernel,
        grid=(rows // step,),
        in_specs=[
            pl.BlockSpec((step, hidden), lambda i: (i, 0)),
            pl.BlockSpec((width, hidden), lambda i: (0, 0)),
            pl.BlockSpec((step, width), lambda i: (i, 0)),
            pl.BlockSpec((1, width), lambda i: (0, 0)),
            pl.BlockSpec((8, width), lambda i: (i, 0)),
        ],
        out_specs=[
            pl.BlockSpec((step, width), lambda i: (i, 0)),
            pl.BlockSpec((8, width), lambda i: (0, 0)),
        ],
        out_shape=[
            jax.ShapeDtypeStruct((rows, width), jnp.bfloat16),
            jax.ShapeDtypeStruct((8, width), jnp.float32),
        ],
        compiler_params=pltpu.CompilerParams(vmem_limit_bytes=VMEM),
        cost_estimate=cost(2 * rows * width * hidden, 2 * rows * hidden),
        name="title_grads",
    )(d_pre, w_up, titles.reshape(rows, width), ln_gain.reshape(1, width), d_pooled)


def rows_kernel(arrived_ref, table_ref, accum_ref, table_out, accum_out):
    step, width_e = table_ref.shape
    slots = arrived_ref.shape[0]
    grads = arrived_ref[:, :width_e]
    ids = arrived_ref[:, width_e : width_e + 1].astype(jnp.int32)
    here = lax.broadcasted_iota(jnp.int32, (slots, step), 1) + pl.program_id(0) * step
    onehot = jnp.where(here == ids, 1.0, 0.0).astype(jnp.bfloat16)
    high = grads.astype(jnp.bfloat16)
    low = (grads - high.astype(jnp.float32)).astype(jnp.bfloat16)
    row_grad = contract_first(onehot, high) + contract_first(onehot, low)
    new_accum = accum_ref[...] + row_grad * row_grad
    accum_out[...] = new_accum
    table_out[...] = table_ref[...] - LEARN_RATE * row_grad * lax.rsqrt(new_accum)


def row_update(arrived, table, accum):
    rows, width_e = table.shape
    step = 512
    tile = pl.BlockSpec((step, width_e), lambda i: (i, 0))
    return pl.pallas_call(
        rows_kernel,
        grid=(rows // step,),
        in_specs=[pl.BlockSpec(arrived.shape, lambda i: (0, 0)), tile, tile],
        out_specs=[tile, tile],
        out_shape=[jax.ShapeDtypeStruct((rows, width_e), jnp.float32)] * 2,
        compiler_params=pltpu.CompilerParams(vmem_limit_bytes=16 << 20),
        cost_estimate=cost(4 * rows * width_e * arrived.shape[0], 16 * rows * width_e),
        name="row_update",
    )(arrived, table, accum)


def per_device(
    titles,
    ln_gain,
    w_up,
    w_down,
    w_proj,
    sample_grad,
    sample_item,
    sample_row,
    row_ids,
    table,
    accum,
):
    n_z, n_y, n_c, n_x = (lax.axis_size(name) for name in DEVICES)
    chips, groups = n_z * n_y * n_x, n_z * n_y * n_c
    devices = chips * n_c
    core, my_x = lax.axis_index("c"), lax.axis_index("x")
    units, length, width = titles.shape
    hidden = w_up.shape[1]
    width_e = sample_grad.shape[1]
    share_f, share_d = hidden // devices, width // devices

    owner = sample_item // units
    spot = (owner // (n_c * n_x) * n_x + owner % n_x) * units + sample_item % units
    of_core = owner // n_x % n_c
    sent = segment_sums(jnp.where(of_core == core, -1, spot), sample_grad, chips * units)
    got = swap_cores(sent)
    mine = segment_sums(jnp.where(of_core == core, spot, -1), sample_grad, chips * units, got)
    mine = mine.reshape(chips, units, width_e)
    mine, ln_gain = lax.optimization_barrier((mine, ln_gain))
    item_all = lax.all_to_all(mine, CHIPS, 0, 0, tiled=True)

    slot_count = row_ids.shape[1]
    rows_here = table.shape[0]
    slot_hot = (sample_row[:, None] == lax.iota(jnp.int32, slot_count)[None, :]).astype(
        jnp.bfloat16
    )
    local_rows = (row_ids[0] % rows_here).astype(jnp.float32)
    row_part = jnp.concatenate(
        [
            contract_first(slot_hot, sample_grad),
            jnp.broadcast_to(local_rows[:, None], (slot_count, 128)),
        ],
        axis=1,
    )
    row_part = row_part.reshape(devices, slot_count // devices, width_e + 128)

    normed_b, slope, mean_act, mean_title = forward(titles, ln_gain, w_up)
    mean_act_b = mean_act.astype(jnp.bfloat16)
    pooled = mean_title + jnp.dot(mean_act_b, w_down, preferred_element_type=jnp.float32)
    lane = lax.iota(jnp.int32, devices * 8)
    source = jnp.where(lane % 8 < share_d, lane // 8 * share_d + lane % 8, -1)
    spread = (lax.iota(jnp.int32, width)[:, None] == source[None, :]).astype(jnp.bfloat16)
    pooled_b = jnp.dot(
        pooled.astype(jnp.bfloat16), spread, preferred_element_type=jnp.float32
    ).astype(jnp.bfloat16)
    item_all, pooled_b, row_part = lax.optimization_barrier((item_all, pooled_b, row_part))

    item_grad = jnp.sum(item_all, axis=0)
    grad_b = item_grad.astype(jnp.bfloat16)
    d_pooled = contract_last(grad_b, w_proj)
    d_act = contract_last(d_pooled.astype(jnp.bfloat16), w_down) / length

    here = [(lax.axis_index(name), lax.axis_size(name)) for name in CHIPS]
    keep_at = jnp.stack([slot_of(core, at, size) for at, size in here])
    send_at = jnp.stack([slot_of(1 - core, at, size) for at, size in here])
    tables = (core.reshape(1), keep_at, send_at)
    slope = pltpu.with_memory_space_constraint(slope, pltpu.HBM)
    d_pre, *sums = up_products(
        tables, 0, (slope, d_act), (mean_act_b, pooled_b), grad_b, normed_b
    )
    d_pre = pltpu.with_memory_space_constraint(d_pre, pltpu.VMEM)
    sums += up_products(tables, 1, (d_pre,), (mean_act_b,), grad_b, normed_b)
    parts = [
        (keep + swap_cores(send)).reshape(n_z, n_y, n_x, -1, width // 2)
        for keep, send in zip(sums[::2], sums[1::2])
    ]

    d_titles, gain_term = title_grads(d_pre, w_up, titles, ln_gain, d_pooled)
    gain_term, row_part = lax.optimization_barrier((gain_term, row_part))
    row_all = lax.all_to_all(row_part, DEVICES, 0, 0, tiled=True)
    parts, (d_titles, gain_term) = halve(parts, "xy", False, (d_titles, gain_term))
    gain_term = (gain_term + swap_cores(gain_term)).reshape(8, -1, 128)
    gain_term = jnp.sum(gain_term, axis=0)
    gain_term = jnp.pad(
        gain_term, ((share_f + 8, 8 - gain_term.shape[0]), (width // 2 - 128, 0))
    )
    parts, (gain_term,) = halve(parts, "xy", True, (gain_term,))
    parts[0] = parts[0] + gain_term
    parts, _ = halve(parts, "yx", False)
    parts, (row_all,) = halve(parts, "yx", True, (row_all,))
    both = [jnp.concatenate(parts, axis=3)]
    beside = row_update(row_all.reshape(slot_count, width_e + 128), table, accum)
    both, (new_table, new_accum) = halve(both, "z", False, tuple(beside))
    both, _ = halve(both, "z", True)

    last = both[0].reshape(-1, width // 2)
    blocks = jnp.stack([last, along(last, "x", 1), along(last, "x", 2), along(last, "x", 3)])
    ordered = jnp.stack(
        [lax.dynamic_index_in_dim(blocks, my_x ^ j, 0, keepdims=False) for j in range(n_x)]
    )
    one, two = ordered[:, : share_f + 16], ordered[:, share_f + 16 :]
    grad_up = jnp.concatenate([one[:, :share_f], two[:, :share_f]], axis=2).reshape(-1, width).T
    one, two, tail = one[:, share_f : share_f + 8], two[:, share_f:], one[:, share_f + 8 :]
    third = jnp.concatenate([one[:, :, width_e:], two[:, :, width_e:]], axis=2)
    outer = jnp.concatenate([one[:, :, :width_e], two[:, :, :width_e], third], axis=1)
    outer = outer.reshape(-1, width_e)
    high = outer.astype(jnp.bfloat16)
    low = (outer - high.astype(jnp.float32)).astype(jnp.bfloat16)
    grad_down = contract_last(high, w_proj) + contract_last(low, w_proj)
    grad_proj = tail[:, :share_d, :width_e].reshape(-1, width_e)
    gains = jnp.sum(tail[:, : width // 128, width_e:], axis=0).reshape(width)
    mine_at = (lax.axis_index("z") * n_y + lax.axis_index("y")) * n_c + core
    grad_gain = lax.dynamic_slice_in_dim(gains, mine_at * (width // groups), width // groups, 0)
    return (
        d_titles.reshape(units, length, width),
        grad_up,
        grad_down,
        grad_proj,
        grad_gain,
        new_table,
        new_accum,
    )


def solution(mesh):
    n_table, n_rep = mesh.devices.shape
    side = n_rep
    fine = Mesh(mesh.devices.reshape(n_table // (2 * side), side, 2, n_rep), DEVICES)
    split, tab = P(DEVICES), P(GROUP)
    return jax.shard_map(
        per_device,
        mesh=fine,
        in_specs=(split, P(), P(), P(), P(), split, split, split, split, split, split),
        out_specs=(split, P(None, GROUP), tab, tab, tab, split, split),
        check_vma=False,
    )
```

```python
import functools
import math

import jax
import jax.numpy as jnp
from jax import lax
from jax.experimental import pallas as pl
from jax.experimental.pallas import tpu as pltpu
from jax.sharding import Mesh
from jax.sharding import PartitionSpec as P

GELU_C = 0.7978845608028654
GELU_K = 0.044715
NORM_EPS = 1e-05
LEARN_RATE = 0.1
CHIPS = ("z", "y", "x")
GROUP = ("z", "y", "c")
DEVICES = ("z", "y", "c", "x")
VMEM = 26 << 20


def contract_first(left, right):
    return lax.dot_general(
        left, right, (((0,), (0,)), ((), ())), preferred_element_type=jnp.float32
    )


def contract_last(left, right):
    return lax.dot_general(
        left, right, (((1,), (1,)), ((), ())), preferred_element_type=jnp.float32
    )


def cost(flops, moved, transcendentals=0):
    return pl.CostEstimate(flops=flops, bytes_accessed=moved, transcendentals=transcendentals)


def swap_cores(block):
    return lax.ppermute(block, "c", [(0, 1), (1, 0)])


def along(block, name, step):
    size = lax.axis_size(name)
    return lax.ppermute(block, name, [(i, i ^ step) for i in range(size)])


def partners(name, second):
    sizes = [lax.axis_size(n) for n in DEVICES]
    at = DEVICES.index(name)
    pairs = []
    for index in range(math.prod(sizes)):
        place, rest = [], index
        for size in reversed(sizes):
            place.insert(0, rest % size)
            rest //= size
        place[at] ^= 1 if (place[DEVICES.index("c")] == 1) == second else 3
        to = 0
        for size, p in zip(sizes, place):
            to = to * size + p
        pairs.append((index, to))
    return pairs


def slot_of(core, here, size):
    block = lax.iota(jnp.int32, size) ^ here
    one = jnp.where(block == 0, 0, jnp.where(block == 1, 2, jnp.where(block == 2, 3, 1)))
    two = jnp.where(block < 2, block, 5 - block)
    return jnp.where(core == 0, one, two)


def halve(parts, names, second, also=()):
    kept, sent = [], []
    for part, name in zip(parts, names):
        dim = ("z", "y", "x").index(name)
        middle = part.shape[dim] // 2
        kept.append(lax.slice_in_dim(part, 0, middle, axis=dim))
        sent.append(
            lax.ppermute(
                lax.slice_in_dim(part, middle, None, axis=dim), DEVICES, partners(name, second)
            )
        )
    if also:
        sent, also = lax.optimization_barrier((sent, also))
    return [k + s for k, s in zip(kept, sent)], also


def layer_norm(rows):
    center = jnp.mean(rows, axis=1, keepdims=True)
    offset = rows - center
    inv_scale = lax.rsqrt(jnp.mean(offset * offset, axis=1, keepdims=True) + NORM_EPS)
    return offset * inv_scale, inv_scale


def item_kernel(key_ref, grad_ref, *refs):
    out_ref = refs[-1]
    rows = out_ref.shape[0]
    place = lax.broadcasted_iota(jnp.int32, (rows, key_ref.shape[1]), 0) + pl.program_id(0) * rows
    onehot = jnp.where(place == key_ref[...], 1.0, 0.0).astype(jnp.bfloat16)
    total = jnp.dot(onehot, grad_ref[...], preferred_element_type=jnp.float32)
    for ref in refs[:-1]:
        total = total + ref[...]
    out_ref[...] = total


def segment_sums(key, sample_grad, count, *more):
    samples, width_e = sample_grad.shape
    step = 512
    return pl.pallas_call(
        item_kernel,
        grid=(count // step,),
        in_specs=[
            pl.BlockSpec((1, samples), lambda i: (0, 0)),
            pl.BlockSpec((samples, width_e), lambda i: (0, 0)),
        ]
        + [pl.BlockSpec((step, width_e), lambda i: (i, 0))] * len(more),
        out_specs=pl.BlockSpec((step, width_e), lambda i: (i, 0)),
        out_shape=jax.ShapeDtypeStruct((count, width_e), jnp.float32),
        compiler_params=pltpu.CompilerParams(vmem_limit_bytes=24 << 20),
        cost_estimate=cost(2 * samples * width_e * count, 4 * width_e * count),
        name="segment_sums",
    )(key.reshape(1, samples), sample_grad, *more)


def forward_kernel(units, titles_ref, gain_ref, w_ref, normed_ref, slope_ref, act_ref, mean_ref):
    rows, width = titles_ref.shape
    length = rows // units
    step = 8 * length

    @pl.when(pl.program_id(0) == 0)
    def _():
        for r in range(units // 8):
            block = titles_ref[r * step : (r + 1) * step, :].astype(jnp.float32)
            normed, _ = layer_norm(block)
            normed_ref[r * step : (r + 1) * step, :] = (normed * gain_ref[...]).astype(jnp.bfloat16)
            mean_ref[r * 8 : (r + 1) * 8, :] = jnp.mean(block.reshape(8, length, width), axis=1)

    for r in range(units // 8):
        pre = jnp.dot(
            normed_ref[r * step : (r + 1) * step, :],
            w_ref[...],
            preferred_element_type=jnp.float32,
        )
        square = pre * pre
        tangent = jnp.tanh(pre * (GELU_C + (GELU_C * GELU_K) * square))
        half = 0.5 + 0.5 * tangent
        value = pre * half
        slope = half + value * (1.0 - tangent) * (GELU_C + (3.0 * GELU_C * GELU_K) * square)
        slope_ref[r * step : (r + 1) * step, :] = slope.astype(jnp.bfloat16)
        act_ref[r * 8 : (r + 1) * 8, :] = jnp.mean(value.reshape(8, length, -1), axis=1)


def forward(titles, ln_gain, w_up):
    units, length, width = titles.shape
    rows, hidden = units * length, w_up.shape[1]
    block = 512
    return pl.pallas_call(
        functools.partial(forward_kernel, units),
        grid=(hidden // block,),
        in_specs=[
            pl.BlockSpec((rows, width), lambda i: (0, 0)),
            pl.BlockSpec((1, width), lambda i: (0, 0)),
            pl.BlockSpec((width, block), lambda i: (0, i)),
        ],
        out_specs=[
            pl.BlockSpec((rows, width), lambda i: (0, 0)),
            pl.BlockSpec((rows, block), lambda i: (0, i)),
            pl.BlockSpec((units, block), lambda i: (0, i)),
            pl.BlockSpec((units, width), lambda i: (0, 0)),
        ],
        out_shape=[
            jax.ShapeDtypeStruct((rows, width), jnp.bfloat16),
            pltpu.HBM((rows, hidden), jnp.bfloat16),
            jax.ShapeDtypeStruct((units, hidden), jnp.float32),
            jax.ShapeDtypeStruct((units, width), jnp.float32),
        ],
        compiler_params=pltpu.CompilerParams(vmem_limit_bytes=24 << 20),
        cost_estimate=cost(8 * rows * width * hidden, 4 * rows * hidden, rows * hidden),
        name="forward",
    )(titles.reshape(rows, width), ln_gain.reshape(1, width), w_up)


def place_sums(core_ref, keep_at, send_at, index, up, down, proj, out_refs):
    slots = 2 * keep_at.shape[1] * keep_at.shape[1]
    part = up.shape[0] // slots
    width_e, width = down.shape[1], up.shape[1]
    half = width_e // 2
    n_x = slots // 8
    first = core_ref[0] == 0
    for q in range(slots // 2):
        y, x = q // n_x, q % n_x
        spots = [at[1, y] * n_x + at[2, x] for at in (keep_at, send_at)]
        pair = (y * 2 * n_x + x, (y * 2 + 1) * n_x + x)

        def store(top, left, rows):
            even, odd = (rows(k) for k in pair)
            end, right = top + even.shape[0], left + even.shape[1]
            out_refs[0][spots[0], top:end, left:right] = jnp.where(first, even, odd)
            out_refs[1][spots[1], top:end, left:right] = jnp.where(first, odd, even)

        store(0, 0, lambda k: up[k * part : (k + 1) * part])
        store(part, 0, lambda k: down[k * part + index * 8 : k * part + index * 8 + 8])
        store(
            part,
            width_e,
            lambda k: down[k * part + 16 : k * part + 24, index * half : (index + 1) * half],
        )
        if index == 0:
            store(part + 8, 0, lambda k: proj[k * 8 : (k + 1) * 8])
            store(part + 8, width_e, lambda k: jnp.zeros((8, width - width_e), jnp.float32))


def first_kernel(
    units, core_ref, keep_at, send_at, slope_ref, act_ref, mean_ref, pool_ref, grad_ref,
    normed_ref, pre_ref, *out_refs
):
    rows, block = slope_ref.shape
    length, step = rows // units, rows // units * 8
    for r in range(units // 8):
        slope = slope_ref[r * step : (r + 1) * step, :].astype(jnp.float32)
        d_pre = slope.reshape(8, length, block) * act_ref[r * 8 : (r + 1) * 8, :][:, None, :]
        pre_ref[r * step : (r + 1) * step, :] = d_pre.reshape(step, block).astype(jnp.bfloat16)
    up = contract_first(pre_ref[...], normed_ref[...])
    down = contract_first(mean_ref[...], grad_ref[...])
    proj = contract_first(pool_ref[...], grad_ref[...])
    place_sums(core_ref, keep_at, send_at, 0, up, down, proj, out_refs)


def other_kernel(
    core_ref, keep_at, send_at, pre_ref, mean_ref, grad_ref, normed_ref, *out_refs
):
    up = contract_first(pre_ref[...], normed_ref[...])
    down = contract_first(mean_ref[...], grad_ref[...])
    place_sums(core_ref, keep_at, send_at, 1, up, down, None, out_refs)


def up_products(tables, index, left, by_column, grad_b, normed_b):
    rows, hidden = left[0].shape
    wide = normed_b.shape[1] // 2
    sides = tables[1].shape[1]
    slots = 2 * sides * sides
    height = hidden // sides // slots + (16, 8)[index]

    def columns(array):
        return pl.BlockSpec((array.shape[0], array.shape[1] // sides), lambda i, c, k, s: (0, i))

    def sums(table):
        return pl.BlockSpec(
            (slots // 2, height, wide), lambda i, *tables: (tables[table][0, i], 0, 0)
        )

    out_specs = [sums(1), sums(2)]
    out_shape = [jax.ShapeDtypeStruct((sides * slots // 2, height, wide), jnp.float32)] * 2
    kernel, name = other_kernel, "other_products"
    if index == 0:
        kernel, name = functools.partial(first_kernel, left[1].shape[0]), "first_products"
        out_specs.insert(0, columns(left[0]))
        out_shape.insert(0, pltpu.VMEM((rows, hidden), jnp.bfloat16))
    return pl.pallas_call(
        kernel,
        grid_spec=pltpu.PrefetchScalarGridSpec(
            num_scalar_prefetch=3,
            grid=(sides,),
            in_specs=[columns(array) for array in left + by_column]
            + [
                pl.BlockSpec(grad_b.shape, lambda i, c, k, s: (0, 0)),
                pl.BlockSpec((rows, wide), lambda i, c, k, s: (0, index)),
            ],
            out_specs=out_specs,
        ),
        out_shape=out_shape,
        compiler_params=pltpu.CompilerParams(vmem_limit_bytes=14 << 20),
        cost_estimate=cost(2 * rows * wide * hidden, 4 * rows * hidden),
        name=name,
    )(*tables, *left, *by_column, grad_b, normed_b)


def titles_kernel(pre_ref, w_ref, titles_ref, gain_ref, pool_ref, out_ref, gain_out):
    rows, width = titles_ref.shape
    units = pool_ref.shape[0]
    length = rows // units
    d_normed = contract_last(pre_ref[...], w_ref[...])
    normed, inv_scale = layer_norm(titles_ref[...].astype(jnp.float32))
    product = d_normed * normed

    @pl.when(pl.program_id(0) == 0)
    def _():
        gain_out[...] = jnp.zeros_like(gain_out)

    gain_out[...] += jnp.sum(product.reshape(rows // 8, 8, width), axis=0)
    d_hat = d_normed * gain_ref[...]
    d_flat = inv_scale * (
        d_hat
        - jnp.mean(d_hat, axis=1, keepdims=True)
        - normed * jnp.mean(d_hat * normed, axis=1, keepdims=True)
    )
    d_block = d_flat.reshape(units, length, width) + (pool_ref[...] * (1.0 / length))[:, None, :]
    out_ref[...] = d_block.reshape(rows, width).astype(jnp.bfloat16)


def title_grads(d_pre, w_up, titles, ln_gain, d_pooled):
    units, length, width = titles.shape
    rows, hidden = d_pre.shape
    step = 8 * length
    return pl.pallas_call(
        titles_kernel,
        grid=(rows // step,),
        in_specs=[
            pl.BlockSpec((step, hidden), lambda i: (i, 0)),
            pl.BlockSpec((width, hidden), lambda i: (0, 0)),
            pl.BlockSpec((step, width), lambda i: (i, 0)),
            pl.BlockSpec((1, width), lambda i: (0, 0)),
            pl.BlockSpec((8, width), lambda i: (i, 0)),
        ],
        out_specs=[
            pl.BlockSpec((step, width), lambda i: (i, 0)),
            pl.BlockSpec((8, width), lambda i: (0, 0)),
        ],
        out_shape=[
            jax.ShapeDtypeStruct((rows, width), jnp.bfloat16),
            jax.ShapeDtypeStruct((8, width), jnp.float32),
        ],
        compiler_params=pltpu.CompilerParams(vmem_limit_bytes=VMEM),
        cost_estimate=cost(2 * rows * width * hidden, 2 * rows * hidden),
        name="title_grads",
    )(d_pre, w_up, titles.reshape(rows, width), ln_gain.reshape(1, width), d_pooled)


def rows_kernel(arrived_ref, table_ref, accum_ref, table_out, accum_out):
    step, width_e = table_ref.shape
    slots = arrived_ref.shape[0]
    grads = arrived_ref[:, :width_e]
    ids = arrived_ref[:, width_e : width_e + 1].astype(jnp.int32)
    here = lax.broadcasted_iota(jnp.int32, (slots, step), 1) + pl.program_id(0) * step
    onehot = jnp.where(here == ids, 1.0, 0.0).astype(jnp.bfloat16)
    high = grads.astype(jnp.bfloat16)
    low = (grads - high.astype(jnp.float32)).astype(jnp.bfloat16)
    row_grad = contract_first(onehot, high) + contract_first(onehot, low)
    new_accum = accum_ref[...] + row_grad * row_grad
    accum_out[...] = new_accum
    table_out[...] = table_ref[...] - LEARN_RATE * row_grad * lax.rsqrt(new_accum)


def row_update(arrived, table, accum):
    rows, width_e = table.shape
    step = 512
    tile = pl.BlockSpec((step, width_e), lambda i: (i, 0))
    return pl.pallas_call(
        rows_kernel,
        grid=(rows // step,),
        in_specs=[pl.BlockSpec(arrived.shape, lambda i: (0, 0)), tile, tile],
        out_specs=[tile, tile],
        out_shape=[jax.ShapeDtypeStruct((rows, width_e), jnp.float32)] * 2,
        compiler_params=pltpu.CompilerParams(vmem_limit_bytes=16 << 20),
        cost_estimate=cost(4 * rows * width_e * arrived.shape[0], 16 * rows * width_e),
        name="row_update",
    )(arrived, table, accum)


def per_device(
    titles,
    ln_gain,
    w_up,
    w_down,
    w_proj,
    sample_grad,
    sample_item,
    sample_row,
    row_ids,
    table,
    accum,
):
    n_z, n_y, n_c, n_x = (lax.axis_size(name) for name in DEVICES)
    chips, groups = n_z * n_y * n_x, n_z * n_y * n_c
    devices = chips * n_c
    core, my_x = lax.axis_index("c"), lax.axis_index("x")
    units, length, width = titles.shape
    hidden = w_up.shape[1]
    width_e = sample_grad.shape[1]
    share_f, share_d = hidden // devices, width // devices

    owner = sample_item // units
    spot = (owner // (n_c * n_x) * n_x + owner % n_x) * units + sample_item % units
    of_core = owner // n_x % n_c
    sent = segment_sums(jnp.where(of_core == core, -1, spot), sample_grad, chips * units)
    got = swap_cores(sent)
    mine = segment_sums(jnp.where(of_core == core, spot, -1), sample_grad, chips * units, got)
    mine = mine.reshape(chips, units, width_e)
    mine, ln_gain = lax.optimization_barrier((mine, ln_gain))
    item_all = lax.all_to_all(mine, CHIPS, 0, 0, tiled=True)

    slot_count = row_ids.shape[1]
    rows_here = table.shape[0]
    slot_hot = (sample_row[:, None] == lax.iota(jnp.int32, slot_count)[None, :]).astype(
        jnp.bfloat16
    )
    local_rows = (row_ids[0] % rows_here).astype(jnp.float32)
    row_part = jnp.concatenate(
        [
            contract_first(slot_hot, sample_grad),
            jnp.broadcast_to(local_rows[:, None], (slot_count, 128)),
        ],
        axis=1,
    )
    row_part = row_part.reshape(devices, slot_count // devices, width_e + 128)

    normed_b, slope, mean_act, mean_title = forward(titles, ln_gain, w_up)
    mean_act_b = mean_act.astype(jnp.bfloat16)
    pooled = mean_title + jnp.dot(mean_act_b, w_down, preferred_element_type=jnp.float32)
    lane = lax.iota(jnp.int32, devices * 8)
    source = jnp.where(lane % 8 < share_d, lane // 8 * share_d + lane % 8, -1)
    spread = (lax.iota(jnp.int32, width)[:, None] == source[None, :]).astype(jnp.bfloat16)
    pooled_b = jnp.dot(
        pooled.astype(jnp.bfloat16), spread, preferred_element_type=jnp.float32
    ).astype(jnp.bfloat16)
    item_all, pooled_b, row_part = lax.optimization_barrier((item_all, pooled_b, row_part))

    item_grad = jnp.sum(item_all, axis=0)
    grad_b = item_grad.astype(jnp.bfloat16)
    d_pooled = contract_last(grad_b, w_proj)
    d_act = contract_last(d_pooled.astype(jnp.bfloat16), w_down) / length

    here = [(lax.axis_index(name), lax.axis_size(name)) for name in CHIPS]
    keep_at = jnp.stack([slot_of(core, at, size) for at, size in here])
    send_at = jnp.stack([slot_of(1 - core, at, size) for at, size in here])
    tables = (core.reshape(1), keep_at, send_at)
    slope = pltpu.with_memory_space_constraint(slope, pltpu.HBM)
    d_pre, *sums = up_products(
        tables, 0, (slope, d_act), (mean_act_b, pooled_b), grad_b, normed_b
    )
    d_pre = pltpu.with_memory_space_constraint(d_pre, pltpu.VMEM)
    sums += up_products(tables, 1, (d_pre,), (mean_act_b,), grad_b, normed_b)
    row_all = lax.all_to_all(row_part, DEVICES, 0, 0, tiled=True)
    sums[3], row_all = lax.optimization_barrier((sums[3], row_all))
    parts = [
        (keep + swap_cores(send)).reshape(n_z, n_y, n_x, -1, width // 2)
        for keep, send in zip(sums[::2], sums[1::2])
    ]

    d_titles, gain_term = title_grads(d_pre, w_up, titles, ln_gain, d_pooled)
    beside = row_update(row_all.reshape(slot_count, width_e + 128), table, accum)
    parts, (d_titles, gain_term, new_table, new_accum) = halve(
        parts, "xy", False, (d_titles, gain_term, *beside)
    )
    gain_term = (gain_term + swap_cores(gain_term)).reshape(8, -1, 128)
    gain_term = jnp.sum(gain_term, axis=0)
    gain_term = jnp.pad(
        gain_term, ((share_f + 8, 8 - gain_term.shape[0]), (width // 2 - 128, 0))
    )
    parts, (gain_term,) = halve(parts, "xy", True, (gain_term,))
    parts[0] = parts[0] + gain_term
    parts, _ = halve(parts, "yx", False)
    parts, _ = halve(parts, "yx", True)
    both = [jnp.concatenate(parts, axis=3)]
    both, _ = halve(both, "z", False)
    both, _ = halve(both, "z", True)

    last = both[0].reshape(-1, width // 2)
    blocks = jnp.stack([last, along(last, "x", 1), along(last, "x", 2), along(last, "x", 3)])
    ordered = jnp.stack(
        [lax.dynamic_index_in_dim(blocks, my_x ^ j, 0, keepdims=False) for j in range(n_x)]
    )
    one, two = ordered[:, : share_f + 16], ordered[:, share_f + 16 :]
    grad_up = jnp.concatenate([one[:, :share_f], two[:, :share_f]], axis=2).reshape(-1, width).T
    one, two, tail = one[:, share_f : share_f + 8], two[:, share_f:], one[:, share_f + 8 :]
    third = jnp.concatenate([one[:, :, width_e:], two[:, :, width_e:]], axis=2)
    outer = jnp.concatenate([one[:, :, :width_e], two[:, :, :width_e], third], axis=1)
    outer = outer.reshape(-1, width_e)
    high = outer.astype(jnp.bfloat16)
    low = (outer - high.astype(jnp.float32)).astype(jnp.bfloat16)
    grad_down = contract_last(high, w_proj) + contract_last(low, w_proj)
    grad_proj = tail[:, :share_d, :width_e].reshape(-1, width_e)
    gains = jnp.sum(tail[:, : width // 128, width_e:], axis=0).reshape(width)
    mine_at = (lax.axis_index("z") * n_y + lax.axis_index("y")) * n_c + core
    grad_gain = lax.dynamic_slice_in_dim(gains, mine_at * (width // groups), width // groups, 0)
    return (
        d_titles.reshape(units, length, width),
        grad_up,
        grad_down,
        grad_proj,
        grad_gain,
        new_table,
        new_accum,
    )


def solution(mesh):
    n_table, n_rep = mesh.devices.shape
    side = n_rep
    fine = Mesh(mesh.devices.reshape(n_table // (2 * side), side, 2, n_rep), DEVICES)
    split, tab = P(DEVICES), P(GROUP)
    return jax.shard_map(
        per_device,
        mesh=fine,
        in_specs=(split, P(), P(), P(), P(), split, split, split, split, split, split),
        out_specs=(split, P(None, GROUP), tab, tab, tab, split, split),
        check_vma=False,
    )
```

```python
import functools
import math

import jax
import jax.numpy as jnp
from jax import lax
from jax.experimental import pallas as pl
from jax.experimental.pallas import tpu as pltpu
from jax.sharding import Mesh
from jax.sharding import PartitionSpec as P

GELU_C = 0.7978845608028654
GELU_K = 0.044715
NORM_EPS = 1e-05
LEARN_RATE = 0.1
CHIPS = ("z", "y", "x")
GROUP = ("z", "y", "c")
DEVICES = ("z", "y", "c", "x")
VMEM = 30 << 20


def contract_first(left, right):
    return lax.dot_general(
        left, right, (((0,), (0,)), ((), ())), preferred_element_type=jnp.float32
    )


def contract_last(left, right):
    return lax.dot_general(
        left, right, (((1,), (1,)), ((), ())), preferred_element_type=jnp.float32
    )


def cost(flops, moved, transcendentals=0):
    return pl.CostEstimate(flops=flops, bytes_accessed=moved, transcendentals=transcendentals)


def swap_cores(block):
    return lax.ppermute(block, "c", [(0, 1), (1, 0)])


def along(block, name, step):
    size = lax.axis_size(name)
    return lax.ppermute(block, name, [(i, i ^ step) for i in range(size)])


def partners(name, second):
    sizes = [lax.axis_size(n) for n in DEVICES]
    at = DEVICES.index(name)
    pairs = []
    for index in range(math.prod(sizes)):
        place, rest = [], index
        for size in reversed(sizes):
            place.insert(0, rest % size)
            rest //= size
        place[at] ^= 1 if (place[DEVICES.index("c")] == 1) == second else 3
        to = 0
        for size, p in zip(sizes, place):
            to = to * size + p
        pairs.append((index, to))
    return pairs


def slot_of(core, here, size):
    block = lax.iota(jnp.int32, size) ^ here
    one = jnp.where(block == 0, 0, jnp.where(block == 1, 2, jnp.where(block == 2, 3, 1)))
    two = jnp.where(block < 2, block, 5 - block)
    return jnp.where(core == 0, one, two)


def halve(parts, names, second, also=()):
    kept, sent = [], []
    for terms, name in zip(parts, names):
        dim = ("z", "y", "x").index(name)
        size = terms[0].shape[dim]
        kept.append(tuple(lax.slice_in_dim(term, 0, size // 2, axis=dim) for term in terms))
        later = [lax.slice_in_dim(term, size // 2, size, axis=dim) for term in terms]
        sent.append(lax.ppermute(sum(later[1:], later[0]), DEVICES, partners(name, second)))
    if also:
        sent, also = lax.optimization_barrier((sent, also))
    return [terms + (got,) for terms, got in zip(kept, sent)], also


def layer_norm(rows):
    center = jnp.mean(rows, axis=1, keepdims=True)
    offset = rows - center
    inv_scale = lax.rsqrt(jnp.mean(offset * offset, axis=1, keepdims=True) + NORM_EPS)
    return offset * inv_scale, inv_scale


def item_kernel(key_ref, grad_ref, *refs):
    out_ref = refs[-1]
    rows = out_ref.shape[0]
    place = lax.broadcasted_iota(jnp.int32, (rows, key_ref.shape[1]), 0) + pl.program_id(0) * rows
    onehot = jnp.where(place == key_ref[...], 1.0, 0.0).astype(jnp.bfloat16)
    total = jnp.dot(onehot, grad_ref[...], preferred_element_type=jnp.float32)
    for ref in refs[:-1]:
        total = total + ref[...]
    out_ref[...] = total


def segment_sums(key, sample_grad, count, *more):
    samples, width_e = sample_grad.shape
    step = 512
    return pl.pallas_call(
        item_kernel,
        grid=(count // step,),
        in_specs=[
            pl.BlockSpec((1, samples), lambda i: (0, 0)),
            pl.BlockSpec((samples, width_e), lambda i: (0, 0)),
        ]
        + [pl.BlockSpec((step, width_e), lambda i: (i, 0))] * len(more),
        out_specs=pl.BlockSpec((step, width_e), lambda i: (i, 0)),
        out_shape=jax.ShapeDtypeStruct((count, width_e), jnp.float32),
        compiler_params=pltpu.CompilerParams(vmem_limit_bytes=24 << 20),
        cost_estimate=cost(2 * samples * width_e * count, 4 * width_e * count),
        name="segment_sums",
    )(key.reshape(1, samples), sample_grad, *more)


def forward_kernel(units, titles_ref, gain_ref, w_ref, normed_ref, slope_ref, act_ref, mean_ref):
    rows, width = titles_ref.shape
    length = rows // units
    step = 8 * length

    @pl.when(pl.program_id(0) == 0)
    def _():
        for r in range(units // 8):
            block = titles_ref[r * step : (r + 1) * step, :].astype(jnp.float32)
            normed, _ = layer_norm(block)
            normed_ref[r * step : (r + 1) * step, :] = (normed * gain_ref[...]).astype(jnp.bfloat16)
            mean_ref[r * 8 : (r + 1) * 8, :] = jnp.mean(block.reshape(8, length, width), axis=1)

    for r in range(units // 8):
        pre = jnp.dot(
            normed_ref[r * step : (r + 1) * step, :],
            w_ref[...],
            preferred_element_type=jnp.float32,
        )
        square = pre * pre
        tangent = jnp.tanh(pre * (GELU_C + (GELU_C * GELU_K) * square))
        half = 0.5 + 0.5 * tangent
        value = pre * half
        slope = half + value * (1.0 - tangent) * (GELU_C + (3.0 * GELU_C * GELU_K) * square)
        slope_ref[r * step : (r + 1) * step, :] = slope.astype(jnp.bfloat16)
        act_ref[r * 8 : (r + 1) * 8, :] = jnp.mean(value.reshape(8, length, -1), axis=1)


def forward(titles, ln_gain, w_up):
    units, length, width = titles.shape
    rows, hidden = units * length, w_up.shape[1]
    block = 512
    return pl.pallas_call(
        functools.partial(forward_kernel, units),
        grid=(hidden // block,),
        in_specs=[
            pl.BlockSpec((rows, width), lambda i: (0, 0)),
            pl.BlockSpec((1, width), lambda i: (0, 0)),
            pl.BlockSpec((width, block), lambda i: (0, i)),
        ],
        out_specs=[
            pl.BlockSpec((rows, width), lambda i: (0, 0)),
            pl.BlockSpec((rows, block), lambda i: (0, i)),
            pl.BlockSpec((units, block), lambda i: (0, i)),
            pl.BlockSpec((units, width), lambda i: (0, 0)),
        ],
        out_shape=[
            jax.ShapeDtypeStruct((rows, width), jnp.bfloat16),
            pltpu.HBM((rows, hidden), jnp.bfloat16),
            jax.ShapeDtypeStruct((units, hidden), jnp.float32),
            jax.ShapeDtypeStruct((units, width), jnp.float32),
        ],
        compiler_params=pltpu.CompilerParams(vmem_limit_bytes=VMEM),
        cost_estimate=cost(8 * rows * width * hidden, 4 * rows * hidden, rows * hidden),
        name="forward",
    )(
        pltpu.with_memory_space_constraint(titles.reshape(rows, width), pltpu.HBM),
        ln_gain.reshape(1, width),
        pltpu.with_memory_space_constraint(w_up, pltpu.HBM),
    )


def place_sums(core_ref, keep_at, send_at, ups, down, proj, out_refs):
    slots = proj.shape[0] // 8
    part = down.shape[0] // slots
    n_x = slots // 8
    first = core_ref[0] == 0
    for q in range(slots // 2):
        y, x = q // n_x, q % n_x
        spots = [at[1, y] * n_x + at[2, x] for at in (keep_at, send_at)]
        pair = (y * 2 * n_x + x, (y * 2 + 1) * n_x + x)

        def store(refs, top, rows):
            even, odd = (rows(k) for k in pair)
            end = top + even.shape[0]
            refs[0][spots[0], top:end, :] = jnp.where(first, even, odd)
            refs[1][spots[1], top:end, :] = jnp.where(first, odd, even)

        for index, up, refs in zip(*ups, zip(out_refs[::2], out_refs[1::2])):
            store(refs, 0, lambda k: up[k * part : (k + 1) * part])
            low = index * 8
            store(refs, part, lambda k: down[k * part + low : k * part + low + 8])
            if index == 0:
                store(refs, part + 8, lambda k: proj[k * 8 : (k + 1) * 8])


def first_kernel(
    units, core_ref, keep_at, send_at, slope_ref, act_ref, mean_ref, pool_ref, grad_ref,
    normed_ref, pre_ref, *out_refs
):
    rows, block = slope_ref.shape
    length, step = rows // units, rows // units * 8
    for r in range(units // 8):
        slope = slope_ref[r * step : (r + 1) * step, :].astype(jnp.float32)
        d_pre = slope.reshape(8, length, block) * act_ref[r * 8 : (r + 1) * 8, :][:, None, :]
        pre_ref[r * step : (r + 1) * step, :] = d_pre.reshape(step, block).astype(jnp.bfloat16)
    up = contract_first(pre_ref[...], normed_ref[...])
    down = contract_first(mean_ref[...], grad_ref[...])
    proj = contract_first(pool_ref[...], grad_ref[...])
    place_sums(core_ref, keep_at, send_at, ((0,), (up,)), down, proj, out_refs)


def other_kernel(
    indices, core_ref, keep_at, send_at, pre_ref, mean_ref, pool_ref, grad_ref, *refs
):
    count = len(indices)
    normed = jnp.concatenate([ref[...] for ref in refs[:count]], axis=1)
    up = contract_first(pre_ref[...], normed)
    down = contract_first(mean_ref[...], grad_ref[...])
    wide = grad_ref.shape[1]
    ups = [up[:, p * wide : (p + 1) * wide] for p in range(count)]
    empty = jnp.zeros((pool_ref.shape[1], 1), jnp.float32)
    place_sums(core_ref, keep_at, send_at, (indices, ups), down, empty, refs[count:])


def up_products(tables, indices, left, normed_b, mean_act_b, pooled_b, grad_b):
    rows, hidden = left[0].shape
    units, width_e = grad_b.shape
    sides = tables[1].shape[1]
    slots = 2 * sides * sides
    part = hidden // sides // slots
    tall = [part + 8 + 8 * (index == 0) for index in indices for _ in range(2)]
    first = len(left) == 2

    def columns(array):
        return pl.BlockSpec((array.shape[0], array.shape[1] // sides), lambda i, c, k, s: (0, i))

    def lanes(index):
        return pl.BlockSpec((rows, width_e), lambda i, c, k, s: (0, index))

    def sums(height, table):
        return pl.BlockSpec(
            (slots // 2, height, width_e), lambda i, *tables: (tables[table][0, i], 0, 0)
        )

    out_specs = [sums(h, 1 + n % 2) for n, h in enumerate(tall)]
    out_shape = [jax.ShapeDtypeStruct((sides * slots // 2, h, width_e), jnp.float32) for h in tall]
    if first:
        kernel = functools.partial(first_kernel, units)
        out_specs.insert(0, columns(left[0]))
        out_shape.insert(0, pltpu.VMEM((rows, hidden), jnp.bfloat16))
    else:
        kernel = functools.partial(other_kernel, indices)
    return pl.pallas_call(
        kernel,
        grid_spec=pltpu.PrefetchScalarGridSpec(
            num_scalar_prefetch=3,
            grid=(sides,),
            in_specs=[columns(array) for array in left]
            + [columns(mean_act_b), columns(pooled_b)]
            + [pl.BlockSpec(grad_b.shape, lambda i, c, k, s: (0, 0))]
            + [lanes(index) for index in indices],
            out_specs=out_specs,
        ),
        out_shape=out_shape,
        compiler_params=pltpu.CompilerParams(vmem_limit_bytes=VMEM),
        cost_estimate=cost(2 * rows * width_e * len(indices) * hidden, 4 * rows * hidden),
        name="first_products" if first else "other_products",
    )(*tables, *left, mean_act_b, pooled_b, grad_b, *[normed_b] * len(indices))


def titles_kernel(pre_ref, w_ref, titles_ref, gain_ref, pool_ref, out_ref, gain_out):
    rows, width = titles_ref.shape
    units = pool_ref.shape[0]
    length = rows // units
    d_normed = contract_last(pre_ref[...], w_ref[...])
    normed, inv_scale = layer_norm(titles_ref[...].astype(jnp.float32))
    product = d_normed * normed

    @pl.when(pl.program_id(0) == 0)
    def _():
        gain_out[...] = jnp.zeros_like(gain_out)

    gain_out[...] += jnp.sum(product.reshape(rows // 8, 8, width), axis=0)
    d_hat = d_normed * gain_ref[...]
    d_flat = inv_scale * (
        d_hat
        - jnp.mean(d_hat, axis=1, keepdims=True)
        - normed * jnp.mean(d_hat * normed, axis=1, keepdims=True)
    )
    d_block = d_flat.reshape(units, length, width) + (pool_ref[...] * (1.0 / length))[:, None, :]
    out_ref[...] = d_block.reshape(rows, width).astype(jnp.bfloat16)


def title_grads(d_pre, w_up, titles, ln_gain, d_pooled):
    units, length, width = titles.shape
    rows, hidden = d_pre.shape
    step = 8 * length
    return pl.pallas_call(
        titles_kernel,
        grid=(rows // step,),
        in_specs=[
            pl.BlockSpec((step, hidden), lambda i: (i, 0)),
            pl.BlockSpec((width, hidden), lambda i: (0, 0)),
            pl.BlockSpec((step, width), lambda i: (i, 0)),
            pl.BlockSpec((1, width), lambda i: (0, 0)),
            pl.BlockSpec((8, width), lambda i: (i, 0)),
        ],
        out_specs=[
            pl.BlockSpec((step, width), lambda i: (i, 0)),
            pl.BlockSpec((8, width), lambda i: (0, 0)),
        ],
        out_shape=[
            jax.ShapeDtypeStruct((rows, width), jnp.bfloat16),
            jax.ShapeDtypeStruct((8, width), jnp.float32),
        ],
        compiler_params=pltpu.CompilerParams(vmem_limit_bytes=VMEM),
        cost_estimate=cost(2 * rows * width * hidden, 2 * rows * hidden),
        name="title_grads",
    )(d_pre, w_up, titles.reshape(rows, width), ln_gain.reshape(1, width), d_pooled)


def rows_kernel(arrived_ref, table_ref, accum_ref, table_out, accum_out):
    step, width_e = table_ref.shape
    slots = arrived_ref.shape[0]
    grads = arrived_ref[:, :width_e]
    ids = arrived_ref[:, width_e : width_e + 1].astype(jnp.int32)
    here = lax.broadcasted_iota(jnp.int32, (slots, step), 1) + pl.program_id(0) * step
    onehot = jnp.where(here == ids, 1.0, 0.0).astype(jnp.bfloat16)
    high = grads.astype(jnp.bfloat16)
    low = (grads - high.astype(jnp.float32)).astype(jnp.bfloat16)
    row_grad = contract_first(onehot, high) + contract_first(onehot, low)
    new_accum = accum_ref[...] + row_grad * row_grad
    accum_out[...] = new_accum
    table_out[...] = table_ref[...] - LEARN_RATE * row_grad * lax.rsqrt(new_accum)


def row_update(arrived, table, accum):
    rows, width_e = table.shape
    step = 512
    tile = pl.BlockSpec((step, width_e), lambda i: (i, 0))
    return pl.pallas_call(
        rows_kernel,
        grid=(rows // step,),
        in_specs=[pl.BlockSpec(arrived.shape, lambda i: (0, 0)), tile, tile],
        out_specs=[tile, tile],
        out_shape=[jax.ShapeDtypeStruct((rows, width_e), jnp.float32)] * 2,
        compiler_params=pltpu.CompilerParams(vmem_limit_bytes=16 << 20),
        cost_estimate=cost(4 * rows * width_e * arrived.shape[0], 16 * rows * width_e),
        name="row_update",
    )(arrived, table, accum)


def per_device(
    titles,
    ln_gain,
    w_up,
    w_down,
    w_proj,
    sample_grad,
    sample_item,
    sample_row,
    row_ids,
    table,
    accum,
):
    n_z, n_y, n_c, n_x = (lax.axis_size(name) for name in DEVICES)
    chips, groups = n_z * n_y * n_x, n_z * n_y * n_c
    devices = chips * n_c
    core, my_x = lax.axis_index("c"), lax.axis_index("x")
    units, length, width = titles.shape
    hidden = w_up.shape[1]
    width_e = sample_grad.shape[1]
    share_f, share_d = hidden // devices, width // devices

    owner = sample_item // units
    spot = (owner // (n_c * n_x) * n_x + owner % n_x) * units + sample_item % units
    of_core = owner // n_x % n_c
    sent = segment_sums(jnp.where(of_core == core, -1, spot), sample_grad, chips * units)
    got = swap_cores(sent)
    mine = segment_sums(jnp.where(of_core == core, spot, -1), sample_grad, chips * units, got)
    mine = mine.reshape(chips, units, width_e)
    mine, ln_gain = lax.optimization_barrier((mine, ln_gain))
    item_all = lax.all_to_all(mine, CHIPS, 0, 0, tiled=True)

    slot_count = row_ids.shape[1]
    rows_here = table.shape[0]
    slot_hot = (sample_row[:, None] == lax.iota(jnp.int32, slot_count)[None, :]).astype(
        jnp.bfloat16
    )
    local_rows = (row_ids[0] % rows_here).astype(jnp.float32)
    row_part = jnp.concatenate(
        [
            contract_first(slot_hot, sample_grad),
            jnp.broadcast_to(local_rows[:, None], (slot_count, 128)),
        ],
        axis=1,
    )
    row_part = row_part.reshape(devices, slot_count // devices, width_e + 128)

    normed_b, slope, mean_act, mean_title = forward(titles, ln_gain, w_up)
    mean_act_b = mean_act.astype(jnp.bfloat16)
    pooled = mean_title + jnp.dot(mean_act_b, w_down, preferred_element_type=jnp.float32)
    lane = lax.iota(jnp.int32, devices * 8)
    source = jnp.where(lane % 8 < share_d, lane // 8 * share_d + lane % 8, -1)
    spread = (lax.iota(jnp.int32, width)[:, None] == source[None, :]).astype(jnp.bfloat16)
    pooled_b = jnp.dot(
        pooled.astype(jnp.bfloat16), spread, preferred_element_type=jnp.float32
    ).astype(jnp.bfloat16)
    item_all, pooled_b, row_part = lax.optimization_barrier((item_all, pooled_b, row_part))

    item_grad = jnp.sum(item_all, axis=0)
    grad_b = item_grad.astype(jnp.bfloat16)
    d_pooled = contract_last(grad_b, w_proj)
    d_act = contract_last(d_pooled.astype(jnp.bfloat16), w_down) / length

    here = [(lax.axis_index(name), lax.axis_size(name)) for name in CHIPS]
    keep_at = jnp.stack([slot_of(core, at, size) for at, size in here])
    send_at = jnp.stack([slot_of(1 - core, at, size) for at, size in here])
    tables = (core.reshape(1), keep_at, send_at)
    items = (normed_b, mean_act_b, pooled_b, grad_b)
    slope = pltpu.with_memory_space_constraint(slope, pltpu.HBM)
    d_pre, *sums = up_products(tables, (0,), (slope, d_act), *items)
    d_pre = pltpu.with_memory_space_constraint(d_pre, pltpu.VMEM)
    for index in (1, 2):
        sums += up_products(tables, (index,), (d_pre,), *items)
    shape = (n_z, n_y, n_x, -1, width_e)
    parts = [
        (keep.reshape(shape), swap_cores(send).reshape(shape))
        for keep, send in zip(sums[::2], sums[1::2])
    ]

    beside = title_grads(d_pre, w_up, titles, ln_gain, d_pooled)
    parts, (d_titles, gain_term) = halve(parts, "xyz", False, tuple(beside))
    (got, row_part) = lax.optimization_barrier((parts[0][-1], row_part))
    parts[0] = parts[0][:-1] + (got,)
    row_all = lax.all_to_all(row_part, DEVICES, 0, 0, tiled=True)
    gain_term = (gain_term + swap_cores(gain_term)).reshape(8, 3, width_e)
    gain_term = jnp.pad(jnp.sum(gain_term, axis=0), ((0, 5), (0, 0)))
    parts, (gain_term,) = halve(parts, "xyz", True, (gain_term,))
    total = sum(parts[0][1:], parts[0][0])
    gain_term = jnp.broadcast_to(gain_term, total.shape[:3] + gain_term.shape)
    parts[0] = (jnp.concatenate([total, gain_term], axis=3),)
    parts, _ = halve(parts, "yzx", False)
    parts, (row_all,) = halve(parts, "yzx", True, (row_all,))
    beside = row_update(row_all.reshape(slot_count, width_e + 128), table, accum)
    parts, (new_table, new_accum) = halve(parts, "zxy", False, tuple(beside))
    parts, _ = halve(parts, "zxy", True)

    flat = [sum(terms[1:], terms[0]).reshape(-1, width_e) for terms in parts]
    last = jnp.concatenate(flat, axis=0)
    blocks = jnp.stack([last, along(last, "x", 1), along(last, "x", 2), along(last, "x", 3)])
    ordered = jnp.stack(
        [lax.dynamic_index_in_dim(blocks, my_x ^ j, 0, keepdims=False) for j in range(n_x)]
    )
    starts = [0, share_f + 24, 2 * share_f + 32]
    grad_up = jnp.concatenate([ordered[:, at : at + share_f] for at in starts], axis=2)
    grad_up = grad_up.reshape(-1, width).T
    outer = jnp.concatenate(
        [ordered[:, at + share_f : at + share_f + 8] for at in starts], axis=1
    ).reshape(-1, width_e)
    high = outer.astype(jnp.bfloat16)
    low = (outer - high.astype(jnp.float32)).astype(jnp.bfloat16)
    grad_down = contract_last(high, w_proj) + contract_last(low, w_proj)
    grad_proj = ordered[:, share_f + 8 : share_f + 8 + share_d].reshape(-1, width_e)
    gains = jnp.sum(ordered[:, share_f + 16 : share_f + 19], axis=0).reshape(width)
    mine_at = (lax.axis_index("z") * n_y + lax.axis_index("y")) * n_c + core
    grad_gain = lax.dynamic_slice_in_dim(gains, mine_at * (width // groups), width // groups, 0)
    return (
        d_titles.reshape(units, length, width),
        grad_up,
        grad_down,
        grad_proj,
        grad_gain,
        new_table,
        new_accum,
    )


def solution(mesh):
    n_table, n_rep = mesh.devices.shape
    side = n_rep
    fine = Mesh(mesh.devices.reshape(n_table // (2 * side), side, 2, n_rep), DEVICES)
    split, tab = P(DEVICES), P(GROUP)
    return jax.shard_map(
        per_device,
        mesh=fine,
        in_specs=(split, P(), P(), P(), P(), split, split, split, split, split, split),
        out_specs=(split, P(None, GROUP), tab, tab, tab, split, split),
        check_vma=False,
    )
```

```python
import functools
import math

import jax
import jax.numpy as jnp
from jax import lax
from jax.experimental import pallas as pl
from jax.experimental.pallas import tpu as pltpu
from jax.sharding import Mesh
from jax.sharding import PartitionSpec as P

GELU_C = 0.7978845608028654
GELU_K = 0.044715
NORM_EPS = 1e-05
LEARN_RATE = 0.1
CHIPS = ("z", "y", "x")
GROUP = ("z", "y", "c")
DEVICES = ("z", "y", "c", "x")
VMEM = 30 << 20


def contract_first(left, right):
    return lax.dot_general(
        left, right, (((0,), (0,)), ((), ())), preferred_element_type=jnp.float32
    )


def contract_last(left, right):
    return lax.dot_general(
        left, right, (((1,), (1,)), ((), ())), preferred_element_type=jnp.float32
    )


def cost(flops, moved, transcendentals=0):
    return pl.CostEstimate(flops=flops, bytes_accessed=moved, transcendentals=transcendentals)


def swap_cores(block):
    return lax.ppermute(block, "c", [(0, 1), (1, 0)])


def along(block, name, step):
    size = lax.axis_size(name)
    return lax.ppermute(block, name, [(i, i ^ step) for i in range(size)])


def partners(name, second):
    sizes = [lax.axis_size(n) for n in DEVICES]
    at = DEVICES.index(name)
    pairs = []
    for index in range(math.prod(sizes)):
        place, rest = [], index
        for size in reversed(sizes):
            place.insert(0, rest % size)
            rest //= size
        place[at] ^= 1 if (place[DEVICES.index("c")] == 1) == second else 3
        to = 0
        for size, p in zip(sizes, place):
            to = to * size + p
        pairs.append((index, to))
    return pairs


def slot_of(core, here, size):
    block = lax.iota(jnp.int32, size) ^ here
    one = jnp.where(block == 0, 0, jnp.where(block == 1, 2, jnp.where(block == 2, 3, 1)))
    two = jnp.where(block < 2, block, 5 - block)
    return jnp.where(core == 0, one, two)


def halve(parts, names, second, also=()):
    kept, sent = [], []
    for part, name in zip(parts, names):
        dim = ("z", "y", "x").index(name)
        middle = part.shape[dim] // 2
        kept.append(lax.slice_in_dim(part, 0, middle, axis=dim))
        sent.append(
            lax.ppermute(
                lax.slice_in_dim(part, middle, None, axis=dim), DEVICES, partners(name, second)
            )
        )
    if also:
        sent, also = lax.optimization_barrier((sent, also))
    return [k + s for k, s in zip(kept, sent)], also


def layer_norm(rows):
    center = jnp.mean(rows, axis=1, keepdims=True)
    offset = rows - center
    inv_scale = lax.rsqrt(jnp.mean(offset * offset, axis=1, keepdims=True) + NORM_EPS)
    return offset * inv_scale, inv_scale


def item_kernel(key_ref, grad_ref, *refs):
    out_ref = refs[-1]
    rows = out_ref.shape[0]
    place = lax.broadcasted_iota(jnp.int32, (rows, key_ref.shape[1]), 0) + pl.program_id(0) * rows
    onehot = jnp.where(place == key_ref[...], 1.0, 0.0).astype(jnp.bfloat16)
    total = jnp.dot(onehot, grad_ref[...], preferred_element_type=jnp.float32)
    for ref in refs[:-1]:
        total = total + ref[...]
    out_ref[...] = total


def segment_sums(key, sample_grad, count, *more):
    samples, width_e = sample_grad.shape
    step = 512
    return pl.pallas_call(
        item_kernel,
        grid=(count // step,),
        in_specs=[
            pl.BlockSpec((1, samples), lambda i: (0, 0)),
            pl.BlockSpec((samples, width_e), lambda i: (0, 0)),
        ]
        + [pl.BlockSpec((step, width_e), lambda i: (i, 0))] * len(more),
        out_specs=pl.BlockSpec((step, width_e), lambda i: (i, 0)),
        out_shape=jax.ShapeDtypeStruct((count, width_e), jnp.float32),
        compiler_params=pltpu.CompilerParams(vmem_limit_bytes=24 << 20),
        cost_estimate=cost(2 * samples * width_e * count, 4 * width_e * count),
        name="segment_sums",
    )(key.reshape(1, samples), sample_grad, *more)


def forward_kernel(units, titles_ref, gain_ref, w_ref, normed_ref, slope_ref, act_ref, mean_ref):
    rows, width = titles_ref.shape
    length = rows // units
    step = 8 * length

    @pl.when(pl.program_id(0) == 0)
    def _():
        for r in range(units // 8):
            block = titles_ref[r * step : (r + 1) * step, :].astype(jnp.float32)
            normed, _ = layer_norm(block)
            normed_ref[r * step : (r + 1) * step, :] = (normed * gain_ref[...]).astype(jnp.bfloat16)
            mean_ref[r * 8 : (r + 1) * 8, :] = jnp.mean(block.reshape(8, length, width), axis=1)

    for r in range(units // 8):
        pre = jnp.dot(
            normed_ref[r * step : (r + 1) * step, :],
            w_ref[...],
            preferred_element_type=jnp.float32,
        )
        square = pre * pre
        tangent = jnp.tanh(pre * (GELU_C + (GELU_C * GELU_K) * square))
        half = 0.5 + 0.5 * tangent
        value = pre * half
        slope = half + value * (1.0 - tangent) * (GELU_C + (3.0 * GELU_C * GELU_K) * square)
        slope_ref[r * step : (r + 1) * step, :] = slope.astype(jnp.bfloat16)
        act_ref[r * 8 : (r + 1) * 8, :] = jnp.mean(value.reshape(8, length, -1), axis=1)


def forward(titles, ln_gain, w_up):
    units, length, width = titles.shape
    rows, hidden = units * length, w_up.shape[1]
    block = 512
    return pl.pallas_call(
        functools.partial(forward_kernel, units),
        grid=(hidden // block,),
        in_specs=[
            pl.BlockSpec((rows, width), lambda i: (0, 0)),
            pl.BlockSpec((1, width), lambda i: (0, 0)),
            pl.BlockSpec((width, block), lambda i: (0, i)),
        ],
        out_specs=[
            pl.BlockSpec((rows, width), lambda i: (0, 0)),
            pl.BlockSpec((rows, block), lambda i: (0, i)),
            pl.BlockSpec((units, block), lambda i: (0, i)),
            pl.BlockSpec((units, width), lambda i: (0, 0)),
        ],
        out_shape=[
            jax.ShapeDtypeStruct((rows, width), jnp.bfloat16),
            pltpu.HBM((rows, hidden), jnp.bfloat16),
            jax.ShapeDtypeStruct((units, hidden), jnp.float32),
            jax.ShapeDtypeStruct((units, width), jnp.float32),
        ],
        compiler_params=pltpu.CompilerParams(vmem_limit_bytes=VMEM),
        cost_estimate=cost(8 * rows * width * hidden, 4 * rows * hidden, rows * hidden),
        name="forward",
    )(
        pltpu.with_memory_space_constraint(titles.reshape(rows, width), pltpu.HBM),
        ln_gain.reshape(1, width),
        pltpu.with_memory_space_constraint(w_up, pltpu.HBM),
    )


def place_sums(core_ref, keep_at, send_at, ups, down, proj, out_refs):
    slots = proj.shape[0] // 8
    part = down.shape[0] // slots
    n_x = slots // 8
    first = core_ref[0] == 0
    for q in range(slots // 2):
        y, x = q // n_x, q % n_x
        spots = [at[1, y] * n_x + at[2, x] for at in (keep_at, send_at)]
        pair = (y * 2 * n_x + x, (y * 2 + 1) * n_x + x)

        def store(refs, top, rows):
            even, odd = (rows(k) for k in pair)
            end = top + even.shape[0]
            refs[0][spots[0], top:end, :] = jnp.where(first, even, odd)
            refs[1][spots[1], top:end, :] = jnp.where(first, odd, even)

        for index, up, refs in zip(*ups, zip(out_refs[::2], out_refs[1::2])):
            store(refs, 0, lambda k: up[k * part : (k + 1) * part])
            low = index * 8
            store(refs, part, lambda k: down[k * part + low : k * part + low + 8])
            if index == 0:
                store(refs, part + 8, lambda k: proj[k * 8 : (k + 1) * 8])


def first_kernel(
    units, core_ref, keep_at, send_at, slope_ref, act_ref, mean_ref, pool_ref, grad_ref,
    normed_ref, pre_ref, *out_refs
):
    rows, block = slope_ref.shape
    length, step = rows // units, rows // units * 8
    for r in range(units // 8):
        slope = slope_ref[r * step : (r + 1) * step, :].astype(jnp.float32)
        d_pre = slope.reshape(8, length, block) * act_ref[r * 8 : (r + 1) * 8, :][:, None, :]
        pre_ref[r * step : (r + 1) * step, :] = d_pre.reshape(step, block).astype(jnp.bfloat16)
    up = contract_first(pre_ref[...], normed_ref[...])
    down = contract_first(mean_ref[...], grad_ref[...])
    proj = contract_first(pool_ref[...], grad_ref[...])
    place_sums(core_ref, keep_at, send_at, ((0,), (up,)), down, proj, out_refs)


def other_kernel(
    indices, core_ref, keep_at, send_at, pre_ref, mean_ref, pool_ref, grad_ref, *refs
):
    count = len(indices)
    normed = jnp.concatenate([ref[...] for ref in refs[:count]], axis=1)
    up = contract_first(pre_ref[...], normed)
    down = contract_first(mean_ref[...], grad_ref[...])
    wide = grad_ref.shape[1]
    ups = [up[:, p * wide : (p + 1) * wide] for p in range(count)]
    empty = jnp.zeros((pool_ref.shape[1], 1), jnp.float32)
    place_sums(core_ref, keep_at, send_at, (indices, ups), down, empty, refs[count:])


def up_products(tables, indices, left, normed_b, mean_act_b, pooled_b, grad_b):
    rows, hidden = left[0].shape
    units, width_e = grad_b.shape
    sides = tables[1].shape[1]
    slots = 2 * sides * sides
    part = hidden // sides // slots
    tall = [part + 8 + 8 * (index == 0) for index in indices for _ in range(2)]
    first = len(left) == 2

    def columns(array):
        return pl.BlockSpec((array.shape[0], array.shape[1] // sides), lambda i, c, k, s: (0, i))

    def lanes(index):
        return pl.BlockSpec((rows, width_e), lambda i, c, k, s: (0, index))

    def sums(height, table):
        return pl.BlockSpec(
            (slots // 2, height, width_e), lambda i, *tables: (tables[table][0, i], 0, 0)
        )

    out_specs = [sums(h, 1 + n % 2) for n, h in enumerate(tall)]
    out_shape = [jax.ShapeDtypeStruct((sides * slots // 2, h, width_e), jnp.float32) for h in tall]
    if first:
        kernel = functools.partial(first_kernel, units)
        out_specs.insert(0, columns(left[0]))
        out_shape.insert(0, pltpu.VMEM((rows, hidden), jnp.bfloat16))
    else:
        kernel = functools.partial(other_kernel, indices)
    return pl.pallas_call(
        kernel,
        grid_spec=pltpu.PrefetchScalarGridSpec(
            num_scalar_prefetch=3,
            grid=(sides,),
            in_specs=[columns(array) for array in left]
            + [columns(mean_act_b), columns(pooled_b)]
            + [pl.BlockSpec(grad_b.shape, lambda i, c, k, s: (0, 0))]
            + [lanes(index) for index in indices],
            out_specs=out_specs,
        ),
        out_shape=out_shape,
        compiler_params=pltpu.CompilerParams(vmem_limit_bytes=VMEM),
        cost_estimate=cost(2 * rows * width_e * len(indices) * hidden, 4 * rows * hidden),
        name="first_products" if first else "other_products",
    )(*tables, *left, mean_act_b, pooled_b, grad_b, *[normed_b] * len(indices))


def titles_kernel(pre_ref, w_ref, titles_ref, gain_ref, pool_ref, out_ref, gain_out):
    rows, width = titles_ref.shape
    units = pool_ref.shape[0]
    length = rows // units
    d_normed = contract_last(pre_ref[...], w_ref[...])
    normed, inv_scale = layer_norm(titles_ref[...].astype(jnp.float32))
    product = d_normed * normed

    @pl.when(pl.program_id(0) == 0)
    def _():
        gain_out[...] = jnp.zeros_like(gain_out)

    gain_out[...] += jnp.sum(product.reshape(rows // 8, 8, width), axis=0)
    d_hat = d_normed * gain_ref[...]
    d_flat = inv_scale * (
        d_hat
        - jnp.mean(d_hat, axis=1, keepdims=True)
        - normed * jnp.mean(d_hat * normed, axis=1, keepdims=True)
    )
    d_block = d_flat.reshape(units, length, width) + (pool_ref[...] * (1.0 / length))[:, None, :]
    out_ref[...] = d_block.reshape(rows, width).astype(jnp.bfloat16)


def title_grads(d_pre, w_up, titles, ln_gain, d_pooled):
    units, length, width = titles.shape
    rows, hidden = d_pre.shape
    step = 8 * length
    return pl.pallas_call(
        titles_kernel,
        grid=(rows // step,),
        in_specs=[
            pl.BlockSpec((step, hidden), lambda i: (i, 0)),
            pl.BlockSpec((width, hidden), lambda i: (0, 0)),
            pl.BlockSpec((step, width), lambda i: (i, 0)),
            pl.BlockSpec((1, width), lambda i: (0, 0)),
            pl.BlockSpec((8, width), lambda i: (i, 0)),
        ],
        out_specs=[
            pl.BlockSpec((step, width), lambda i: (i, 0)),
            pl.BlockSpec((8, width), lambda i: (0, 0)),
        ],
        out_shape=[
            jax.ShapeDtypeStruct((rows, width), jnp.bfloat16),
            jax.ShapeDtypeStruct((8, width), jnp.float32),
        ],
        compiler_params=pltpu.CompilerParams(vmem_limit_bytes=VMEM),
        cost_estimate=cost(2 * rows * width * hidden, 2 * rows * hidden),
        name="title_grads",
    )(d_pre, w_up, titles.reshape(rows, width), ln_gain.reshape(1, width), d_pooled)


def rows_kernel(arrived_ref, table_ref, accum_ref, table_out, accum_out):
    step, width_e = table_ref.shape
    slots = arrived_ref.shape[0]
    grads = arrived_ref[:, :width_e]
    ids = arrived_ref[:, width_e : width_e + 1].astype(jnp.int32)
    here = lax.broadcasted_iota(jnp.int32, (slots, step), 1) + pl.program_id(0) * step
    onehot = jnp.where(here == ids, 1.0, 0.0).astype(jnp.bfloat16)
    high = grads.astype(jnp.bfloat16)
    low = (grads - high.astype(jnp.float32)).astype(jnp.bfloat16)
    row_grad = contract_first(onehot, high) + contract_first(onehot, low)
    new_accum = accum_ref[...] + row_grad * row_grad
    accum_out[...] = new_accum
    table_out[...] = table_ref[...] - LEARN_RATE * row_grad * lax.rsqrt(new_accum)


def row_update(arrived, table, accum):
    rows, width_e = table.shape
    step = 512
    tile = pl.BlockSpec((step, width_e), lambda i: (i, 0))
    return pl.pallas_call(
        rows_kernel,
        grid=(rows // step,),
        in_specs=[pl.BlockSpec(arrived.shape, lambda i: (0, 0)), tile, tile],
        out_specs=[tile, tile],
        out_shape=[jax.ShapeDtypeStruct((rows, width_e), jnp.float32)] * 2,
        compiler_params=pltpu.CompilerParams(vmem_limit_bytes=16 << 20),
        cost_estimate=cost(4 * rows * width_e * arrived.shape[0], 16 * rows * width_e),
        name="row_update",
    )(
        arrived,
        pltpu.with_memory_space_constraint(table, pltpu.HBM),
        pltpu.with_memory_space_constraint(accum, pltpu.HBM),
    )


def per_device(
    titles,
    ln_gain,
    w_up,
    w_down,
    w_proj,
    sample_grad,
    sample_item,
    sample_row,
    row_ids,
    table,
    accum,
):
    n_z, n_y, n_c, n_x = (lax.axis_size(name) for name in DEVICES)
    chips, groups = n_z * n_y * n_x, n_z * n_y * n_c
    devices = chips * n_c
    core, my_x = lax.axis_index("c"), lax.axis_index("x")
    units, length, width = titles.shape
    hidden = w_up.shape[1]
    width_e = sample_grad.shape[1]
    share_f, share_d = hidden // devices, width // devices

    owner = sample_item // units
    spot = (owner // (n_c * n_x) * n_x + owner % n_x) * units + sample_item % units
    of_core = owner // n_x % n_c
    sent = segment_sums(jnp.where(of_core == core, -1, spot), sample_grad, chips * units)
    got = swap_cores(sent)
    mine = segment_sums(jnp.where(of_core == core, spot, -1), sample_grad, chips * units, got)
    mine = mine.reshape(chips, units, width_e)
    mine, ln_gain = lax.optimization_barrier((mine, ln_gain))
    item_all = lax.all_to_all(mine, CHIPS, 0, 0, tiled=True)

    slot_count = row_ids.shape[1]
    rows_here = table.shape[0]
    slot_hot = (sample_row[:, None] == lax.iota(jnp.int32, slot_count)[None, :]).astype(
        jnp.bfloat16
    )
    local_rows = (row_ids[0] % rows_here).astype(jnp.float32)
    row_part = jnp.concatenate(
        [
            contract_first(slot_hot, sample_grad),
            jnp.broadcast_to(local_rows[:, None], (slot_count, 128)),
        ],
        axis=1,
    )
    row_part = row_part.reshape(devices, slot_count // devices, width_e + 128)

    normed_b, slope, mean_act, mean_title = forward(titles, ln_gain, w_up)
    mean_act_b = mean_act.astype(jnp.bfloat16)
    pooled = mean_title + jnp.dot(mean_act_b, w_down, preferred_element_type=jnp.float32)
    lane = lax.iota(jnp.int32, devices * 8)
    source = jnp.where(lane % 8 < share_d, lane // 8 * share_d + lane % 8, -1)
    spread = (lax.iota(jnp.int32, width)[:, None] == source[None, :]).astype(jnp.bfloat16)
    pooled_b = jnp.dot(
        pooled.astype(jnp.bfloat16), spread, preferred_element_type=jnp.float32
    ).astype(jnp.bfloat16)
    item_all, pooled_b, row_part = lax.optimization_barrier((item_all, pooled_b, row_part))

    item_grad = jnp.sum(item_all, axis=0)
    grad_b = item_grad.astype(jnp.bfloat16)
    d_pooled = contract_last(grad_b, w_proj)
    d_act = contract_last(d_pooled.astype(jnp.bfloat16), w_down) / length

    here = [(lax.axis_index(name), lax.axis_size(name)) for name in CHIPS]
    keep_at = jnp.stack([slot_of(core, at, size) for at, size in here])
    send_at = jnp.stack([slot_of(1 - core, at, size) for at, size in here])
    tables = (core.reshape(1), keep_at, send_at)
    items = (normed_b, mean_act_b, pooled_b, grad_b)
    slope = pltpu.with_memory_space_constraint(slope, pltpu.HBM)
    d_pre, *sums = up_products(tables, (0,), (slope, d_act), *items)
    d_pre = pltpu.with_memory_space_constraint(d_pre, pltpu.VMEM)
    for index in (1, 2):
        sums += up_products(tables, (index,), (d_pre,), *items)
    parts = [
        (keep + swap_cores(send)).reshape(n_z, n_y, n_x, -1, width_e)
        for keep, send in zip(sums[::2], sums[1::2])
    ]

    beside = title_grads(d_pre, w_up, titles, ln_gain, d_pooled)
    parts, (d_titles, gain_term) = halve(parts, "xyz", False, tuple(beside))
    parts, row_part = lax.optimization_barrier((parts, row_part))
    row_all = lax.all_to_all(row_part, DEVICES, 0, 0, tiled=True)
    gain_term = (gain_term + swap_cores(gain_term)).reshape(8, 3, width_e)
    gain_term = jnp.pad(jnp.sum(gain_term, axis=0), ((0, 5), (0, 0)))
    parts, (gain_term,) = halve(parts, "xyz", True, (gain_term,))
    gain_term = jnp.broadcast_to(gain_term, parts[0].shape[:3] + gain_term.shape)
    parts[0] = jnp.concatenate([parts[0], gain_term], axis=3)
    parts, _ = halve(parts, "yzx", False)
    parts, (row_all,) = halve(parts, "yzx", True, (row_all,))
    new_table, new_accum = row_update(
        row_all.reshape(slot_count, width_e + 128), table, accum
    )
    parts, _ = halve(parts, "zxy", False)
    parts, _ = halve(parts, "zxy", True)

    flat = [part.reshape(-1, width_e) for part in parts]
    last = jnp.concatenate(flat, axis=0)
    blocks = jnp.stack([last, along(last, "x", 1), along(last, "x", 2), along(last, "x", 3)])
    ordered = jnp.stack(
        [lax.dynamic_index_in_dim(blocks, my_x ^ j, 0, keepdims=False) for j in range(n_x)]
    )
    starts = [0, share_f + 24, 2 * share_f + 32]
    grad_up = jnp.concatenate([ordered[:, at : at + share_f] for at in starts], axis=2)
    grad_up = grad_up.reshape(-1, width).T
    outer = jnp.concatenate(
        [ordered[:, at + share_f : at + share_f + 8] for at in starts], axis=1
    ).reshape(-1, width_e)
    high = outer.astype(jnp.bfloat16)
    low = (outer - high.astype(jnp.float32)).astype(jnp.bfloat16)
    grad_down = contract_last(high, w_proj) + contract_last(low, w_proj)
    grad_proj = ordered[:, share_f + 8 : share_f + 8 + share_d].reshape(-1, width_e)
    gains = jnp.sum(ordered[:, share_f + 16 : share_f + 19], axis=0).reshape(width)
    mine_at = (lax.axis_index("z") * n_y + lax.axis_index("y")) * n_c + core
    grad_gain = lax.dynamic_slice_in_dim(gains, mine_at * (width // groups), width // groups, 0)
    return (
        d_titles.reshape(units, length, width),
        grad_up,
        grad_down,
        grad_proj,
        grad_gain,
        new_table,
        new_accum,
    )


def solution(mesh):
    n_table, n_rep = mesh.devices.shape
    side = n_rep
    fine = Mesh(mesh.devices.reshape(n_table // (2 * side), side, 2, n_rep), DEVICES)
    split, tab = P(DEVICES), P(GROUP)
    return jax.shard_map(
        per_device,
        mesh=fine,
        in_specs=(split, P(), P(), P(), P(), split, split, split, split, split, split),
        out_specs=(split, P(None, GROUP), tab, tab, tab, split, split),
        check_vma=False,
    )
```

```python
import functools
import math

import jax
import jax.numpy as jnp
from jax import lax
from jax.experimental import pallas as pl
from jax.experimental.pallas import tpu as pltpu
from jax.sharding import Mesh
from jax.sharding import PartitionSpec as P

GELU_C = 0.7978845608028654
GELU_K = 0.044715
NORM_EPS = 1e-05
LEARN_RATE = 0.1
CHIPS = ("z", "y", "x")
GROUP = ("z", "y", "c")
DEVICES = ("z", "y", "c", "x")
VMEM = 30 << 20


def contract_first(left, right):
    return lax.dot_general(
        left, right, (((0,), (0,)), ((), ())), preferred_element_type=jnp.float32
    )


def contract_last(left, right):
    return lax.dot_general(
        left, right, (((1,), (1,)), ((), ())), preferred_element_type=jnp.float32
    )


def cost(flops, moved, transcendentals=0):
    return pl.CostEstimate(flops=flops, bytes_accessed=moved, transcendentals=transcendentals)


def swap_cores(block):
    return lax.ppermute(block, "c", [(0, 1), (1, 0)])


def along(block, name, step):
    size = lax.axis_size(name)
    return lax.ppermute(block, name, [(i, i ^ step) for i in range(size)])


def partners(name, second):
    sizes = [lax.axis_size(n) for n in DEVICES]
    at = DEVICES.index(name)
    pairs = []
    for index in range(math.prod(sizes)):
        place, rest = [], index
        for size in reversed(sizes):
            place.insert(0, rest % size)
            rest //= size
        place[at] ^= 1 if (place[DEVICES.index("c")] == 1) == second else 3
        to = 0
        for size, p in zip(sizes, place):
            to = to * size + p
        pairs.append((index, to))
    return pairs


def slot_of(core, here, size):
    block = lax.iota(jnp.int32, size) ^ here
    one = jnp.where(block == 0, 0, jnp.where(block == 1, 2, jnp.where(block == 2, 3, 1)))
    two = jnp.where(block < 2, block, 5 - block)
    return jnp.where(core == 0, one, two)


def halve(parts, names, second, also=()):
    kept, sent = [], []
    for part, name in zip(parts, names):
        dim = ("z", "y", "x").index(name)
        middle = part.shape[dim] // 2
        kept.append(lax.slice_in_dim(part, 0, middle, axis=dim))
        sent.append(
            lax.ppermute(
                lax.slice_in_dim(part, middle, None, axis=dim), DEVICES, partners(name, second)
            )
        )
    if also:
        sent, also = lax.optimization_barrier((sent, also))
    return [k + s for k, s in zip(kept, sent)], also


def layer_norm(rows):
    center = jnp.mean(rows, axis=1, keepdims=True)
    offset = rows - center
    inv_scale = lax.rsqrt(jnp.mean(offset * offset, axis=1, keepdims=True) + NORM_EPS)
    return offset * inv_scale, inv_scale


def item_kernel(key_ref, grad_ref, *refs):
    out_ref = refs[-1]
    rows = out_ref.shape[0]
    place = lax.broadcasted_iota(jnp.int32, (rows, key_ref.shape[1]), 0) + pl.program_id(0) * rows
    onehot = jnp.where(place == key_ref[...], 1.0, 0.0).astype(jnp.bfloat16)
    total = jnp.dot(onehot, grad_ref[...], preferred_element_type=jnp.float32)
    for ref in refs[:-1]:
        total = total + ref[...]
    out_ref[...] = total


def segment_sums(key, sample_grad, count, *more):
    samples, width_e = sample_grad.shape
    step = 512
    return pl.pallas_call(
        item_kernel,
        grid=(count // step,),
        in_specs=[
            pl.BlockSpec((1, samples), lambda i: (0, 0)),
            pl.BlockSpec((samples, width_e), lambda i: (0, 0)),
        ]
        + [pl.BlockSpec((step, width_e), lambda i: (i, 0))] * len(more),
        out_specs=pl.BlockSpec((step, width_e), lambda i: (i, 0)),
        out_shape=jax.ShapeDtypeStruct((count, width_e), jnp.float32),
        compiler_params=pltpu.CompilerParams(vmem_limit_bytes=24 << 20),
        cost_estimate=cost(2 * samples * width_e * count, 4 * width_e * count),
        name="segment_sums",
    )(key.reshape(1, samples), pltpu.with_memory_space_constraint(sample_grad, pltpu.HBM), *more)


def forward_kernel(units, titles_ref, gain_ref, w_ref, normed_ref, slope_ref, act_ref, mean_ref):
    rows, width = titles_ref.shape
    length = rows // units
    step = 8 * length

    @pl.when(pl.program_id(0) == 0)
    def _():
        for r in range(units // 8):
            block = titles_ref[r * step : (r + 1) * step, :].astype(jnp.float32)
            normed, _ = layer_norm(block)
            normed_ref[r * step : (r + 1) * step, :] = (normed * gain_ref[...]).astype(jnp.bfloat16)
            mean_ref[r * 8 : (r + 1) * 8, :] = jnp.mean(block.reshape(8, length, width), axis=1)

    for r in range(units // 8):
        pre = jnp.dot(
            normed_ref[r * step : (r + 1) * step, :],
            w_ref[...],
            preferred_element_type=jnp.float32,
        )
        square = pre * pre
        tangent = jnp.tanh(pre * (GELU_C + (GELU_C * GELU_K) * square))
        half = 0.5 + 0.5 * tangent
        value = pre * half
        slope = half + value * (1.0 - tangent) * (GELU_C + (3.0 * GELU_C * GELU_K) * square)
        slope_ref[r * step : (r + 1) * step, :] = slope.astype(jnp.bfloat16)
        act_ref[r * 8 : (r + 1) * 8, :] = jnp.mean(value.reshape(8, length, -1), axis=1)


def forward(titles, ln_gain, w_up):
    units, length, width = titles.shape
    rows, hidden = units * length, w_up.shape[1]
    block = 512
    return pl.pallas_call(
        functools.partial(forward_kernel, units),
        grid=(hidden // block,),
        in_specs=[
            pl.BlockSpec((rows, width), lambda i: (0, 0)),
            pl.BlockSpec((1, width), lambda i: (0, 0)),
            pl.BlockSpec((width, block), lambda i: (0, i)),
        ],
        out_specs=[
            pl.BlockSpec((rows, width), lambda i: (0, 0)),
            pl.BlockSpec((rows, block), lambda i: (0, i)),
            pl.BlockSpec((units, block), lambda i: (0, i)),
            pl.BlockSpec((units, width), lambda i: (0, 0)),
        ],
        out_shape=[
            jax.ShapeDtypeStruct((rows, width), jnp.bfloat16),
            pltpu.HBM((rows, hidden), jnp.bfloat16),
            jax.ShapeDtypeStruct((units, hidden), jnp.float32),
            jax.ShapeDtypeStruct((units, width), jnp.float32),
        ],
        compiler_params=pltpu.CompilerParams(vmem_limit_bytes=VMEM),
        cost_estimate=cost(8 * rows * width * hidden, 4 * rows * hidden, rows * hidden),
        name="forward",
    )(
        pltpu.with_memory_space_constraint(titles.reshape(rows, width), pltpu.HBM),
        ln_gain.reshape(1, width),
        pltpu.with_memory_space_constraint(w_up, pltpu.HBM),
    )


def place_sums(core_ref, keep_at, send_at, ups, down, proj, out_refs):
    slots = proj.shape[0] // 8
    part = down.shape[0] // slots
    n_x = slots // 8
    first = core_ref[0] == 0
    for q in range(slots // 2):
        y, x = q // n_x, q % n_x
        spots = [at[1, y] * n_x + at[2, x] for at in (keep_at, send_at)]
        pair = (y * 2 * n_x + x, (y * 2 + 1) * n_x + x)

        def store(refs, top, rows):
            even, odd = (rows(k) for k in pair)
            end = top + even.shape[0]
            refs[0][spots[0], top:end, :] = jnp.where(first, even, odd)
            refs[1][spots[1], top:end, :] = jnp.where(first, odd, even)

        for index, up, refs in zip(*ups, zip(out_refs[::2], out_refs[1::2])):
            store(refs, 0, lambda k: up[k * part : (k + 1) * part])
            low = index * 8
            store(refs, part, lambda k: down[k * part + low : k * part + low + 8])
            if index == 0:
                store(refs, part + 8, lambda k: proj[k * 8 : (k + 1) * 8])


def first_kernel(
    units, core_ref, keep_at, send_at, slope_ref, act_ref, mean_ref, pool_ref, grad_ref,
    normed_ref, pre_ref, *out_refs
):
    rows, block = slope_ref.shape
    length, step = rows // units, rows // units * 8
    for r in range(units // 8):
        slope = slope_ref[r * step : (r + 1) * step, :].astype(jnp.float32)
        d_pre = slope.reshape(8, length, block) * act_ref[r * 8 : (r + 1) * 8, :][:, None, :]
        pre_ref[r * step : (r + 1) * step, :] = d_pre.reshape(step, block).astype(jnp.bfloat16)
    up = contract_first(pre_ref[...], normed_ref[...])
    down = contract_first(mean_ref[...], grad_ref[...])
    proj = contract_first(pool_ref[...], grad_ref[...])
    place_sums(core_ref, keep_at, send_at, ((0,), (up,)), down, proj, out_refs)


def other_kernel(
    indices, core_ref, keep_at, send_at, pre_ref, mean_ref, pool_ref, grad_ref, *refs
):
    count = len(indices)
    normed = jnp.concatenate([ref[...] for ref in refs[:count]], axis=1)
    up = contract_first(pre_ref[...], normed)
    down = contract_first(mean_ref[...], grad_ref[...])
    wide = grad_ref.shape[1]
    ups = [up[:, p * wide : (p + 1) * wide] for p in range(count)]
    empty = jnp.zeros((pool_ref.shape[1], 1), jnp.float32)
    place_sums(core_ref, keep_at, send_at, (indices, ups), down, empty, refs[count:])


def up_products(tables, indices, left, normed_b, mean_act_b, pooled_b, grad_b):
    rows, hidden = left[0].shape
    units, width_e = grad_b.shape
    sides = tables[1].shape[1]
    slots = 2 * sides * sides
    part = hidden // sides // slots
    tall = [part + 8 + 8 * (index == 0) for index in indices for _ in range(2)]
    first = len(left) == 2

    def columns(array):
        return pl.BlockSpec((array.shape[0], array.shape[1] // sides), lambda i, c, k, s: (0, i))

    def lanes(index):
        return pl.BlockSpec((rows, width_e), lambda i, c, k, s: (0, index))

    def sums(height, table):
        return pl.BlockSpec(
            (slots // 2, height, width_e), lambda i, *tables: (tables[table][0, i], 0, 0)
        )

    out_specs = [sums(h, 1 + n % 2) for n, h in enumerate(tall)]
    out_shape = [jax.ShapeDtypeStruct((sides * slots // 2, h, width_e), jnp.float32) for h in tall]
    if first:
        kernel = functools.partial(first_kernel, units)
        out_specs.insert(0, columns(left[0]))
        out_shape.insert(0, pltpu.VMEM((rows, hidden), jnp.bfloat16))
    else:
        kernel = functools.partial(other_kernel, indices)
    return pl.pallas_call(
        kernel,
        grid_spec=pltpu.PrefetchScalarGridSpec(
            num_scalar_prefetch=3,
            grid=(sides,),
            in_specs=[columns(array) for array in left]
            + [columns(mean_act_b), columns(pooled_b)]
            + [pl.BlockSpec(grad_b.shape, lambda i, c, k, s: (0, 0))]
            + [lanes(index) for index in indices],
            out_specs=out_specs,
        ),
        out_shape=out_shape,
        compiler_params=pltpu.CompilerParams(vmem_limit_bytes=VMEM),
        cost_estimate=cost(2 * rows * width_e * len(indices) * hidden, 4 * rows * hidden),
        name="first_products" if first else "other_products",
    )(*tables, *left, mean_act_b, pooled_b, grad_b, *[normed_b] * len(indices))


def titles_kernel(pre_ref, w_ref, titles_ref, gain_ref, pool_ref, out_ref, gain_out):
    rows, width = titles_ref.shape
    units = pool_ref.shape[0]
    length = rows // units
    d_normed = contract_last(pre_ref[...], w_ref[...])
    normed, inv_scale = layer_norm(titles_ref[...].astype(jnp.float32))
    product = d_normed * normed

    @pl.when(pl.program_id(0) == 0)
    def _():
        gain_out[...] = jnp.zeros_like(gain_out)

    gain_out[...] += jnp.sum(product.reshape(rows // 8, 8, width), axis=0)
    d_hat = d_normed * gain_ref[...]
    d_flat = inv_scale * (
        d_hat
        - jnp.mean(d_hat, axis=1, keepdims=True)
        - normed * jnp.mean(d_hat * normed, axis=1, keepdims=True)
    )
    d_block = d_flat.reshape(units, length, width) + (pool_ref[...] * (1.0 / length))[:, None, :]
    out_ref[...] = d_block.reshape(rows, width).astype(jnp.bfloat16)


def title_grads(d_pre, w_up, titles, ln_gain, d_pooled):
    units, length, width = titles.shape
    rows, hidden = d_pre.shape
    step = 8 * length
    return pl.pallas_call(
        titles_kernel,
        grid=(rows // step,),
        in_specs=[
            pl.BlockSpec((step, hidden), lambda i: (i, 0)),
            pl.BlockSpec((width, hidden), lambda i: (0, 0)),
            pl.BlockSpec((step, width), lambda i: (i, 0)),
            pl.BlockSpec((1, width), lambda i: (0, 0)),
            pl.BlockSpec((8, width), lambda i: (i, 0)),
        ],
        out_specs=[
            pl.BlockSpec((step, width), lambda i: (i, 0)),
            pl.BlockSpec((8, width), lambda i: (0, 0)),
        ],
        out_shape=[
            jax.ShapeDtypeStruct((rows, width), jnp.bfloat16),
            jax.ShapeDtypeStruct((8, width), jnp.float32),
        ],
        compiler_params=pltpu.CompilerParams(vmem_limit_bytes=VMEM),
        cost_estimate=cost(2 * rows * width * hidden, 2 * rows * hidden),
        name="title_grads",
    )(d_pre, w_up, titles.reshape(rows, width), ln_gain.reshape(1, width), d_pooled)


def rows_kernel(arrived_ref, table_ref, accum_ref, table_out, accum_out):
    step, width_e = table_ref.shape
    slots = arrived_ref.shape[0]
    grads = arrived_ref[:, :width_e]
    ids = arrived_ref[:, width_e : width_e + 1].astype(jnp.int32)
    here = lax.broadcasted_iota(jnp.int32, (slots, step), 1) + pl.program_id(0) * step
    onehot = jnp.where(here == ids, 1.0, 0.0).astype(jnp.bfloat16)
    high = grads.astype(jnp.bfloat16)
    low = (grads - high.astype(jnp.float32)).astype(jnp.bfloat16)
    row_grad = contract_first(onehot, high) + contract_first(onehot, low)
    new_accum = accum_ref[...] + row_grad * row_grad
    accum_out[...] = new_accum
    table_out[...] = table_ref[...] - LEARN_RATE * row_grad * lax.rsqrt(new_accum)


def row_update(arrived, table, accum):
    rows, width_e = table.shape
    step = 256
    tile = pl.BlockSpec((step, width_e), lambda i: (i, 0))
    return pl.pallas_call(
        rows_kernel,
        grid=(rows // step,),
        in_specs=[pl.BlockSpec(arrived.shape, lambda i: (0, 0)), tile, tile],
        out_specs=[tile, tile],
        out_shape=[jax.ShapeDtypeStruct((rows, width_e), jnp.float32)] * 2,
        compiler_params=pltpu.CompilerParams(vmem_limit_bytes=16 << 20),
        cost_estimate=cost(4 * rows * width_e * arrived.shape[0], 16 * rows * width_e),
        name="row_update",
    )(
        arrived,
        pltpu.with_memory_space_constraint(table, pltpu.HBM),
        pltpu.with_memory_space_constraint(accum, pltpu.HBM),
    )


def per_device(
    titles,
    ln_gain,
    w_up,
    w_down,
    w_proj,
    sample_grad,
    sample_item,
    sample_row,
    row_ids,
    table,
    accum,
):
    n_z, n_y, n_c, n_x = (lax.axis_size(name) for name in DEVICES)
    chips, groups = n_z * n_y * n_x, n_z * n_y * n_c
    devices = chips * n_c
    core, my_x = lax.axis_index("c"), lax.axis_index("x")
    units, length, width = titles.shape
    hidden = w_up.shape[1]
    width_e = sample_grad.shape[1]
    share_f, share_d = hidden // devices, width // devices

    owner = sample_item // units
    spot = (owner // (n_c * n_x) * n_x + owner % n_x) * units + sample_item % units
    of_core = owner // n_x % n_c
    sent = segment_sums(jnp.where(of_core == core, -1, spot), sample_grad, chips * units)
    got = swap_cores(sent)
    mine = segment_sums(jnp.where(of_core == core, spot, -1), sample_grad, chips * units, got)
    mine = mine.reshape(chips, units, width_e)
    mine, ln_gain = lax.optimization_barrier((mine, ln_gain))
    item_all = lax.all_to_all(mine, CHIPS, 0, 0, tiled=True)

    slot_count = row_ids.shape[1]
    rows_here = table.shape[0]
    slot_hot = (sample_row[:, None] == lax.iota(jnp.int32, slot_count)[None, :]).astype(
        jnp.bfloat16
    )
    local_rows = (row_ids[0] % rows_here).astype(jnp.float32)
    row_part = jnp.concatenate(
        [
            contract_first(slot_hot, sample_grad),
            jnp.broadcast_to(local_rows[:, None], (slot_count, 128)),
        ],
        axis=1,
    )
    row_part = row_part.reshape(devices, slot_count // devices, width_e + 128)

    normed_b, slope, mean_act, mean_title = forward(titles, ln_gain, w_up)
    mean_act_b = mean_act.astype(jnp.bfloat16)
    pooled = mean_title + jnp.dot(mean_act_b, w_down, preferred_element_type=jnp.float32)
    lane = lax.iota(jnp.int32, devices * 8)
    source = jnp.where(lane % 8 < share_d, lane // 8 * share_d + lane % 8, -1)
    spread = (lax.iota(jnp.int32, width)[:, None] == source[None, :]).astype(jnp.bfloat16)
    pooled_b = jnp.dot(
        pooled.astype(jnp.bfloat16), spread, preferred_element_type=jnp.float32
    ).astype(jnp.bfloat16)
    item_all, pooled_b, row_part = lax.optimization_barrier((item_all, pooled_b, row_part))

    item_grad = jnp.sum(item_all, axis=0)
    grad_b = item_grad.astype(jnp.bfloat16)
    d_pooled = contract_last(grad_b, w_proj)
    d_act = contract_last(d_pooled.astype(jnp.bfloat16), w_down) / length

    here = [(lax.axis_index(name), lax.axis_size(name)) for name in CHIPS]
    keep_at = jnp.stack([slot_of(core, at, size) for at, size in here])
    send_at = jnp.stack([slot_of(1 - core, at, size) for at, size in here])
    tables = (core.reshape(1), keep_at, send_at)
    items = (normed_b, mean_act_b, pooled_b, grad_b)
    slope = pltpu.with_memory_space_constraint(slope, pltpu.HBM)
    d_pre, *sums = up_products(tables, (0,), (slope, d_act), *items)
    d_pre = pltpu.with_memory_space_constraint(d_pre, pltpu.VMEM)
    for index in (1, 2):
        sums += up_products(tables, (index,), (d_pre,), *items)
    parts = [
        (keep + swap_cores(send)).reshape(n_z, n_y, n_x, -1, width_e)
        for keep, send in zip(sums[::2], sums[1::2])
    ]

    beside = title_grads(d_pre, w_up, titles, ln_gain, d_pooled)
    parts, (d_titles, gain_term) = halve(parts, "xyz", False, tuple(beside))
    parts, row_part = lax.optimization_barrier((parts, row_part))
    row_all = lax.all_to_all(row_part, DEVICES, 0, 0, tiled=True)
    gain_term = (gain_term + swap_cores(gain_term)).reshape(8, 3, width_e)
    gain_term = jnp.pad(jnp.sum(gain_term, axis=0), ((0, 5), (0, 0)))
    parts, (gain_term,) = halve(parts, "xyz", True, (gain_term,))
    gain_term = jnp.broadcast_to(gain_term, parts[0].shape[:3] + gain_term.shape)
    parts[0] = jnp.concatenate([parts[0], gain_term], axis=3)
    parts, _ = halve(parts, "yzx", False)
    parts, (row_all,) = halve(parts, "yzx", True, (row_all,))
    row_all = row_all.reshape(slot_count, width_e + 128)
    parts, (row_all,) = halve(parts, "zxy", False, (row_all,))
    new_table, new_accum = row_update(row_all, table, accum)
    parts, _ = halve(parts, "zxy", True)

    flat = [part.reshape(-1, width_e) for part in parts]
    last = jnp.concatenate(flat, axis=0)
    blocks = jnp.stack([last, along(last, "x", 1), along(last, "x", 2), along(last, "x", 3)])
    ordered = jnp.stack(
        [lax.dynamic_index_in_dim(blocks, my_x ^ j, 0, keepdims=False) for j in range(n_x)]
    )
    starts = [0, share_f + 24, 2 * share_f + 32]
    grad_up = jnp.concatenate([ordered[:, at : at + share_f] for at in starts], axis=2)
    grad_up = grad_up.reshape(-1, width).T
    outer = jnp.concatenate(
        [ordered[:, at + share_f : at + share_f + 8] for at in starts], axis=1
    ).reshape(-1, width_e)
    high = outer.astype(jnp.bfloat16)
    low = (outer - high.astype(jnp.float32)).astype(jnp.bfloat16)
    grad_down = contract_last(high, w_proj) + contract_last(low, w_proj)
    grad_proj = ordered[:, share_f + 8 : share_f + 8 + share_d].reshape(-1, width_e)
    gains = jnp.sum(ordered[:, share_f + 16 : share_f + 19], axis=0).reshape(width)
    mine_at = (lax.axis_index("z") * n_y + lax.axis_index("y")) * n_c + core
    grad_gain = lax.dynamic_slice_in_dim(gains, mine_at * (width // groups), width // groups, 0)
    return (
        d_titles.reshape(units, length, width),
        grad_up,
        grad_down,
        grad_proj,
        grad_gain,
        new_table,
        new_accum,
    )


def solution(mesh):
    n_table, n_rep = mesh.devices.shape
    side = n_rep
    fine = Mesh(mesh.devices.reshape(n_table // (2 * side), side, 2, n_rep), DEVICES)
    split, tab = P(DEVICES), P(GROUP)
    return jax.shard_map(
        per_device,
        mesh=fine,
        in_specs=(split, P(), P(), P(), P(), split, split, split, split, split, split),
        out_specs=(split, P(None, GROUP), tab, tab, tab, split, split),
        check_vma=False,
    )
```

```python
import functools
import math

import jax
import jax.numpy as jnp
from jax import lax
from jax.experimental import pallas as pl
from jax.experimental.pallas import tpu as pltpu
from jax.sharding import Mesh
from jax.sharding import PartitionSpec as P

GELU_C = 0.7978845608028654
GELU_K = 0.044715
NORM_EPS = 1e-05
LEARN_RATE = 0.1
CHIPS = ("z", "y", "x")
GROUP = ("z", "y", "c")
DEVICES = ("z", "y", "c", "x")
VMEM = 30 << 20


def contract_first(left, right):
    return lax.dot_general(
        left, right, (((0,), (0,)), ((), ())), preferred_element_type=jnp.float32
    )


def contract_last(left, right):
    return lax.dot_general(
        left, right, (((1,), (1,)), ((), ())), preferred_element_type=jnp.float32
    )


def cost(flops, moved, transcendentals=0):
    return pl.CostEstimate(flops=flops, bytes_accessed=moved, transcendentals=transcendentals)


def swap_cores(block):
    return lax.ppermute(block, "c", [(0, 1), (1, 0)])


def along(block, name, step):
    size = lax.axis_size(name)
    return lax.ppermute(block, name, [(i, i ^ step) for i in range(size)])


def partners(name, second):
    sizes = [lax.axis_size(n) for n in DEVICES]
    at = DEVICES.index(name)
    pairs = []
    for index in range(math.prod(sizes)):
        place, rest = [], index
        for size in reversed(sizes):
            place.insert(0, rest % size)
            rest //= size
        place[at] ^= 1 if (place[DEVICES.index("c")] == 1) == second else 3
        to = 0
        for size, p in zip(sizes, place):
            to = to * size + p
        pairs.append((index, to))
    return pairs


def slot_of(core, here, size):
    block = lax.iota(jnp.int32, size) ^ here
    one = jnp.where(block == 0, 0, jnp.where(block == 1, 2, jnp.where(block == 2, 3, 1)))
    two = jnp.where(block < 2, block, 5 - block)
    return jnp.where(core == 0, one, two)


def halve(parts, names, second, also=()):
    kept, sent = [], []
    for part, name in zip(parts, names):
        dim = ("z", "y", "x").index(name)
        middle = part.shape[dim] // 2
        kept.append(lax.slice_in_dim(part, 0, middle, axis=dim))
        sent.append(
            lax.ppermute(
                lax.slice_in_dim(part, middle, None, axis=dim), DEVICES, partners(name, second)
            )
        )
    if also:
        sent, also = lax.optimization_barrier((sent, also))
    return [k + s for k, s in zip(kept, sent)], also


def layer_norm(rows):
    center = jnp.mean(rows, axis=1, keepdims=True)
    offset = rows - center
    inv_scale = lax.rsqrt(jnp.mean(offset * offset, axis=1, keepdims=True) + NORM_EPS)
    return offset * inv_scale, inv_scale


def item_kernel(key_ref, grad_ref, *refs):
    out_ref = refs[-1]
    rows = out_ref.shape[0]
    place = lax.broadcasted_iota(jnp.int32, (rows, key_ref.shape[1]), 0) + pl.program_id(0) * rows
    onehot = jnp.where(place == key_ref[...], 1.0, 0.0).astype(jnp.bfloat16)
    total = jnp.dot(onehot, grad_ref[...], preferred_element_type=jnp.float32)
    for ref in refs[:-1]:
        total = total + ref[...]
    out_ref[...] = total


def segment_sums(key, sample_grad, count, *more):
    samples, width_e = sample_grad.shape
    step = 512
    return pl.pallas_call(
        item_kernel,
        grid=(count // step,),
        in_specs=[
            pl.BlockSpec((1, samples), lambda i: (0, 0)),
            pl.BlockSpec((samples, width_e), lambda i: (0, 0)),
        ]
        + [pl.BlockSpec((step, width_e), lambda i: (i, 0))] * len(more),
        out_specs=pl.BlockSpec((step, width_e), lambda i: (i, 0)),
        out_shape=jax.ShapeDtypeStruct((count, width_e), jnp.float32),
        compiler_params=pltpu.CompilerParams(vmem_limit_bytes=24 << 20),
        cost_estimate=cost(2 * samples * width_e * count, 4 * width_e * count),
        name="segment_sums",
    )(key.reshape(1, samples), sample_grad, *more)


def forward_kernel(units, titles_ref, gain_ref, w_ref, normed_ref, slope_ref, act_ref, mean_ref):
    rows, width = titles_ref.shape
    length = rows // units
    step = 8 * length

    @pl.when(pl.program_id(0) == 0)
    def _():
        for r in range(units // 8):
            block = titles_ref[r * step : (r + 1) * step, :].astype(jnp.float32)
            normed, _ = layer_norm(block)
            normed_ref[r * step : (r + 1) * step, :] = (normed * gain_ref[...]).astype(jnp.bfloat16)
            mean_ref[r * 8 : (r + 1) * 8, :] = jnp.mean(block.reshape(8, length, width), axis=1)

    for r in range(units // 8):
        pre = jnp.dot(
            normed_ref[r * step : (r + 1) * step, :],
            w_ref[...],
            preferred_element_type=jnp.float32,
        )
        square = pre * pre
        tangent = jnp.tanh(pre * (GELU_C + (GELU_C * GELU_K) * square))
        half = 0.5 + 0.5 * tangent
        value = pre * half
        slope = half + value * (1.0 - tangent) * (GELU_C + (3.0 * GELU_C * GELU_K) * square)
        slope_ref[r * step : (r + 1) * step, :] = slope.astype(jnp.bfloat16)
        act_ref[r * 8 : (r + 1) * 8, :] = jnp.mean(value.reshape(8, length, -1), axis=1)


def forward(titles, ln_gain, w_up):
    units, length, width = titles.shape
    rows, hidden = units * length, w_up.shape[1]
    block = 512
    return pl.pallas_call(
        functools.partial(forward_kernel, units),
        grid=(hidden // block,),
        in_specs=[
            pl.BlockSpec((rows, width), lambda i: (0, 0)),
            pl.BlockSpec((1, width), lambda i: (0, 0)),
            pl.BlockSpec((width, block), lambda i: (0, i)),
        ],
        out_specs=[
            pl.BlockSpec((rows, width), lambda i: (0, 0)),
            pl.BlockSpec((rows, block), lambda i: (0, i)),
            pl.BlockSpec((units, block), lambda i: (0, i)),
            pl.BlockSpec((units, width), lambda i: (0, 0)),
        ],
        out_shape=[
            jax.ShapeDtypeStruct((rows, width), jnp.bfloat16),
            pltpu.HBM((rows, hidden), jnp.bfloat16),
            jax.ShapeDtypeStruct((units, hidden), jnp.float32),
            jax.ShapeDtypeStruct((units, width), jnp.float32),
        ],
        compiler_params=pltpu.CompilerParams(vmem_limit_bytes=VMEM),
        cost_estimate=cost(8 * rows * width * hidden, 4 * rows * hidden, rows * hidden),
        name="forward",
    )(
        pltpu.with_memory_space_constraint(titles.reshape(rows, width), pltpu.HBM),
        ln_gain.reshape(1, width),
        pltpu.with_memory_space_constraint(w_up, pltpu.HBM),
    )


def place_sums(core_ref, keep_at, send_at, ups, down, proj, out_refs):
    slots = proj.shape[0] // 8
    part = down.shape[0] // slots
    n_x = slots // 8
    first = core_ref[0] == 0
    for q in range(slots // 2):
        y, x = q // n_x, q % n_x
        spots = [at[1, y] * n_x + at[2, x] for at in (keep_at, send_at)]
        pair = (y * 2 * n_x + x, (y * 2 + 1) * n_x + x)

        def store(refs, top, rows):
            even, odd = (rows(k) for k in pair)
            end = top + even.shape[0]
            refs[0][spots[0], top:end, :] = jnp.where(first, even, odd)
            refs[1][spots[1], top:end, :] = jnp.where(first, odd, even)

        for index, up, refs in zip(*ups, zip(out_refs[::2], out_refs[1::2])):
            store(refs, 0, lambda k: up[k * part : (k + 1) * part])
            low = index * 8
            store(refs, part, lambda k: down[k * part + low : k * part + low + 8])
            if index == 0:
                store(refs, part + 8, lambda k: proj[k * 8 : (k + 1) * 8])


def first_kernel(
    units, core_ref, keep_at, send_at, slope_ref, mean_ref, pool_ref, grad_ref,
    pool_grad_ref, down_ref, normed_ref, pre_ref, *out_refs
):
    rows, block = slope_ref.shape
    length, step = rows // units, rows // units * 8
    d_act = contract_last(pool_grad_ref[...], down_ref[...]) * (1.0 / length)
    for r in range(units // 8):
        slope = slope_ref[r * step : (r + 1) * step, :].astype(jnp.float32)
        d_pre = slope.reshape(8, length, block) * d_act[r * 8 : (r + 1) * 8, :][:, None, :]
        pre_ref[r * step : (r + 1) * step, :] = d_pre.reshape(step, block).astype(jnp.bfloat16)
    up = contract_first(pre_ref[...], normed_ref[...])
    down = contract_first(mean_ref[...], grad_ref[...])
    proj = contract_first(pool_ref[...], grad_ref[...])
    place_sums(core_ref, keep_at, send_at, ((0,), (up,)), down, proj, out_refs)


def other_kernel(
    indices, core_ref, keep_at, send_at, pre_ref, mean_ref, pool_ref, grad_ref, *refs
):
    count = len(indices)
    normed = jnp.concatenate([ref[...] for ref in refs[:count]], axis=1)
    up = contract_first(pre_ref[...], normed)
    down = contract_first(mean_ref[...], grad_ref[...])
    wide = grad_ref.shape[1]
    ups = [up[:, p * wide : (p + 1) * wide] for p in range(count)]
    empty = jnp.zeros((pool_ref.shape[1], 1), jnp.float32)
    place_sums(core_ref, keep_at, send_at, (indices, ups), down, empty, refs[count:])


def up_products(tables, indices, left, normed_b, mean_act_b, pooled_b, grad_b):
    rows, hidden = left[0].shape
    units, width_e = grad_b.shape
    sides = tables[1].shape[1]
    slots = 2 * sides * sides
    part = hidden // sides // slots
    tall = [part + 8 + 8 * (index == 0) for index in indices for _ in range(2)]
    first = len(left) == 3

    def columns(array):
        return pl.BlockSpec((array.shape[0], array.shape[1] // sides), lambda i, c, k, s: (0, i))

    def lanes(index):
        return pl.BlockSpec((rows, width_e), lambda i, c, k, s: (0, index))

    def sums(height, table):
        return pl.BlockSpec(
            (slots // 2, height, width_e), lambda i, *tables: (tables[table][0, i], 0, 0)
        )

    out_specs = [sums(h, 1 + n % 2) for n, h in enumerate(tall)]
    out_shape = [jax.ShapeDtypeStruct((sides * slots // 2, h, width_e), jnp.float32) for h in tall]
    extra = []
    if first:
        width = left[1].shape[1]
        extra = [
            pl.BlockSpec((units, width), lambda i, c, k, s: (0, 0)),
            pl.BlockSpec((hidden // sides, width), lambda i, c, k, s: (i, 0)),
        ]
        kernel = functools.partial(first_kernel, units)
        out_specs.insert(0, columns(left[0]))
        out_shape.insert(0, pltpu.VMEM((rows, hidden), jnp.bfloat16))
    else:
        kernel = functools.partial(other_kernel, indices)
    return pl.pallas_call(
        kernel,
        grid_spec=pltpu.PrefetchScalarGridSpec(
            num_scalar_prefetch=3,
            grid=(sides,),
            in_specs=[columns(left[0]), columns(mean_act_b), columns(pooled_b)]
            + [pl.BlockSpec(grad_b.shape, lambda i, c, k, s: (0, 0))]
            + extra
            + [lanes(index) for index in indices],
            out_specs=out_specs,
        ),
        out_shape=out_shape,
        compiler_params=pltpu.CompilerParams(vmem_limit_bytes=VMEM),
        cost_estimate=cost(2 * rows * width_e * len(indices) * hidden, 4 * rows * hidden),
        name="first_products" if first else "other_products",
    )(*tables, left[0], mean_act_b, pooled_b, grad_b, *left[1:], *[normed_b] * len(indices))


def titles_kernel(pre_ref, w_ref, titles_ref, gain_ref, pool_ref, out_ref, gain_out):
    rows, width = titles_ref.shape
    units = pool_ref.shape[0]
    length = rows // units
    d_normed = contract_last(pre_ref[...], w_ref[...])
    normed, inv_scale = layer_norm(titles_ref[...].astype(jnp.float32))
    product = d_normed * normed

    @pl.when(pl.program_id(0) == 0)
    def _():
        gain_out[...] = jnp.zeros_like(gain_out)

    gain_out[...] += jnp.sum(product.reshape(rows // 8, 8, width), axis=0)
    d_hat = d_normed * gain_ref[...]
    d_flat = inv_scale * (
        d_hat
        - jnp.mean(d_hat, axis=1, keepdims=True)
        - normed * jnp.mean(d_hat * normed, axis=1, keepdims=True)
    )
    d_block = d_flat.reshape(units, length, width) + (pool_ref[...] * (1.0 / length))[:, None, :]
    out_ref[...] = d_block.reshape(rows, width).astype(jnp.bfloat16)


def title_grads(d_pre, w_up, titles, ln_gain, d_pooled):
    units, length, width = titles.shape
    rows, hidden = d_pre.shape
    step = 8 * length
    return pl.pallas_call(
        titles_kernel,
        grid=(rows // step,),
        in_specs=[
            pl.BlockSpec((step, hidden), lambda i: (i, 0)),
            pl.BlockSpec((width, hidden), lambda i: (0, 0)),
            pl.BlockSpec((step, width), lambda i: (i, 0)),
            pl.BlockSpec((1, width), lambda i: (0, 0)),
            pl.BlockSpec((8, width), lambda i: (i, 0)),
        ],
        out_specs=[
            pl.BlockSpec((step, width), lambda i: (i, 0)),
            pl.BlockSpec((8, width), lambda i: (0, 0)),
        ],
        out_shape=[
            jax.ShapeDtypeStruct((rows, width), jnp.bfloat16),
            jax.ShapeDtypeStruct((8, width), jnp.float32),
        ],
        compiler_params=pltpu.CompilerParams(vmem_limit_bytes=VMEM),
        cost_estimate=cost(2 * rows * width * hidden, 2 * rows * hidden),
        name="title_grads",
    )(d_pre, w_up, titles.reshape(rows, width), ln_gain.reshape(1, width), d_pooled)


def rows_kernel(arrived_ref, table_ref, accum_ref, table_out, accum_out):
    step, width_e = table_ref.shape
    slots = arrived_ref.shape[0]
    grads = arrived_ref[:, :width_e]
    ids = arrived_ref[:, width_e : width_e + 1].astype(jnp.int32)
    here = lax.broadcasted_iota(jnp.int32, (slots, step), 1) + pl.program_id(0) * step
    onehot = jnp.where(here == ids, 1.0, 0.0).astype(jnp.bfloat16)
    high = grads.astype(jnp.bfloat16)
    low = (grads - high.astype(jnp.float32)).astype(jnp.bfloat16)
    row_grad = contract_first(onehot, high) + contract_first(onehot, low)
    new_accum = accum_ref[...] + row_grad * row_grad
    accum_out[...] = new_accum
    table_out[...] = table_ref[...] - LEARN_RATE * row_grad * lax.rsqrt(new_accum)


def row_update(arrived, table, accum):
    rows, width_e = table.shape
    step = 1024
    tile = pl.BlockSpec((step, width_e), lambda i: (i, 0))
    return pl.pallas_call(
        rows_kernel,
        grid=(rows // step,),
        in_specs=[pl.BlockSpec(arrived.shape, lambda i: (0, 0)), tile, tile],
        out_specs=[tile, tile],
        out_shape=[jax.ShapeDtypeStruct((rows, width_e), jnp.float32)] * 2,
        compiler_params=pltpu.CompilerParams(vmem_limit_bytes=24 << 20),
        cost_estimate=cost(4 * rows * width_e * arrived.shape[0], 16 * rows * width_e),
        name="row_update",
    )(
        arrived,
        pltpu.with_memory_space_constraint(table, pltpu.HBM),
        pltpu.with_memory_space_constraint(accum, pltpu.HBM),
    )


def per_device(
    titles,
    ln_gain,
    w_up,
    w_down,
    w_proj,
    sample_grad,
    sample_item,
    sample_row,
    row_ids,
    table,
    accum,
):
    n_z, n_y, n_c, n_x = (lax.axis_size(name) for name in DEVICES)
    chips, groups = n_z * n_y * n_x, n_z * n_y * n_c
    devices = chips * n_c
    core, my_x = lax.axis_index("c"), lax.axis_index("x")
    units, length, width = titles.shape
    hidden = w_up.shape[1]
    width_e = sample_grad.shape[1]
    share_f, share_d = hidden // devices, width // devices

    owner = sample_item // units
    spot = (owner // (n_c * n_x) * n_x + owner % n_x) * units + sample_item % units
    of_core = owner // n_x % n_c
    sent = segment_sums(jnp.where(of_core == core, -1, spot), sample_grad, chips * units)
    got = swap_cores(sent)
    mine = segment_sums(jnp.where(of_core == core, spot, -1), sample_grad, chips * units, got)
    mine = mine.reshape(chips, units, width_e)
    mine, ln_gain = lax.optimization_barrier((mine, ln_gain))
    item_all = lax.all_to_all(mine, CHIPS, 0, 0, tiled=True)

    slot_count = row_ids.shape[1]
    rows_here = table.shape[0]
    slot_hot = (sample_row[:, None] == lax.iota(jnp.int32, slot_count)[None, :]).astype(
        jnp.bfloat16
    )
    local_rows = (row_ids[0] % rows_here).astype(jnp.float32)
    row_part = jnp.concatenate(
        [
            contract_first(slot_hot, sample_grad),
            jnp.broadcast_to(local_rows[:, None], (slot_count, 128)),
        ],
        axis=1,
    )
    row_part = row_part.reshape(devices, slot_count // devices, width_e + 128)

    normed_b, slope, mean_act, mean_title = forward(titles, ln_gain, w_up)
    mean_act_b = mean_act.astype(jnp.bfloat16)
    pooled = mean_title + jnp.dot(mean_act_b, w_down, preferred_element_type=jnp.float32)
    lane = lax.iota(jnp.int32, devices * 8)
    source = jnp.where(lane % 8 < share_d, lane // 8 * share_d + lane % 8, -1)
    spread = (lax.iota(jnp.int32, width)[:, None] == source[None, :]).astype(jnp.bfloat16)
    pooled_b = jnp.dot(
        pooled.astype(jnp.bfloat16), spread, preferred_element_type=jnp.float32
    ).astype(jnp.bfloat16)
    item_all, pooled_b, row_part = lax.optimization_barrier((item_all, pooled_b, row_part))

    item_grad = jnp.sum(item_all, axis=0)
    grad_b = item_grad.astype(jnp.bfloat16)
    d_pooled = contract_last(grad_b, w_proj)
    d_pooled_b = d_pooled.astype(jnp.bfloat16)

    here = [(lax.axis_index(name), lax.axis_size(name)) for name in CHIPS]
    keep_at = jnp.stack([slot_of(core, at, size) for at, size in here])
    send_at = jnp.stack([slot_of(1 - core, at, size) for at, size in here])
    tables = (core.reshape(1), keep_at, send_at)
    items = (normed_b, mean_act_b, pooled_b, grad_b)
    slope = pltpu.with_memory_space_constraint(slope, pltpu.HBM)
    d_pre, *sums = up_products(tables, (0,), (slope, d_pooled_b, w_down), *items)
    d_pre = pltpu.with_memory_space_constraint(d_pre, pltpu.VMEM)
    for index in (1, 2):
        sums += up_products(tables, (index,), (d_pre,), *items)
    parts = [
        (keep + swap_cores(send)).reshape(n_z, n_y, n_x, -1, width_e)
        for keep, send in zip(sums[::2], sums[1::2])
    ]

    beside = title_grads(d_pre, w_up, titles, ln_gain, d_pooled)
    parts, (d_titles, gain_term) = halve(parts, "xyz", False, tuple(beside))
    parts, row_part = lax.optimization_barrier((parts, row_part))
    row_all = lax.all_to_all(row_part, DEVICES, 0, 0, tiled=True)
    gain_term = (gain_term + swap_cores(gain_term)).reshape(8, 3, width_e)
    gain_term = jnp.pad(jnp.sum(gain_term, axis=0), ((0, 5), (0, 0)))
    parts, (gain_term,) = halve(parts, "xyz", True, (gain_term,))
    gain_term = jnp.broadcast_to(gain_term, parts[0].shape[:3] + gain_term.shape)
    parts[0] = jnp.concatenate([parts[0], gain_term], axis=3)
    parts, _ = halve(parts, "yzx", False)
    parts, (row_all,) = halve(parts, "yzx", True, (row_all,))
    new_table, new_accum = row_update(
        row_all.reshape(slot_count, width_e + 128), table, accum
    )
    parts, _ = halve(parts, "zxy", False)
    parts, _ = halve(parts, "zxy", True)

    flat = [part.reshape(-1, width_e) for part in parts]
    last = jnp.concatenate(flat, axis=0)
    blocks = jnp.stack([last, along(last, "x", 1), along(last, "x", 2), along(last, "x", 3)])
    ordered = jnp.stack(
        [lax.dynamic_index_in_dim(blocks, my_x ^ j, 0, keepdims=False) for j in range(n_x)]
    )
    starts = [0, share_f + 24, 2 * share_f + 32]
    grad_up = jnp.concatenate([ordered[:, at : at + share_f] for at in starts], axis=2)
    grad_up = grad_up.reshape(-1, width).T
    outer = jnp.concatenate(
        [ordered[:, at + share_f : at + share_f + 8] for at in starts], axis=1
    ).reshape(-1, width_e)
    high = outer.astype(jnp.bfloat16)
    low = (outer - high.astype(jnp.float32)).astype(jnp.bfloat16)
    grad_down = contract_last(high, w_proj) + contract_last(low, w_proj)
    grad_proj = ordered[:, share_f + 8 : share_f + 8 + share_d].reshape(-1, width_e)
    gains = jnp.sum(ordered[:, share_f + 16 : share_f + 19], axis=0).reshape(width)
    mine_at = (lax.axis_index("z") * n_y + lax.axis_index("y")) * n_c + core
    grad_gain = lax.dynamic_slice_in_dim(gains, mine_at * (width // groups), width // groups, 0)
    return (
        d_titles.reshape(units, length, width),
        grad_up,
        grad_down,
        grad_proj,
        grad_gain,
        new_table,
        new_accum,
    )


def solution(mesh):
    n_table, n_rep = mesh.devices.shape
    side = n_rep
    fine = Mesh(mesh.devices.reshape(n_table // (2 * side), side, 2, n_rep), DEVICES)
    split, tab = P(DEVICES), P(GROUP)
    return jax.shard_map(
        per_device,
        mesh=fine,
        in_specs=(split, P(), P(), P(), P(), split, split, split, split, split, split),
        out_specs=(split, P(None, GROUP), tab, tab, tab, split, split),
        check_vma=False,
    )
```

```python
import functools
import math

import jax
import jax.numpy as jnp
from jax import lax
from jax.experimental import pallas as pl
from jax.experimental.pallas import tpu as pltpu
from jax.sharding import Mesh
from jax.sharding import PartitionSpec as P

GELU_C = 0.7978845608028654
GELU_K = 0.044715
NORM_EPS = 1e-05
LEARN_RATE = 0.1
CHIPS = ("z", "y", "x")
GROUP = ("z", "y", "c")
DEVICES = ("z", "y", "c", "x")
VMEM = 30 << 20


def contract_first(left, right):
    return lax.dot_general(
        left, right, (((0,), (0,)), ((), ())), preferred_element_type=jnp.float32
    )


def contract_last(left, right):
    return lax.dot_general(
        left, right, (((1,), (1,)), ((), ())), preferred_element_type=jnp.float32
    )


def cost(flops, moved, transcendentals=0):
    return pl.CostEstimate(flops=flops, bytes_accessed=moved, transcendentals=transcendentals)


def swap_cores(block):
    return lax.ppermute(block, "c", [(0, 1), (1, 0)])


def along(block, name, step):
    size = lax.axis_size(name)
    return lax.ppermute(block, name, [(i, i ^ step) for i in range(size)])


def partners(name, second):
    sizes = [lax.axis_size(n) for n in DEVICES]
    at = DEVICES.index(name)
    pairs = []
    for index in range(math.prod(sizes)):
        place, rest = [], index
        for size in reversed(sizes):
            place.insert(0, rest % size)
            rest //= size
        place[at] ^= 1 if (place[DEVICES.index("c")] == 1) == second else 3
        to = 0
        for size, p in zip(sizes, place):
            to = to * size + p
        pairs.append((index, to))
    return pairs


def slot_of(core, here, size):
    block = lax.iota(jnp.int32, size) ^ here
    one = jnp.where(block == 0, 0, jnp.where(block == 1, 2, jnp.where(block == 2, 3, 1)))
    two = jnp.where(block < 2, block, 5 - block)
    return jnp.where(core == 0, one, two)


def halve(parts, names, second, also=()):
    kept, sent = [], []
    for part, name in zip(parts, names):
        dim = ("z", "y", "x").index(name)
        middle = part.shape[dim] // 2
        kept.append(lax.slice_in_dim(part, 0, middle, axis=dim))
        sent.append(
            lax.ppermute(
                lax.slice_in_dim(part, middle, None, axis=dim), DEVICES, partners(name, second)
            )
        )
    if also:
        sent, also = lax.optimization_barrier((sent, also))
    return [k + s for k, s in zip(kept, sent)], also


def layer_norm(rows):
    center = jnp.mean(rows, axis=1, keepdims=True)
    offset = rows - center
    inv_scale = lax.rsqrt(jnp.mean(offset * offset, axis=1, keepdims=True) + NORM_EPS)
    return offset * inv_scale, inv_scale


def item_kernel(key_ref, grad_ref, *refs):
    out_ref = refs[-1]
    rows = out_ref.shape[0]
    place = lax.broadcasted_iota(jnp.int32, (rows, key_ref.shape[1]), 0) + pl.program_id(0) * rows
    onehot = jnp.where(place == key_ref[...], 1.0, 0.0).astype(jnp.bfloat16)
    total = jnp.dot(onehot, grad_ref[...], preferred_element_type=jnp.float32)
    for ref in refs[:-1]:
        total = total + ref[...]
    out_ref[...] = total


def segment_sums(key, sample_grad, count, *more):
    samples, width_e = sample_grad.shape
    step = 512
    return pl.pallas_call(
        item_kernel,
        grid=(count // step,),
        in_specs=[
            pl.BlockSpec((1, samples), lambda i: (0, 0)),
            pl.BlockSpec((samples, width_e), lambda i: (0, 0)),
        ]
        + [pl.BlockSpec((step, width_e), lambda i: (i, 0))] * len(more),
        out_specs=pl.BlockSpec((step, width_e), lambda i: (i, 0)),
        out_shape=jax.ShapeDtypeStruct((count, width_e), jnp.float32),
        compiler_params=pltpu.CompilerParams(vmem_limit_bytes=24 << 20),
        cost_estimate=cost(2 * samples * width_e * count, 4 * width_e * count),
        name="segment_sums",
    )(key.reshape(1, samples), sample_grad, *more)


def forward_kernel(units, titles_ref, gain_ref, w_ref, normed_ref, slope_ref, act_ref, mean_ref):
    rows, width = titles_ref.shape
    length = rows // units
    step = 8 * length

    @pl.when(pl.program_id(0) == 0)
    def _():
        for r in range(units // 8):
            block = titles_ref[r * step : (r + 1) * step, :].astype(jnp.float32)
            normed, _ = layer_norm(block)
            normed_ref[r * step : (r + 1) * step, :] = (normed * gain_ref[...]).astype(jnp.bfloat16)
            mean_ref[r * 8 : (r + 1) * 8, :] = jnp.mean(block.reshape(8, length, width), axis=1)

    for r in range(units // 8):
        pre = jnp.dot(
            normed_ref[r * step : (r + 1) * step, :],
            w_ref[...],
            preferred_element_type=jnp.float32,
        )
        square = pre * pre
        tangent = jnp.tanh(pre * (GELU_C + (GELU_C * GELU_K) * square))
        half = 0.5 + 0.5 * tangent
        value = pre * half
        slope = half + value * (1.0 - tangent) * (GELU_C + (3.0 * GELU_C * GELU_K) * square)
        slope_ref[r * step : (r + 1) * step, :] = slope.astype(jnp.bfloat16)
        act_ref[r * 8 : (r + 1) * 8, :] = jnp.mean(value.reshape(8, length, -1), axis=1)


def forward(titles, ln_gain, w_up):
    units, length, width = titles.shape
    rows, hidden = units * length, w_up.shape[1]
    block = 512
    return pl.pallas_call(
        functools.partial(forward_kernel, units),
        grid=(hidden // block,),
        in_specs=[
            pl.BlockSpec((rows, width), lambda i: (0, 0)),
            pl.BlockSpec((1, width), lambda i: (0, 0)),
            pl.BlockSpec((width, block), lambda i: (0, i)),
        ],
        out_specs=[
            pl.BlockSpec((rows, width), lambda i: (0, 0)),
            pl.BlockSpec((rows, block), lambda i: (0, i)),
            pl.BlockSpec((units, block), lambda i: (0, i)),
            pl.BlockSpec((units, width), lambda i: (0, 0)),
        ],
        out_shape=[
            jax.ShapeDtypeStruct((rows, width), jnp.bfloat16),
            pltpu.HBM((rows, hidden), jnp.bfloat16),
            jax.ShapeDtypeStruct((units, hidden), jnp.float32),
            jax.ShapeDtypeStruct((units, width), jnp.float32),
        ],
        compiler_params=pltpu.CompilerParams(vmem_limit_bytes=VMEM),
        cost_estimate=cost(8 * rows * width * hidden, 4 * rows * hidden, rows * hidden),
        name="forward",
    )(
        pltpu.with_memory_space_constraint(titles.reshape(rows, width), pltpu.HBM),
        ln_gain.reshape(1, width),
        pltpu.with_memory_space_constraint(w_up, pltpu.HBM),
    )


def place_sums(core_ref, keep_at, send_at, ups, down, proj, out_refs):
    slots = proj.shape[0] // 8
    part = down.shape[0] // slots
    n_x = slots // 8
    first = core_ref[0] == 0
    for q in range(slots // 2):
        y, x = q // n_x, q % n_x
        spots = [at[1, y] * n_x + at[2, x] for at in (keep_at, send_at)]
        pair = (y * 2 * n_x + x, (y * 2 + 1) * n_x + x)

        def store(refs, top, rows):
            even, odd = (rows(k) for k in pair)
            end = top + even.shape[0]
            refs[0][spots[0], top:end, :] = jnp.where(first, even, odd)
            refs[1][spots[1], top:end, :] = jnp.where(first, odd, even)

        for index, up, refs in zip(*ups, zip(out_refs[::2], out_refs[1::2])):
            store(refs, 0, lambda k: up[k * part : (k + 1) * part])
            low = index * 8
            store(refs, part, lambda k: down[k * part + low : k * part + low + 8])
            if index == 0:
                store(refs, part + 8, lambda k: proj[k * 8 : (k + 1) * 8])


def first_kernel(
    units, core_ref, keep_at, send_at, slope_ref, act_ref, mean_ref, pool_ref, grad_ref,
    normed_ref, pre_ref, *out_refs
):
    rows, block = slope_ref.shape
    length, step = rows // units, rows // units * 8
    for r in range(units // 8):
        slope = slope_ref[r * step : (r + 1) * step, :].astype(jnp.float32)
        d_pre = slope.reshape(8, length, block) * act_ref[r * 8 : (r + 1) * 8, :][:, None, :]
        pre_ref[r * step : (r + 1) * step, :] = d_pre.reshape(step, block).astype(jnp.bfloat16)
    up = contract_first(pre_ref[...], normed_ref[...])
    down = contract_first(mean_ref[...], grad_ref[...])
    proj = contract_first(pool_ref[...], grad_ref[...])
    place_sums(core_ref, keep_at, send_at, ((0,), (up,)), down, proj, out_refs)


def other_kernel(
    indices, core_ref, keep_at, send_at, pre_ref, mean_ref, pool_ref, grad_ref, *refs
):
    count = len(indices)
    normed = jnp.concatenate([ref[...] for ref in refs[:count]], axis=1)
    up = contract_first(pre_ref[...], normed)
    down = contract_first(mean_ref[...], grad_ref[...])
    wide = grad_ref.shape[1]
    ups = [up[:, p * wide : (p + 1) * wide] for p in range(count)]
    empty = jnp.zeros((pool_ref.shape[1], 1), jnp.float32)
    place_sums(core_ref, keep_at, send_at, (indices, ups), down, empty, refs[count:])


def up_products(tables, indices, left, normed_b, mean_act_b, pooled_b, grad_b):
    rows, hidden = left[0].shape
    units, width_e = grad_b.shape
    sides = tables[1].shape[1]
    slots = 2 * sides * sides
    part = hidden // sides // slots
    tall = [part + 8 + 8 * (index == 0) for index in indices for _ in range(2)]
    first = len(left) == 2

    def columns(array):
        return pl.BlockSpec((array.shape[0], array.shape[1] // sides), lambda i, c, k, s: (0, i))

    def lanes(index):
        return pl.BlockSpec((rows, width_e), lambda i, c, k, s: (0, index))

    def sums(height, table):
        return pl.BlockSpec(
            (slots // 2, height, width_e), lambda i, *tables: (tables[table][0, i], 0, 0)
        )

    out_specs = [sums(h, 1 + n % 2) for n, h in enumerate(tall)]
    out_shape = [jax.ShapeDtypeStruct((sides * slots // 2, h, width_e), jnp.float32) for h in tall]
    if first:
        kernel = functools.partial(first_kernel, units)
        out_specs.insert(0, columns(left[0]))
        out_shape.insert(0, pltpu.VMEM((rows, hidden), jnp.bfloat16))
    else:
        kernel = functools.partial(other_kernel, indices)
    return pl.pallas_call(
        kernel,
        grid_spec=pltpu.PrefetchScalarGridSpec(
            num_scalar_prefetch=3,
            grid=(sides,),
            in_specs=[columns(array) for array in left]
            + [columns(mean_act_b), columns(pooled_b)]
            + [pl.BlockSpec(grad_b.shape, lambda i, c, k, s: (0, 0))]
            + [lanes(index) for index in indices],
            out_specs=out_specs,
        ),
        out_shape=out_shape,
        compiler_params=pltpu.CompilerParams(vmem_limit_bytes=VMEM),
        cost_estimate=cost(2 * rows * width_e * len(indices) * hidden, 4 * rows * hidden),
        name="first_products" if first else "other_products",
    )(*tables, *left, mean_act_b, pooled_b, grad_b, *[normed_b] * len(indices))


def titles_kernel(pre_ref, w_ref, titles_ref, gain_ref, pool_ref, out_ref, gain_out):
    rows, width = titles_ref.shape
    units = pool_ref.shape[0]
    length = rows // units
    d_normed = contract_last(pre_ref[...], w_ref[...])
    normed, inv_scale = layer_norm(titles_ref[...].astype(jnp.float32))
    product = d_normed * normed

    @pl.when(pl.program_id(0) == 0)
    def _():
        gain_out[...] = jnp.zeros_like(gain_out)

    gain_out[...] += jnp.sum(product.reshape(rows // 8, 8, width), axis=0)
    d_hat = d_normed * gain_ref[...]
    d_flat = inv_scale * (
        d_hat
        - jnp.mean(d_hat, axis=1, keepdims=True)
        - normed * jnp.mean(d_hat * normed, axis=1, keepdims=True)
    )
    d_block = d_flat.reshape(units, length, width) + (pool_ref[...] * (1.0 / length))[:, None, :]
    out_ref[...] = d_block.reshape(rows, width).astype(jnp.bfloat16)


def title_grads(d_pre, w_up, titles, ln_gain, d_pooled):
    units, length, width = titles.shape
    rows, hidden = d_pre.shape
    step = 8 * length
    return pl.pallas_call(
        titles_kernel,
        grid=(rows // step,),
        in_specs=[
            pl.BlockSpec((step, hidden), lambda i: (i, 0)),
            pl.BlockSpec((width, hidden), lambda i: (0, 0)),
            pl.BlockSpec((step, width), lambda i: (i, 0)),
            pl.BlockSpec((1, width), lambda i: (0, 0)),
            pl.BlockSpec((8, width), lambda i: (i, 0)),
        ],
        out_specs=[
            pl.BlockSpec((step, width), lambda i: (i, 0)),
            pl.BlockSpec((8, width), lambda i: (0, 0)),
        ],
        out_shape=[
            jax.ShapeDtypeStruct((rows, width), jnp.bfloat16),
            jax.ShapeDtypeStruct((8, width), jnp.float32),
        ],
        compiler_params=pltpu.CompilerParams(vmem_limit_bytes=VMEM),
        cost_estimate=cost(2 * rows * width * hidden, 2 * rows * hidden),
        name="title_grads",
    )(d_pre, w_up, titles.reshape(rows, width), ln_gain.reshape(1, width), d_pooled)


def rows_kernel(arrived_ref, table_ref, accum_ref, table_out, accum_out):
    step, width_e = table_ref.shape
    slots = arrived_ref.shape[0]
    grads = arrived_ref[:, :width_e]
    ids = arrived_ref[:, width_e : width_e + 1].astype(jnp.int32)
    here = lax.broadcasted_iota(jnp.int32, (slots, step), 1) + pl.program_id(0) * step
    onehot = jnp.where(here == ids, 1.0, 0.0).astype(jnp.bfloat16)
    high = grads.astype(jnp.bfloat16)
    low = (grads - high.astype(jnp.float32)).astype(jnp.bfloat16)
    row_grad = contract_first(onehot, high) + contract_first(onehot, low)
    new_accum = accum_ref[...] + row_grad * row_grad
    accum_out[...] = new_accum
    table_out[...] = table_ref[...] - LEARN_RATE * row_grad * lax.rsqrt(new_accum)


def row_update(arrived, table, accum):
    rows, width_e = table.shape
    step = 1024
    tile = pl.BlockSpec((step, width_e), lambda i: (i, 0))
    return pl.pallas_call(
        rows_kernel,
        grid=(rows // step,),
        in_specs=[pl.BlockSpec(arrived.shape, lambda i: (0, 0)), tile, tile],
        out_specs=[tile, tile],
        out_shape=[jax.ShapeDtypeStruct((rows, width_e), jnp.float32)] * 2,
        compiler_params=pltpu.CompilerParams(vmem_limit_bytes=24 << 20),
        cost_estimate=cost(4 * rows * width_e * arrived.shape[0], 16 * rows * width_e),
        name="row_update",
    )(
        arrived,
        pltpu.with_memory_space_constraint(table, pltpu.HBM),
        pltpu.with_memory_space_constraint(accum, pltpu.HBM),
    )


def per_device(
    titles,
    ln_gain,
    w_up,
    w_down,
    w_proj,
    sample_grad,
    sample_item,
    sample_row,
    row_ids,
    table,
    accum,
):
    n_z, n_y, n_c, n_x = (lax.axis_size(name) for name in DEVICES)
    chips, groups = n_z * n_y * n_x, n_z * n_y * n_c
    devices = chips * n_c
    core, my_x = lax.axis_index("c"), lax.axis_index("x")
    units, length, width = titles.shape
    hidden = w_up.shape[1]
    width_e = sample_grad.shape[1]
    share_f, share_d = hidden // devices, width // devices

    owner = sample_item // units
    spot = (owner // (n_c * n_x) * n_x + owner % n_x) * units + sample_item % units
    of_core = owner // n_x % n_c
    sent = segment_sums(jnp.where(of_core == core, -1, spot), sample_grad, chips * units)
    got = swap_cores(sent)
    mine = segment_sums(jnp.where(of_core == core, spot, -1), sample_grad, chips * units, got)
    mine = mine.reshape(chips, units, width_e)
    mine, ln_gain = lax.optimization_barrier((mine, ln_gain))
    item_all = lax.all_to_all(mine, CHIPS, 0, 0, tiled=True)

    slot_count = row_ids.shape[1]
    rows_here = table.shape[0]
    slot_hot = (sample_row[:, None] == lax.iota(jnp.int32, slot_count)[None, :]).astype(
        jnp.bfloat16
    )
    local_rows = (row_ids[0] % rows_here).astype(jnp.float32)
    row_part = jnp.concatenate(
        [
            contract_first(slot_hot, sample_grad),
            jnp.broadcast_to(local_rows[:, None], (slot_count, 128)),
        ],
        axis=1,
    )
    row_part = row_part.reshape(devices, slot_count // devices, width_e + 128)

    normed_b, slope, mean_act, mean_title = forward(titles, ln_gain, w_up)
    mean_act_b = mean_act.astype(jnp.bfloat16)
    pooled = mean_title + jnp.dot(mean_act_b, w_down, preferred_element_type=jnp.float32)
    lane = lax.iota(jnp.int32, devices * 8)
    source = jnp.where(lane % 8 < share_d, lane // 8 * share_d + lane % 8, -1)
    spread = (lax.iota(jnp.int32, width)[:, None] == source[None, :]).astype(jnp.bfloat16)
    pooled_b = jnp.dot(
        pooled.astype(jnp.bfloat16), spread, preferred_element_type=jnp.float32
    ).astype(jnp.bfloat16)
    item_all, pooled_b, row_part = lax.optimization_barrier((item_all, pooled_b, row_part))

    item_grad = jnp.sum(item_all, axis=0)
    grad_b = item_grad.astype(jnp.bfloat16)
    d_pooled = contract_last(grad_b, w_proj)
    d_act = contract_last(d_pooled.astype(jnp.bfloat16), w_down) / length

    here = [(lax.axis_index(name), lax.axis_size(name)) for name in CHIPS]
    keep_at = jnp.stack([slot_of(core, at, size) for at, size in here])
    send_at = jnp.stack([slot_of(1 - core, at, size) for at, size in here])
    tables = (core.reshape(1), keep_at, send_at)
    items = (normed_b, mean_act_b, pooled_b, grad_b)
    slope = pltpu.with_memory_space_constraint(slope, pltpu.HBM)
    d_pre, *sums = up_products(tables, (0,), (slope, d_act), *items)
    d_pre = pltpu.with_memory_space_constraint(d_pre, pltpu.VMEM)
    for index in (1, 2):
        sums += up_products(tables, (index,), (d_pre,), *items)
    parts = [
        (keep + swap_cores(send)).reshape(n_z, n_y, n_x, -1, width_e)
        for keep, send in zip(sums[::2], sums[1::2])
    ]

    beside = title_grads(d_pre, w_up, titles, ln_gain, d_pooled)
    parts, (d_titles, gain_term) = halve(parts, "xyz", False, tuple(beside))
    parts, row_part = lax.optimization_barrier((parts, row_part))
    row_all = lax.all_to_all(row_part, DEVICES, 0, 0, tiled=True)
    gain_term = (gain_term + swap_cores(gain_term)).reshape(8, 3, width_e)
    gain_term = jnp.pad(jnp.sum(gain_term, axis=0), ((0, 5), (0, 0)))
    parts, (gain_term,) = halve(parts, "xyz", True, (gain_term,))
    gain_term = jnp.broadcast_to(gain_term, parts[0].shape[:3] + gain_term.shape)
    parts[0] = jnp.concatenate([parts[0], gain_term], axis=3)
    parts, _ = halve(parts, "yzx", False)
    parts, (row_all,) = halve(parts, "yzx", True, (row_all,))
    new_table, new_accum = row_update(
        row_all.reshape(slot_count, width_e + 128), table, accum
    )
    parts, _ = halve(parts, "zxy", False)
    parts, _ = halve(parts, "zxy", True)

    flat = [part.reshape(-1, width_e) for part in parts]
    last = jnp.concatenate(flat, axis=0)
    blocks = jnp.stack([last, along(last, "x", 1), along(last, "x", 2), along(last, "x", 3)])
    ordered = jnp.stack(
        [lax.dynamic_index_in_dim(blocks, my_x ^ j, 0, keepdims=False) for j in range(n_x)]
    )
    starts = [0, share_f + 24, 2 * share_f + 32]
    grad_up = jnp.concatenate([ordered[:, at : at + share_f] for at in starts], axis=2)
    grad_up = grad_up.reshape(-1, width).T
    outer = jnp.concatenate(
        [ordered[:, at + share_f : at + share_f + 8] for at in starts], axis=1
    ).reshape(-1, width_e)
    high = outer.astype(jnp.bfloat16)
    low = (outer - high.astype(jnp.float32)).astype(jnp.bfloat16)
    grad_down = contract_last(high, w_proj) + contract_last(low, w_proj)
    grad_proj = ordered[:, share_f + 8 : share_f + 8 + share_d].reshape(-1, width_e)
    gains = jnp.sum(ordered[:, share_f + 16 : share_f + 19], axis=0).reshape(width)
    mine_at = (lax.axis_index("z") * n_y + lax.axis_index("y")) * n_c + core
    grad_gain = lax.dynamic_slice_in_dim(gains, mine_at * (width // groups), width // groups, 0)
    return (
        d_titles.reshape(units, length, width),
        grad_up,
        grad_down,
        grad_proj,
        grad_gain,
        new_table,
        new_accum,
    )


def solution(mesh):
    n_table, n_rep = mesh.devices.shape
    side = n_rep
    fine = Mesh(mesh.devices.reshape(n_table // (2 * side), side, 2, n_rep), DEVICES)
    split, tab = P(DEVICES), P(GROUP)
    return jax.shard_map(
        per_device,
        mesh=fine,
        in_specs=(split, P(), P(), P(), P(), split, split, split, split, split, split),
        out_specs=(split, P(None, GROUP), tab, tab, tab, split, split),
        check_vma=False,
    )
```
